256 devices in a mesh: cells: 32 (over z, x), genes: 8 (over y, core).
Axes of the slice: x: 4, y: 4, z: 8, core: 2. Of those that a mesh axis runs over, the one named last changes fastest.
Arguments:
- block_tiles: bfloat16 [10240, 1024, 128], P('cells', 'genes'), may hold values from -0.375 to 0.375
- block_coords: int32 [10240, 16], P('cells', 'genes'), may hold values from 0 to 31, as said below
- block_counts: int32 [32, 8], P('cells', 'genes'), may hold values from 40 to 320, as said below
- basis_rows: bfloat16 [32768, 256], P(('cells', 'genes')), may hold values from -0.03125 to 0.03125
Outputs:
- gene_products: float32 [32768, 256], P(('cells', 'genes'))
The draws below stay inside these ranges and needn't reach their ends.
Inputs may be any that keep to these rules, and one draw needn't show every extreme that they name: `block_coords`: column 2 g of device rows gives a block of cells below 16, column 2 g + 1 a tile of genes below 32; the live slots of one device name distinct pairs; slots at or past the device's count hold valid coordinates and tiles that are not part of X. `block_counts`: at least 40 live slots a device; some device uses all 320.
All inputs are finite; a program needn't handle non-finite values.
Results may differ from the reference program's by a relative error of at most 0.0017.
Values may be sent and summed in bfloat16 or wider, within the bound.
A program may use at most 64 MiB of HBM per device.

```python
import jax
import jax.numpy as jnp
from jax import lax

BLK = 128
GENES = 32768
RANK = 256
ROW_BLOCKS = 16
GENE_BLOCKS = 32
SLOTS = 320
SLAB = 128
CELLS = 65536
N_CELLS = 32
N_GENES = 8


def draw_block_counts(key, part):
    key = jax.random.fold_in(key, 11)
    first_key, second_key = jax.random.split(key)
    lowest = SLOTS // 8
    spread = jax.random.randint(first_key, (N_CELLS * N_GENES,), 0, 17)
    counts = lowest + spread * spread * (SLOTS - lowest) // 256
    fullest = jax.random.randint(second_key, (), 0, N_CELLS * N_GENES)
    counts = jnp.where(jnp.arange(N_CELLS * N_GENES) == fullest, SLOTS, counts)
    return counts.reshape(N_CELLS, N_GENES).astype(jnp.int32)


def draw_block_coords(key, part):
    key = jax.random.fold_in(key, 23)
    device_keys = jax.random.split(key, N_CELLS * N_GENES)

    def one_device(device_key):
        return jax.random.permutation(device_key, ROW_BLOCKS * GENE_BLOCKS)[:SLOTS]
    chosen = jax.vmap(one_device)(device_keys)
    rows_part = chosen // GENE_BLOCKS
    genes_part = chosen % GENE_BLOCKS
    stacked = jnp.stack([rows_part, genes_part], axis=-1).reshape(N_CELLS, N_GENES, SLOTS, 2)
    return stacked.transpose(0, 2, 1, 3).reshape(N_CELLS * SLOTS, N_GENES * 2).astype(jnp.int32)


def block_levels(own_key, dims, cuts, low, high):
    def one(dim, shards_of):
        heights = jax.random.uniform(jax.random.fold_in(jax.random.fold_in(own_key, 6), dim), (shards_of,), jnp.float32, low / len(cuts), high / len(cuts))
        return jnp.repeat(jnp.exp(heights), dims[dim] // shards_of).reshape((-1,) + (1,) * (len(dims) - dim - 1))

    gain = one(*cuts[0])
    for cut in cuts[1:]:
        gain = gain * one(*cut)
    return gain


def scatter_about(stream_key, dims, scale, most, pieces=(), held_as=jnp.bfloat16):
    values = scale * jax.random.normal(stream_key, dims, jnp.float32)
    if pieces:
        values = values * block_levels(stream_key, dims, pieces, -0.22, 0.18)
    return jnp.clip(values, -most, most).astype(held_as)


def setup_inputs(seed: int = 0) -> dict:
    seeds = jax.random.split(jax.random.key(seed), 5)
    block_tiles = scatter_about(seeds[0], (N_CELLS * SLOTS, N_GENES * BLK, BLK), (CELLS ** -0.25), 0.375, ((0, 32), (1, 8)))
    block_coords = draw_block_coords(jax.random.fold_in(seeds[4], 71), 0)
    block_counts = draw_block_counts(jax.random.fold_in(seeds[4], 71), 0)
    basis_rows = scatter_about(seeds[3], (GENES, RANK), GENES ** -0.5, 0.03125, ((0, 256),))
    return {"block_tiles": block_tiles, "block_coords": block_coords, "block_counts": block_counts, "basis_rows": basis_rows}


def reference(block_tiles, block_coords, block_counts, basis_rows):
    tile_view = block_tiles.reshape(N_CELLS, SLOTS, N_GENES, BLK, BLK).transpose(0, 2, 1, 3, 4)
    coord_view = block_coords.reshape(N_CELLS, SLOTS, N_GENES, 2).transpose(0, 2, 1, 3)
    group_basis = basis_rows.reshape(N_CELLS, N_GENES, SLAB, RANK).transpose(1, 0, 2, 3)
    group_basis = group_basis.reshape(N_GENES, GENE_BLOCKS, BLK, RANK)
    slot_ids = jnp.arange(SLOTS).astype(jnp.int32)

    def cell_shard(cell):
        def per_group(running, group):
            tiles_here = tile_view[cell, group].astype(jnp.float32)
            rows_here = coord_view[cell, group, :, 0].astype(jnp.int32)
            genes_here = coord_view[cell, group, :, 1].astype(jnp.int32)
            live = slot_ids < block_counts[cell, group]
            chosen = group_basis[group][genes_here].astype(jnp.float32)
            product = jnp.einsum("sab,sbk->sak", tiles_here, chosen)
            product = jnp.where(live[:, None, None], product, jnp.zeros_like(product))
            return running.at[rows_here].add(product), None

        start_rows = jnp.zeros((ROW_BLOCKS, BLK, RANK), jnp.float32)
        total, _ = lax.scan(per_group, start_rows, jnp.arange(N_GENES).astype(jnp.int32))
        return total

    cell_basis = lax.map(cell_shard, jnp.arange(N_CELLS).astype(jnp.int32)).astype(jnp.bfloat16)

    def gene_group(group):
        def per_cell(running, cell):
            tiles_here = tile_view[cell, group].astype(jnp.float32)
            rows_here = coord_view[cell, group, :, 0].astype(jnp.int32)
            genes_here = coord_view[cell, group, :, 1].astype(jnp.int32)
            live = slot_ids < block_counts[cell, group]
            chosen = cell_basis[cell][rows_here].astype(jnp.float32)
            product = jnp.einsum("sab,sak->sbk", tiles_here, chosen)
            product = jnp.where(live[:, None, None], product, jnp.zeros_like(product))
            return running.at[genes_here].add(product), None

        start_genes = jnp.zeros((GENE_BLOCKS, BLK, RANK), jnp.float32)
        total, _ = lax.scan(per_cell, start_genes, jnp.arange(N_CELLS).astype(jnp.int32))
        return total

    grouped = lax.map(gene_group, jnp.arange(N_GENES).astype(jnp.int32))
    grouped = grouped.reshape(N_GENES, N_CELLS, SLAB, RANK).transpose(1, 0, 2, 3)
    return grouped.reshape(GENES, RANK)
```

```python
import functools

import jax
import jax.numpy as jnp
from jax import lax
from jax.experimental import pallas as pl
from jax.experimental.pallas import tpu as pltpu
from jax.sharding import PartitionSpec as P

MESH = pl.DeviceIdType.MESH
BF = jnp.bfloat16
F32 = jnp.float32

NX, NY, NZ = 4, 4, 8
BLK = 128
RANK = 256
ROWS = 2048
COLS = 4096
CHUNK = 256
SLOTS = 320
GA = 48

ORDER = {0: 0, 1: 1, -1: 2, 2: 3, -2: 4, 3: 5, -3: 6, 4: 7}
GROUPS = ((0, 1), (1, 3), (3, 5), (5, 7), (7, 8))

NH = 1
R = RANK // NH
RA = 96 // NH
RB = R - RA
RB1 = 80 if NH == 1 else 48
N_SEM = 120 * NH


class Board:
    def __init__(self, ssem, rsem, where):
        self.ssem, self.rsem, self.where = ssem, rsem, where
        self.sent = []

    def send(self, src, dst, to):
        n = len(self.sent)
        copy = pltpu.make_async_remote_copy(
            src_ref=src, dst_ref=dst, send_sem=self.ssem.at[n], recv_sem=self.rsem.at[n],
            device_id=self.where[to], device_id_type=MESH)
        copy.start()
        self.sent.append(copy)
        return copy


def kernel(slot_ref, tiles_hbm, basis, out, tiles, xd, q, p, pcr, yr, cbt, zt,
           za, zb, as_p, as_m, ar_p, ar_m, bs, br, axr, bzr_p, bzr_m, ssem, rsem, tsem):
    c = lax.axis_index("cells")
    g = lax.axis_index("genes")
    z, x = c // NX, c % NX
    y, core = g // 2, g % 2

    def at(dz, dx, dy, dc):
        return (((z + dz + NZ) % NZ) * NX + (x + dx + NX) % NX,
                ((y + dy + NY) % NY) * 2 + (core + dc) % 2)

    where = {
        "x+": at(0, 1, 0, 0), "x-": at(0, -1, 0, 0),
        "z+": at(1, 0, 0, 0), "z-": at(-1, 0, 0, 0),
        "y+": at(0, 0, 1, 0), "y-": at(0, 0, -1, 0),
        "c": at(0, 0, 0, 1),
    }
    board = Board(ssem, rsem, where)
    send = board.send

    n_loads = 8
    per = SLOTS // n_loads
    loads = [pltpu.make_async_copy(tiles_hbm.at[pl.ds(i * per, per)],
                                   tiles.at[pl.ds(i * per, per)], tsem.at[i]) for i in range(n_loads)]
    for load in loads:
        load.start()

    barrier = pltpu.get_barrier_semaphore()
    for to in where.values():
        pl.semaphore_signal(barrier, inc=1, device_id=to, device_id_type=MESH)
    q[0, 0] = basis[...]
    tiles[SLOTS] = jnp.zeros((BLK, BLK), BF)
    pl.semaphore_wait(barrier, len(where))

    def densify(lo, hi):
        def row(r, carry):
            for col in range(lo * 4, hi * 4):
                s = slot_ref[r * 32 + col]
                xd[pl.ds(pl.multiple_of(r * BLK, BLK), BLK), col * BLK:(col + 1) * BLK] = tiles[s]
            return carry
        lax.fori_loop(0, ROWS // BLK, row, 0)

    def gather(h):
        hs = slice(h * R, (h + 1) * R)
        a, b = slice(0, GA), slice(GA, BLK)
        cut = {0: GA + 48, 1: GA + 32}
        m = {}

        def bx(k):
            lo, hi = GROUPS[k]
            m["bx+", k] = send(q.at[lo:hi, 0, b, hs], q.at[lo:hi, 3, b, hs], "x+")
            m["bx-", k] = send(q.at[lo:hi, 0, b, hs], q.at[lo:hi, 1, b, hs], "x-")

        def bxf(k):
            lo, hi = GROUPS[k]
            e = cut[k % 2]
            m["bx+", k].wait_recv()
            m["bf+", k] = send(q.at[lo:hi, 3, GA:e, hs], q.at[lo:hi, 2, GA:e, hs], "x+")
            m["bx-", k].wait_recv()
            m["bf-", k] = send(q.at[lo:hi, 1, e:BLK, hs], q.at[lo:hi, 2, e:BLK, hs], "x-")

        def az(d):
            lo, hi = (0, 4) if d < 4 else (0, 2)
            m["az+", d] = send(q.at[ORDER[1 - d], lo:hi, a, hs],
                               q.at[ORDER[-d if d < 4 else 4], lo:hi, a, hs], "z+")
            lo, hi = (0, 4) if d < 4 else (2, 4)
            m["az-", d] = send(q.at[ORDER[d - 1], lo:hi, a, hs], q.at[ORDER[d], lo:hi, a, hs], "z-")

        def bz(d):
            e = BLK if d < 4 else GA + 48
            m["bz+", d] = send(q.at[ORDER[1 - d], 0, GA:e, hs],
                               q.at[ORDER[-d if d < 4 else 4], 0, GA:e, hs], "z+")
            s = GA if d < 4 else GA + 48
            m["bz-", d] = send(q.at[ORDER[d - 1], 0, s:BLK, hs], q.at[ORDER[d], 0, s:BLK, hs], "z-")

        def wait(kind, d):
            m[kind + "+", d].wait_recv()
            m[kind + "-", d].wait_recv()

        m["ax+"] = send(q.at[0, 0, a, hs], q.at[0, 3, a, hs], "x+")
        m["ax-"] = send(q.at[0, 0, a, hs], q.at[0, 1, a, hs], "x-")
        bz(1)
        bx(0)
        if h == 0:
            for load in loads:
                load.wait()
            densify(*GROUPS[0])
        yield
        m["ax+"].wait_recv()
        m["af+"] = send(q.at[0, 3, 0:32, hs], q.at[0, 2, 0:32, hs], "x+")
        m["ax-"].wait_recv()
        m["af-"] = send(q.at[0, 1, 32:GA, hs], q.at[0, 2, 32:GA, hs], "x-")
        wait("bz", 1)
        bz(2)
        bx(1)
        m["af+"].wait_recv()
        m["af-"].wait_recv()
        az(1)
        bxf(0)
        if h == 0:
            densify(*GROUPS[1])
        yield
        wait("az", 1)
        az(2)
        wait("bz", 2)
        bz(3)
        bx(2)
        bxf(1)
        wait("bf", 0)
        if h == 0:
            densify(*GROUPS[2])
        cells_group(0, h)
        yield
        wait("az", 2)
        az(3)
        wait("bz", 3)
        bz(4)
        bx(3)
        bxf(2)
        wait("bf", 1)
        if h == 0:
            densify(*GROUPS[3])
        cells_group(1, h)
        yield
        wait("az", 3)
        az(4)
        wait("bz", 4)
        bx(4)
        bxf(3)
        wait("bf", 2)
        if h == 0:
            densify(*GROUPS[4])
        cells_group(2, h)
        yield
        bxf(4)
        wait("bf", 3)
        cells_group(3, h)
        wait("az", 4)
        wait("bf", 4)
        yield

    def cells_dot(rows, k, h):
        lo, hi = GROUPS[k]
        right = q[lo:hi, :, :, h * R:(h + 1) * R].reshape((hi - lo) * 512, R)
        return jnp.dot(xd[rows, lo * 512:hi * 512], right, preferred_element_type=F32)

    def cells_group(k, h):
        hs = slice(h * R, (h + 1) * R)

        def step(i, carry):
            rows = pl.ds(pl.multiple_of(i * 512, 512), 512)
            part = cells_dot(rows, k, h)
            p[rows, hs] = part if k == 0 else p[rows, hs] + part
            return carry
        lax.fori_loop(0, ROWS // 512, step, 0)

    def reduce_cells(h):
        hs = slice(h * R, (h + 1) * R)
        half = CHUNK // 2
        pair, m = [], {}

        def last(i):
            rows = slice(i * CHUNK, (i + 1) * CHUNK)
            return p[rows, hs] + cells_dot(rows, 4, h)

        for i in range(4):
            rows = slice(i * CHUNK, (i + 1) * CHUNK)
            p[rows, hs] = last(i)
            pair.append(send(p.at[rows, hs], pcr.at[i, :, hs], "c"))
        yield
        lows = [slice((4 + i) * CHUNK, (4 + i) * CHUNK + half) for i in range(4)]
        highs = [slice((4 + i) * CHUNK + half, (5 + i) * CHUNK) for i in range(4)]

        def own(i):
            part = last(4 + i)
            pair[i].wait_recv()
            p[(4 + i) * CHUNK:(5 + i) * CHUNK, hs] = part + pcr[i, :, hs]

        own(0)
        m["h+"] = send(p.at[lows[0], hs], yr.at[0, :, hs], "y+")
        m["h-"] = send(p.at[highs[0], hs], yr.at[1, :, hs], "y-")
        own(1)
        m["s+"] = send(p.at[highs[1], hs], yr.at[2, :, hs], "y+")
        own(2)
        m["s-"] = send(p.at[lows[2], hs], yr.at[3, :, hs], "y-")
        yield
        m["h+"].wait_recv()
        p[lows[1], hs] = p[lows[1], hs] + yr[0, :, hs]
        m["f+"] = send(p.at[lows[1], hs], yr.at[4, :, hs], "y+")
        m["h-"].wait_recv()
        p[highs[2], hs] = p[highs[2], hs] + yr[1, :, hs]
        m["f-"] = send(p.at[highs[2], hs], yr.at[5, :, hs], "y-")
        own(3)
        yield
        m["s+"].wait_recv()
        m["s-"].wait_recv()
        low = p[lows[3], hs] + yr[3, :, hs]
        high = p[highs[3], hs] + yr[2, :, hs]
        m["f+"].wait_recv()
        m["f-"].wait_recv()
        total = jnp.concatenate([low + yr[4, :, hs], high + yr[5, :, hs]], axis=0)

        def lanes(i):
            return slice(i * CHUNK, (i + 1) * CHUNK)

        mid = h * R + R // 2
        up, down = slice(h * R, mid), slice(mid, (h + 1) * R)
        cbt[hs, lanes(7)] = total.T.astype(BF)
        m["g+"] = send(cbt.at[hs, lanes(7)], cbt.at[hs, lanes(6)], "y+")
        m["g-"] = send(cbt.at[hs, lanes(7)], cbt.at[hs, lanes(5)], "y-")
        m["c3"] = send(cbt.at[hs, lanes(7)], cbt.at[hs, lanes(3)], "c")
        yield
        m["g+"].wait_recv()
        m["k+"] = send(cbt.at[up, lanes(6)], cbt.at[up, lanes(4)], "y+")
        m["c2"] = send(cbt.at[hs, lanes(6)], cbt.at[hs, lanes(2)], "c")
        m["g-"].wait_recv()
        m["k-"] = send(cbt.at[down, lanes(5)], cbt.at[down, lanes(4)], "y-")
        m["c1"] = send(cbt.at[hs, lanes(5)], cbt.at[hs, lanes(1)], "c")
        yield
        m["k+"].wait_recv()
        m["k-"].wait_recv()
        m["c0"] = send(cbt.at[hs, lanes(4)], cbt.at[hs, lanes(0)], "c")
        for i in range(4):
            m["c%d" % i].wait_recv()
        yield

    def reduce_genes(h):
        hs = slice(h * R, (h + 1) * R)
        a = slice(h * R, h * R + RA)
        b1 = slice(h * R + RA, h * R + RA + RB1)
        b2 = slice(h * R + RA + RB1, (h + 1) * R)
        v1, v2 = slice(0, RB1), slice(RB1, RB)
        m = {}

        def genes_group(k):
            lo, hi = GROUPS[k]
            for n in range(lo, hi):
                zt[n, hs] = jnp.dot(cbt[hs, :], xd[:, n * 512:(n + 1) * 512],
                                    preferred_element_type=F32)

        def lanes(dx):
            return slice(dx * BLK, (dx + 1) * BLK)

        def a_z(d):
            if d == 4:
                as_p[h, 3, :, 0:256] = zt[7, a, 0:256].astype(BF)
                m["az+", 4] = send(as_p.at[h, 3, :, 0:256], ar_p.at[h, 3, :, 0:256], "z+")
                as_m[h, 3, :, 0:256] = zt[7, a, 256:512].astype(BF)
                m["az-", 4] = send(as_m.at[h, 3, :, 0:256], ar_m.at[h, 3, :, 0:256], "z-")
                return
            i = d - 1
            m["az+", d + 1].wait_recv()
            if d == 3:
                as_p[h, i, :, 0:256] = (zt[ORDER[d], a, 0:256] + ar_p[h, 3, :, 0:256].astype(F32)).astype(BF)
                as_p[h, i, :, 256:512] = zt[ORDER[d], a, 256:512].astype(BF)
            else:
                as_p[h, i] = (zt[ORDER[d], a] + ar_p[h, i + 1].astype(F32)).astype(BF)
            m["az+", d] = send(as_p.at[h, i], ar_p.at[h, i], "z+")
            m["az-", d + 1].wait_recv()
            if d == 3:
                as_m[h, i, :, 0:256] = zt[ORDER[-d], a, 0:256].astype(BF)
                as_m[h, i, :, 256:512] = (zt[ORDER[-d], a, 256:512] + ar_m[h, 3, :, 0:256].astype(F32)).astype(BF)
            else:
                as_m[h, i] = (zt[ORDER[-d], a] + ar_m[h, i + 1].astype(F32)).astype(BF)
            m["az-", d] = send(as_m.at[h, i], ar_m.at[h, i], "z-")

        def b_send(kind, k, value, to):
            lo, hi = GROUPS[k]
            rows = v1 if kind in (0, 3, 4) else slice(0, RB - RB1)
            bs[h, kind, lo:hi, rows] = value.astype(BF)
            m["b", kind, k] = send(bs.at[h, kind, lo:hi, rows], br.at[h, kind, lo:hi, rows], to)

        def b_got(kind, k):
            lo, hi = GROUPS[k]
            rows = v1 if kind in (0, 3, 4) else slice(0, RB - RB1)
            m["b", kind, k].wait_recv()
            return br[h, kind, lo:hi, rows].astype(F32)

        def b_first(k):
            lo, hi = GROUPS[k]
            b_send(0, k, zt[lo:hi, b1, lanes(2)], "x+")
            b_send(1, k, zt[lo:hi, b2, lanes(2)], "x-")
            b_send(2, k, zt[lo:hi, b2, lanes(1)], "x+")
            b_send(3, k, zt[lo:hi, b1, lanes(3)], "x-")

        def b_merge(k):
            lo, hi = GROUPS[k]
            b_send(4, k, zt[lo:hi, b1, lanes(1)] + b_got(0, k), "x+")
            b_send(5, k, zt[lo:hi, b2, lanes(3)] + b_got(1, k), "x-")

        def b_total(k):
            lo, hi = GROUPS[k]
            zb[h, lo:hi, v1] = zt[lo:hi, b1, lanes(0)] + b_got(3, k) + b_got(4, k)
            zb[h, lo:hi, v2] = zt[lo:hi, b2, lanes(0)] + b_got(2, k) + b_got(5, k)

        def b_z(d):
            if d == 4:
                m["bz+", 4] = send(zb.at[h, 7, v1], bzr_p.at[h, 3, v1], "z+")
                m["bz-", 4] = send(zb.at[h, 7, v2], bzr_m.at[h, 3, v2], "z-")
                return
            i = d - 1
            up = v1 if d == 3 else slice(0, RB)
            down = v2 if d == 3 else slice(0, RB)
            m["bz+", d + 1].wait_recv()
            zb[h, ORDER[d], up] = zb[h, ORDER[d], up] + bzr_p[h, i + 1, up]
            m["bz+", d] = send(zb.at[h, ORDER[d]], bzr_p.at[h, i], "z+")
            m["bz-", d + 1].wait_recv()
            zb[h, ORDER[-d], down] = zb[h, ORDER[-d], down] + bzr_m[h, i + 1, down]
            m["bz-", d] = send(zb.at[h, ORDER[-d]], bzr_m.at[h, i], "z-")

        genes_group(4)
        a_z(4)
        b_first(4)
        yield
        genes_group(3)
        a_z(3)
        b_first(3)
        b_merge(4)
        yield
        genes_group(2)
        a_z(2)
        b_first(2)
        b_merge(3)
        b_total(4)
        b_z(4)
        yield
        genes_group(1)
        a_z(1)
        b_first(1)
        b_merge(2)
        b_total(3)
        b_z(3)
        yield
        genes_group(0)
        b_first(0)
        b_merge(1)
        b_total(2)
        b_z(2)
        m["az+", 1].wait_recv()
        m["az-", 1].wait_recv()
        za[h] = zt[0, a] + ar_p[h, 0].astype(F32) + ar_m[h, 0].astype(F32)
        r1, r2 = slice(0, RA // 2), slice(RA // 2, RA)
        m["a0"] = send(za.at[h, r1, lanes(2)], axr.at[h, 0], "x+")
        m["a1"] = send(za.at[h, r2, lanes(2)], axr.at[h, 1], "x-")
        m["a2"] = send(za.at[h, r2, lanes(1)], axr.at[h, 2], "x+")
        m["a3"] = send(za.at[h, r1, lanes(3)], axr.at[h, 3], "x-")
        yield
        b_merge(0)
        b_total(1)
        b_z(1)
        m["a0"].wait_recv()
        za[h, r1, lanes(1)] = za[h, r1, lanes(1)] + axr[h, 0]
        m["a4"] = send(za.at[h, r1, lanes(1)], axr.at[h, 4], "x+")
        m["a1"].wait_recv()
        za[h, r2, lanes(3)] = za[h, r2, lanes(3)] + axr[h, 1]
        m["a5"] = send(za.at[h, r2, lanes(3)], axr.at[h, 5], "x-")
        b_total(0)
        yield
        for i in range(2, 6):
            m["a%d" % i].wait_recv()
        top = jnp.concatenate([za[h, r1, lanes(0)] + axr[h, 3] + axr[h, 4],
                               za[h, r2, lanes(0)] + axr[h, 2] + axr[h, 5]], axis=0)
        m["bz+", 1].wait_recv()
        m["bz-", 1].wait_recv()
        bottom = zb[h, 0] + bzr_p[h, 0] + bzr_m[h, 0]
        out[:, hs] = jnp.concatenate([top, bottom], axis=0).T
        yield

    for h in range(NH):
        for _ in gather(h):
            pass
        for _ in reduce_cells(h):
            pass
        for _ in reduce_genes(h):
            pass

    for copy in board.sent:
        copy.wait_send()


def local(block_tiles, block_coords, block_counts, basis_rows):
    c, g = lax.axis_index("cells"), lax.axis_index("genes")
    z, x, y, core = c // NX, c % NX, g // 2, g % 2
    b, k = block_coords[:, 0], block_coords[:, 1]
    chunk = b // 2
    dy = (chunk % 4 - y + NY) % NY
    dy = jnp.where(dy == 0, 3, jnp.where(dy == 3, 2, 2 - dy))
    pos = jnp.where(chunk // 4 == core, 4, 0) + dy
    dz = (k // NX - z + NZ) % NZ
    dz = jnp.where(dz == 0, 0, jnp.where(dz <= 3, 2 * dz - 1, jnp.where(dz == 4, 7, 2 * (NZ - dz))))
    place = (pos * 2 + b % 2) * 32 + dz * NX + (k % NX - x + NX) % NX
    ids = jnp.arange(SLOTS, dtype=jnp.int32)
    place = jnp.where(ids < block_counts[0, 0], place, -1)
    hit = place[:, None] == jnp.arange(512, dtype=jnp.int32)[None, :]
    slots = jnp.min(jnp.where(hit, ids[:, None], SLOTS), axis=0)

    vmem = pl.BlockSpec(memory_space=pltpu.VMEM)
    return pl.pallas_call(
        kernel,
        out_shape=jax.ShapeDtypeStruct((BLK, RANK), F32),
        in_specs=[pl.BlockSpec(memory_space=pltpu.SMEM), pl.BlockSpec(memory_space=pl.ANY), vmem],
        out_specs=vmem,
        scratch_shapes=[
            pltpu.VMEM((SLOTS + 1, BLK, BLK), BF),
            pltpu.VMEM((ROWS, COLS), BF),
            pltpu.VMEM((NZ, NX, BLK, RANK), BF),
            pltpu.VMEM((ROWS, RANK), F32),
            pltpu.VMEM((4, CHUNK, RANK), F32),
            pltpu.VMEM((6, CHUNK // 2, RANK), F32),
            pltpu.VMEM((RANK, ROWS), BF),
            pltpu.VMEM((NZ, RANK, 512), F32),
            pltpu.VMEM((NH, RA, 512), F32),
            pltpu.VMEM((NH, NZ, RB, BLK), F32),
            pltpu.VMEM((NH, 4, RA, 512), BF),
            pltpu.VMEM((NH, 4, RA, 512), BF),
            pltpu.VMEM((NH, 4, RA, 512), BF),
            pltpu.VMEM((NH, 4, RA, 512), BF),
            pltpu.VMEM((NH, 6, NZ, RB1, BLK), BF),
            pltpu.VMEM((NH, 6, NZ, RB1, BLK), BF),
            pltpu.VMEM((NH, 6, RA // 2, BLK), F32),
            pltpu.VMEM((NH, 4, RB, BLK), F32),
            pltpu.VMEM((NH, 4, RB, BLK), F32),
            pltpu.SemaphoreType.DMA((N_SEM,)),
            pltpu.SemaphoreType.DMA((N_SEM,)),
            pltpu.SemaphoreType.DMA((8,)),
        ],
        compiler_params=pltpu.CompilerParams(
            collective_id=0, has_side_effects=True, vmem_limit_bytes=60 * 1024 * 1024),
        cost_estimate=pl.CostEstimate(flops=4 * ROWS * COLS * RANK, bytes_accessed=11_000_000,
                                      transcendentals=0),
    )(slots, block_tiles, basis_rows)


def solution(mesh):
    return jax.shard_map(
        local,
        mesh=mesh,
        in_specs=(
            P("cells", "genes", None),
            P("cells", "genes"),
            P("cells", "genes"),
            P(("cells", "genes"), None),
        ),
        out_specs=P(("cells", "genes"), None),
        check_vma=False,
    )
```

```python
import functools

import jax
import jax.numpy as jnp
from jax import lax
from jax.experimental import pallas as pl
from jax.experimental.pallas import tpu as pltpu
from jax.sharding import PartitionSpec as P

MESH = pl.DeviceIdType.MESH
BF = jnp.bfloat16
F32 = jnp.float32

NX, NY, NZ = 4, 4, 8
BLK = 128
RANK = 256
ROWS = 2048
COLS = 4096
CHUNK = 256
SLOTS = 320
GA = 48

ORDER = {0: 0, 1: 1, -1: 2, 2: 3, -2: 4, 3: 5, -3: 6, 4: 7}
GROUPS = ((0, 1), (1, 3), (3, 5), (5, 7), (7, 8))

NH = 1
R = RANK // NH
RA = 96 // NH
RB = R - RA
RB1 = 80 if NH == 1 else 48
N_SEM = 120 * NH


class Board:
    def __init__(self, ssem, rsem, where):
        self.ssem, self.rsem, self.where = ssem, rsem, where
        self.sent = []

    def send(self, src, dst, to):
        n = len(self.sent)
        copy = pltpu.make_async_remote_copy(
            src_ref=src, dst_ref=dst, send_sem=self.ssem.at[n], recv_sem=self.rsem.at[n],
            device_id=self.where[to], device_id_type=MESH)
        copy.start()
        self.sent.append(copy)
        return copy


def kernel(count_ref, coords, tiles_hbm, basis, out, tiles, xd, q, p, pcr, yr, cbt, zt,
           za, zb, as_p, as_m, ar_p, ar_m, bs, br, axr, bzr_p, bzr_m, slot_v, slot_ref, ssem, rsem, tsem, slot_sem):
    c = lax.axis_index("cells")
    g = lax.axis_index("genes")
    z, x = c // NX, c % NX
    y, core = g // 2, g % 2

    def at(dz, dx, dy, dc):
        return (((z + dz + NZ) % NZ) * NX + (x + dx + NX) % NX,
                ((y + dy + NY) % NY) * 2 + (core + dc) % 2)

    where = {
        "x+": at(0, 1, 0, 0), "x-": at(0, -1, 0, 0),
        "z+": at(1, 0, 0, 0), "z-": at(-1, 0, 0, 0),
        "y+": at(0, 0, 1, 0), "y-": at(0, 0, -1, 0),
        "c": at(0, 0, 0, 1),
    }
    board = Board(ssem, rsem, where)
    send = board.send

    n_loads = 8
    per = SLOTS // n_loads
    loads = [pltpu.make_async_copy(tiles_hbm.at[pl.ds(i * per, per)],
                                   tiles.at[pl.ds(i * per, per)], tsem.at[i]) for i in range(n_loads)]
    for load in loads:
        load.start()

    barrier = pltpu.get_barrier_semaphore()
    for to in where.values():
        pl.semaphore_signal(barrier, inc=1, device_id=to, device_id_type=MESH)
    q[0, 0] = basis[...]
    tiles[SLOTS] = jnp.zeros((BLK, BLK), BF)

    b, k = coords[0:1, :], coords[1:2, :]
    chunk = lax.shift_right_logical(b, 1)
    dy = ((chunk & 3) - y) & 3
    dy = jnp.where(dy == 0, 3, jnp.where(dy == 3, 2, 2 - dy))
    pos = jnp.where(lax.shift_right_logical(chunk, 2) == core, 4, 0) + dy
    dz = (lax.shift_right_logical(k, 2) - z) & 7
    dz = jnp.where(dz == 0, 0, jnp.where(dz <= 3, 2 * dz - 1, jnp.where(dz == 4, 7, 2 * (NZ - dz))))
    place = (pos * 2 + (b & 1)) * 32 + dz * NX + (((k & 3) - x) & 3)
    live = lax.broadcasted_iota(jnp.int32, (1, SLOTS), 1) < count_ref[...]
    place = jnp.broadcast_to(jnp.where(live, place, -1), (8, SLOTS)).T[:, 0:1]
    ids = lax.broadcasted_iota(jnp.int32, (SLOTS, 1), 0)
    hit = place == lax.broadcasted_iota(jnp.int32, (SLOTS, 512), 1)
    slot_v[...] = jnp.min(jnp.where(hit, ids, SLOTS), axis=0, keepdims=True)
    to_smem = pltpu.make_async_copy(slot_v, slot_ref, slot_sem)
    to_smem.start()
    pl.semaphore_wait(barrier, len(where))

    def densify(lo, hi):
        def row(r, carry):
            for col in range(lo * 4, hi * 4):
                s = slot_ref[0, r * 32 + col]
                xd[pl.ds(pl.multiple_of(r * BLK, BLK), BLK), col * BLK:(col + 1) * BLK] = tiles[s]
            return carry
        lax.fori_loop(0, ROWS // BLK, row, 0)

    def gather(h):
        hs = slice(h * R, (h + 1) * R)
        a, b = slice(0, GA), slice(GA, BLK)
        cut = {0: GA + 48, 1: GA + 32}
        m = {}

        def bx(k):
            lo, hi = GROUPS[k]
            m["bx+", k] = send(q.at[lo:hi, 0, b, hs], q.at[lo:hi, 3, b, hs], "x+")
            m["bx-", k] = send(q.at[lo:hi, 0, b, hs], q.at[lo:hi, 1, b, hs], "x-")

        def bxf(k):
            lo, hi = GROUPS[k]
            e = cut[k % 2]
            m["bx+", k].wait_recv()
            m["bf+", k] = send(q.at[lo:hi, 3, GA:e, hs], q.at[lo:hi, 2, GA:e, hs], "x+")
            m["bx-", k].wait_recv()
            m["bf-", k] = send(q.at[lo:hi, 1, e:BLK, hs], q.at[lo:hi, 2, e:BLK, hs], "x-")

        def az(d):
            lo, hi = (0, 4) if d < 4 else (0, 2)
            m["az+", d] = send(q.at[ORDER[1 - d], lo:hi, a, hs],
                               q.at[ORDER[-d if d < 4 else 4], lo:hi, a, hs], "z+")
            lo, hi = (0, 4) if d < 4 else (2, 4)
            m["az-", d] = send(q.at[ORDER[d - 1], lo:hi, a, hs], q.at[ORDER[d], lo:hi, a, hs], "z-")

        def bz(d):
            e = BLK if d < 4 else GA + 48
            m["bz+", d] = send(q.at[ORDER[1 - d], 0, GA:e, hs],
                               q.at[ORDER[-d if d < 4 else 4], 0, GA:e, hs], "z+")
            s = GA if d < 4 else GA + 48
            m["bz-", d] = send(q.at[ORDER[d - 1], 0, s:BLK, hs], q.at[ORDER[d], 0, s:BLK, hs], "z-")

        def wait(kind, d):
            m[kind + "+", d].wait_recv()
            m[kind + "-", d].wait_recv()

        m["ax+"] = send(q.at[0, 0, a, hs], q.at[0, 3, a, hs], "x+")
        m["ax-"] = send(q.at[0, 0, a, hs], q.at[0, 1, a, hs], "x-")
        bz(1)
        bx(0)
        yield
        m["ax+"].wait_recv()
        m["af+"] = send(q.at[0, 3, 0:32, hs], q.at[0, 2, 0:32, hs], "x+")
        m["ax-"].wait_recv()
        m["af-"] = send(q.at[0, 1, 32:GA, hs], q.at[0, 2, 32:GA, hs], "x-")
        wait("bz", 1)
        bz(2)
        bx(1)
        m["af+"].wait_recv()
        m["af-"].wait_recv()
        az(1)
        bxf(0)
        yield
        wait("az", 1)
        az(2)
        wait("bz", 2)
        bz(3)
        bx(2)
        bxf(1)
        wait("bf", 0)
        if h == 0:
            to_smem.wait()
            for load in loads:
                load.wait()
            densify(*GROUPS[0])
        cells_group(0, h)
        yield
        wait("az", 2)
        az(3)
        wait("bz", 3)
        bz(4)
        bx(3)
        bxf(2)
        wait("bf", 1)
        if h == 0:
            densify(*GROUPS[1])
        cells_group(1, h)
        yield
        wait("az", 3)
        az(4)
        wait("bz", 4)
        bx(4)
        bxf(3)
        wait("bf", 2)
        if h == 0:
            densify(*GROUPS[2])
        cells_group(2, h)
        yield
        bxf(4)
        wait("bf", 3)
        if h == 0:
            densify(*GROUPS[3])
            densify(*GROUPS[4])
        cells_group(3, h)
        wait("az", 4)
        wait("bf", 4)
        yield

    def cells_dot(rows, k, h):
        lo, hi = GROUPS[k]
        right = q[lo:hi, :, :, h * R:(h + 1) * R].reshape((hi - lo) * 512, R)
        return jnp.dot(xd[rows, lo * 512:hi * 512], right, preferred_element_type=F32)

    def cells_group(k, h):
        hs = slice(h * R, (h + 1) * R)

        def step(i, carry):
            rows = pl.ds(pl.multiple_of(i * 256, 256), 256)
            part = cells_dot(rows, k, h)
            p[rows, hs] = part if k == 0 else p[rows, hs] + part
            return carry
        lax.fori_loop(0, ROWS // 256, step, 0)

    def reduce_cells(h):
        hs = slice(h * R, (h + 1) * R)
        half = CHUNK // 2
        m = {}

        def to_pair(i, n):
            rows = pl.ds(i * CHUNK if isinstance(i, int) else pl.multiple_of(i * CHUNK, CHUNK), CHUNK)
            return pltpu.make_async_remote_copy(
                src_ref=p.at[rows, hs], dst_ref=pcr.at[i, :, hs], send_sem=ssem.at[n],
                recv_sem=rsem.at[n], device_id=where["c"], device_id_type=MESH)

        first = len(board.sent)
        pair = [to_pair(i, first + i) for i in range(4)]
        board.sent += pair

        def last(i):
            rows = pl.ds(pl.multiple_of(i * CHUNK, CHUNK), CHUNK)
            p[rows, hs] = p[rows, hs] + cells_dot(rows, 4, h)

        def other_core(i, carry):
            last(i)
            to_pair(i, first + i).start()
            return carry

        def own_core(i, carry):
            last(i)
            return carry

        lax.fori_loop(0, 4, other_core, 0)
        yield
        lax.fori_loop(4, 8, own_core, 0)
        lows = [slice((4 + i) * CHUNK, (4 + i) * CHUNK + half) for i in range(4)]
        highs = [slice((4 + i) * CHUNK + half, (5 + i) * CHUNK) for i in range(4)]

        def own(i):
            rows = slice((4 + i) * CHUNK, (5 + i) * CHUNK)
            pair[i].wait_recv()
            p[rows, hs] = p[rows, hs] + pcr[i, :, hs]

        own(0)
        m["h+"] = send(p.at[lows[0], hs], yr.at[0, :, hs], "y+")
        m["h-"] = send(p.at[highs[0], hs], yr.at[1, :, hs], "y-")
        own(1)
        m["s+"] = send(p.at[highs[1], hs], yr.at[2, :, hs], "y+")
        own(2)
        m["s-"] = send(p.at[lows[2], hs], yr.at[3, :, hs], "y-")
        yield
        m["h+"].wait_recv()
        p[lows[1], hs] = p[lows[1], hs] + yr[0, :, hs]
        m["f+"] = send(p.at[lows[1], hs], yr.at[4, :, hs], "y+")
        m["h-"].wait_recv()
        p[highs[2], hs] = p[highs[2], hs] + yr[1, :, hs]
        m["f-"] = send(p.at[highs[2], hs], yr.at[5, :, hs], "y-")
        own(3)
        yield
        m["s+"].wait_recv()
        m["s-"].wait_recv()
        low = p[lows[3], hs] + yr[3, :, hs]
        high = p[highs[3], hs] + yr[2, :, hs]
        m["f+"].wait_recv()
        m["f-"].wait_recv()
        total = jnp.concatenate([low + yr[4, :, hs], high + yr[5, :, hs]], axis=0)

        def lanes(i):
            return slice(i * CHUNK, (i + 1) * CHUNK)

        mid = h * R + R // 2
        up, down = slice(h * R, mid), slice(mid, (h + 1) * R)
        cbt[hs, lanes(7)] = total.T.astype(BF)
        m["g+"] = send(cbt.at[hs, lanes(7)], cbt.at[hs, lanes(6)], "y+")
        m["g-"] = send(cbt.at[hs, lanes(7)], cbt.at[hs, lanes(5)], "y-")
        m["c3"] = send(cbt.at[hs, lanes(7)], cbt.at[hs, lanes(3)], "c")
        yield
        m["g+"].wait_recv()
        m["k+"] = send(cbt.at[up, lanes(6)], cbt.at[up, lanes(4)], "y+")
        m["c2"] = send(cbt.at[hs, lanes(6)], cbt.at[hs, lanes(2)], "c")
        m["g-"].wait_recv()
        m["k-"] = send(cbt.at[down, lanes(5)], cbt.at[down, lanes(4)], "y-")
        m["c1"] = send(cbt.at[hs, lanes(5)], cbt.at[hs, lanes(1)], "c")
        yield
        m["k+"].wait_recv()
        m["k-"].wait_recv()
        m["c0"] = send(cbt.at[hs, lanes(4)], cbt.at[hs, lanes(0)], "c")
        for i in range(4):
            m["c%d" % i].wait_recv()
        yield

    def reduce_genes(h):
        hs = slice(h * R, (h + 1) * R)
        a = slice(h * R, h * R + RA)
        b1 = slice(h * R + RA, h * R + RA + RB1)
        b2 = slice(h * R + RA + RB1, (h + 1) * R)
        v1, v2 = slice(0, RB1), slice(RB1, RB)
        m = {}

        def genes(lo, hi):
            def step(i, carry):
                cols = pl.ds(pl.multiple_of(i * 256, 256), 256)
                zt[i // 2, i % 2, hs] = jnp.dot(cbt[hs, :], xd[:, cols], preferred_element_type=F32)
                return carry
            lax.fori_loop(lo * 2, hi * 2, step, 0)

        def lanes(dx):
            return slice(dx * BLK, (dx + 1) * BLK)

        def part(n, rows, dx):
            return zt[n, dx // 2, rows, lanes(dx % 2)]

        def a_z(d):
            if d == 4:
                as_p[h, 3, :, 0:256] = zt[7, 0, a].astype(BF)
                m["az+", 4] = send(as_p.at[h, 3, :, 0:256], ar_p.at[h, 3, :, 0:256], "z+")
                as_m[h, 3, :, 0:256] = zt[7, 1, a].astype(BF)
                m["az-", 4] = send(as_m.at[h, 3, :, 0:256], ar_m.at[h, 3, :, 0:256], "z-")
                return
            i = d - 1
            m["az+", d + 1].wait_recv()
            lo, hi = slice(0, 256), slice(256, 512)
            as_p[h, i, :, lo] = (zt[ORDER[d], 0, a] + ar_p[h, i + 1, :, lo].astype(F32)).astype(BF)
            high = zt[ORDER[d], 1, a]
            if d < 3:
                high = high + ar_p[h, i + 1, :, hi].astype(F32)
            as_p[h, i, :, hi] = high.astype(BF)
            m["az+", d] = send(as_p.at[h, i], ar_p.at[h, i], "z+")
            m["az-", d + 1].wait_recv()
            low = zt[ORDER[-d], 0, a]
            if d < 3:
                low = low + ar_m[h, i + 1, :, lo].astype(F32)
            as_m[h, i, :, lo] = low.astype(BF)
            far = lo if d == 3 else hi
            as_m[h, i, :, hi] = (zt[ORDER[-d], 1, a] + ar_m[h, i + 1, :, far].astype(F32)).astype(BF)
            m["az-", d] = send(as_m.at[h, i], ar_m.at[h, i], "z-")

        def b_send(kind, k, value, to):
            lo, hi = GROUPS[k]
            rows = v1 if kind in (0, 3, 4) else slice(0, RB - RB1)
            bs[h, kind, lo:hi, rows] = value.astype(BF)
            m["b", kind, k] = send(bs.at[h, kind, lo:hi, rows], br.at[h, kind, lo:hi, rows], to)

        def b_got(kind, k):
            lo, hi = GROUPS[k]
            rows = v1 if kind in (0, 3, 4) else slice(0, RB - RB1)
            m["b", kind, k].wait_recv()
            return br[h, kind, lo:hi, rows].astype(F32)

        def b_first(k):
            lo, hi = GROUPS[k]
            b_send(0, k, part(slice(lo, hi), b1, 2), "x+")
            b_send(1, k, part(slice(lo, hi), b2, 2), "x-")
            b_send(2, k, part(slice(lo, hi), b2, 1), "x+")
            b_send(3, k, part(slice(lo, hi), b1, 3), "x-")

        def b_merge(k):
            lo, hi = GROUPS[k]
            b_send(4, k, part(slice(lo, hi), b1, 1) + b_got(0, k), "x+")
            b_send(5, k, part(slice(lo, hi), b2, 3) + b_got(1, k), "x-")

        def b_total(k):
            lo, hi = GROUPS[k]
            zb[h, lo:hi, v1] = part(slice(lo, hi), b1, 0) + b_got(3, k) + b_got(4, k)
            zb[h, lo:hi, v2] = part(slice(lo, hi), b2, 0) + b_got(2, k) + b_got(5, k)

        def b_z(d):
            if d == 4:
                m["bz+", 4] = send(zb.at[h, 7, v1], bzr_p.at[h, 3, v1], "z+")
                m["bz-", 4] = send(zb.at[h, 7, v2], bzr_m.at[h, 3, v2], "z-")
                return
            i = d - 1
            up = v1 if d == 3 else slice(0, RB)
            down = v2 if d == 3 else slice(0, RB)
            m["bz+", d + 1].wait_recv()
            zb[h, ORDER[d], up] = zb[h, ORDER[d], up] + bzr_p[h, i + 1, up]
            m["bz+", d] = send(zb.at[h, ORDER[d]], bzr_p.at[h, i], "z+")
            m["bz-", d + 1].wait_recv()
            zb[h, ORDER[-d], down] = zb[h, ORDER[-d], down] + bzr_m[h, i + 1, down]
            m["bz-", d] = send(zb.at[h, ORDER[-d]], bzr_m.at[h, i], "z-")

        genes(7, 8)
        a_z(4)
        b_first(4)
        yield
        genes(5, 7)
        a_z(3)
        b_first(3)
        b_merge(4)
        yield
        genes(3, 5)
        a_z(2)
        b_first(2)
        b_merge(3)
        b_total(4)
        b_z(4)
        yield
        genes(0, 3)
        a_z(1)
        b_first(1)
        b_merge(2)
        b_total(3)
        b_z(3)
        yield
        b_first(0)
        b_merge(1)
        b_total(2)
        b_z(2)
        m["az+", 1].wait_recv()
        m["az-", 1].wait_recv()
        for i in range(2):
            cols = slice(i * 256, (i + 1) * 256)
            za[h, :, cols] = zt[0, i, a] + ar_p[h, 0, :, cols].astype(F32) + ar_m[h, 0, :, cols].astype(F32)
        r1, r2 = slice(0, RA // 2), slice(RA // 2, RA)
        m["a0"] = send(za.at[h, r1, lanes(2)], axr.at[h, 0], "x+")
        m["a1"] = send(za.at[h, r2, lanes(2)], axr.at[h, 1], "x-")
        m["a2"] = send(za.at[h, r2, lanes(1)], axr.at[h, 2], "x+")
        m["a3"] = send(za.at[h, r1, lanes(3)], axr.at[h, 3], "x-")
        yield
        b_merge(0)
        b_total(1)
        b_z(1)
        m["a0"].wait_recv()
        za[h, r1, lanes(1)] = za[h, r1, lanes(1)] + axr[h, 0]
        m["a4"] = send(za.at[h, r1, lanes(1)], axr.at[h, 4], "x+")
        m["a1"].wait_recv()
        za[h, r2, lanes(3)] = za[h, r2, lanes(3)] + axr[h, 1]
        m["a5"] = send(za.at[h, r2, lanes(3)], axr.at[h, 5], "x-")
        b_total(0)
        yield
        for i in range(2, 6):
            m["a%d" % i].wait_recv()
        top = jnp.concatenate([za[h, r1, lanes(0)] + axr[h, 3] + axr[h, 4],
                               za[h, r2, lanes(0)] + axr[h, 2] + axr[h, 5]], axis=0)
        m["bz+", 1].wait_recv()
        m["bz-", 1].wait_recv()
        bottom = zb[h, 0] + bzr_p[h, 0] + bzr_m[h, 0]
        out[:, hs] = jnp.concatenate([top, bottom], axis=0).T
        yield

    for h in range(NH):
        for stage in (gather, reduce_cells, reduce_genes):
            for _ in stage(h):
                pass

    for copy in board.sent:
        copy.wait_send()


def local(block_tiles, block_coords, block_counts, basis_rows):
    vmem = pl.BlockSpec(memory_space=pltpu.VMEM)
    return pl.pallas_call(
        kernel,
        out_shape=jax.ShapeDtypeStruct((BLK, RANK), F32),
        in_specs=[vmem, vmem, pl.BlockSpec(memory_space=pl.ANY), vmem],
        out_specs=vmem,
        scratch_shapes=[
            pltpu.VMEM((SLOTS + 1, BLK, BLK), BF),
            pltpu.VMEM((ROWS, COLS), BF),
            pltpu.VMEM((NZ, NX, BLK, RANK), BF),
            pltpu.VMEM((ROWS, RANK), F32),
            pltpu.VMEM((4, CHUNK, RANK), F32),
            pltpu.VMEM((6, CHUNK // 2, RANK), F32),
            pltpu.VMEM((RANK, ROWS), BF),
            pltpu.VMEM((NZ, 2, RANK, 256), F32),
            pltpu.VMEM((NH, RA, 512), F32),
            pltpu.VMEM((NH, NZ, RB, BLK), F32),
            pltpu.VMEM((NH, 4, RA, 512), BF),
            pltpu.VMEM((NH, 4, RA, 512), BF),
            pltpu.VMEM((NH, 4, RA, 512), BF),
            pltpu.VMEM((NH, 4, RA, 512), BF),
            pltpu.VMEM((NH, 6, NZ, RB1, BLK), BF),
            pltpu.VMEM((NH, 6, NZ, RB1, BLK), BF),
            pltpu.VMEM((NH, 6, RA // 2, BLK), F32),
            pltpu.VMEM((NH, 4, RB, BLK), F32),
            pltpu.VMEM((NH, 4, RB, BLK), F32),
            pltpu.VMEM((1, 512), jnp.int32),
            pltpu.SMEM((1, 512), jnp.int32),
            pltpu.SemaphoreType.DMA((N_SEM,)),
            pltpu.SemaphoreType.DMA((N_SEM,)),
            pltpu.SemaphoreType.DMA((8,)),
            pltpu.SemaphoreType.DMA,
        ],
        compiler_params=pltpu.CompilerParams(
            collective_id=0, has_side_effects=True, vmem_limit_bytes=60 * 1024 * 1024),
        cost_estimate=pl.CostEstimate(flops=4 * ROWS * COLS * RANK, bytes_accessed=11_000_000,
                                      transcendentals=0),
    )(block_counts, block_coords.T, block_tiles, basis_rows)


def solution(mesh):
    return jax.shard_map(
        local,
        mesh=mesh,
        in_specs=(
            P("cells", "genes", None),
            P("cells", "genes"),
            P("cells", "genes"),
            P(("cells", "genes"), None),
        ),
        out_specs=P(("cells", "genes"), None),
        check_vma=False,
    )
```

```python
import functools

import jax
import jax.numpy as jnp
from jax import lax
from jax.experimental import pallas as pl
from jax.experimental.pallas import tpu as pltpu
from jax.sharding import PartitionSpec as P

MESH = pl.DeviceIdType.MESH
BF = jnp.bfloat16
F32 = jnp.float32

NX, NY, NZ = 4, 4, 8
BLK = 128
RANK = 256
ROWS = 2048
COLS = 4096
CHUNK = 256
SLOTS = 320
GA = 48

ORDER = {0: 0, 1: 1, -1: 2, 2: 3, -2: 4, 3: 5, -3: 6, 4: 7}
GROUPS = ((0, 1), (1, 3), (3, 5), (5, 7), (7, 8))

NH = 1
R = RANK // NH
RA = 96 // NH
RB = R - RA
RB1 = 80 if NH == 1 else 48
N_SEM = 120 * NH


class Board:
    def __init__(self, ssem, rsem, where):
        self.ssem, self.rsem, self.where = ssem, rsem, where
        self.sent = []

    def send(self, src, dst, to):
        n = len(self.sent)
        copy = pltpu.make_async_remote_copy(
            src_ref=src, dst_ref=dst, send_sem=self.ssem.at[n], recv_sem=self.rsem.at[n],
            device_id=self.where[to], device_id_type=MESH)
        copy.start()
        self.sent.append(copy)
        return copy


def gather_kernel(count_ref, coords, tiles_hbm, basis, q, xd_out, tiles, xd,
                  slot_v, slot_ref, ssem, rsem, tsem, slot_sem, out_sem):
    c = lax.axis_index("cells")
    g = lax.axis_index("genes")
    z, x = c // NX, c % NX
    y, core = g // 2, g % 2

    def at(dz, dx, dy, dc):
        return (((z + dz + NZ) % NZ) * NX + (x + dx + NX) % NX,
                ((y + dy + NY) % NY) * 2 + (core + dc) % 2)

    where = {
        "x+": at(0, 1, 0, 0), "x-": at(0, -1, 0, 0),
        "z+": at(1, 0, 0, 0), "z-": at(-1, 0, 0, 0),
        "y+": at(0, 0, 1, 0), "y-": at(0, 0, -1, 0),
        "c": at(0, 0, 0, 1),
    }
    board = Board(ssem, rsem, where)
    send = board.send

    n_loads = 8
    per = SLOTS // n_loads
    loads = [pltpu.make_async_copy(tiles_hbm.at[pl.ds(i * per, per)],
                                   tiles.at[pl.ds(i * per, per)], tsem.at[i]) for i in range(n_loads)]
    for load in loads:
        load.start()

    barrier = pltpu.get_barrier_semaphore()
    for to in where.values():
        pl.semaphore_signal(barrier, inc=1, device_id=to, device_id_type=MESH)
    q[0, 0] = basis[...]
    tiles[SLOTS] = jnp.zeros((BLK, BLK), BF)

    b, k = coords[0:1, :], coords[1:2, :]
    chunk = lax.shift_right_logical(b, 1)
    dy = ((chunk & 3) - y) & 3
    dy = jnp.where(dy == 0, 3, jnp.where(dy == 3, 2, 2 - dy))
    pos = jnp.where(lax.shift_right_logical(chunk, 2) == core, 4, 0) + dy
    dz = (lax.shift_right_logical(k, 2) - z) & 7
    dz = jnp.where(dz == 0, 0, jnp.where(dz <= 3, 2 * dz - 1, jnp.where(dz == 4, 7, 2 * (NZ - dz))))
    place = (pos * 2 + (b & 1)) * 32 + dz * NX + (((k & 3) - x) & 3)
    live = lax.broadcasted_iota(jnp.int32, (1, SLOTS), 1) < count_ref[...]
    place = jnp.broadcast_to(jnp.where(live, place, -1), (8, SLOTS)).T[:, 0:1]
    ids = lax.broadcasted_iota(jnp.int32, (SLOTS, 1), 0)
    hit = place == lax.broadcasted_iota(jnp.int32, (SLOTS, 512), 1)
    slot_v[...] = jnp.min(jnp.where(hit, ids, SLOTS), axis=0, keepdims=True)
    to_smem = pltpu.make_async_copy(slot_v, slot_ref, slot_sem)
    to_smem.start()
    pl.semaphore_wait(barrier, len(where))

    def densify(lo, hi):
        def row(r, carry):
            for col in range(lo * 4, hi * 4):
                s = slot_ref[0, r * 32 + col]
                xd[pl.ds(pl.multiple_of(r * BLK, BLK), BLK), col * BLK:(col + 1) * BLK] = tiles[s]
            return carry
        lax.fori_loop(0, ROWS // BLK, row, 0)

    def gather(h):
        hs = slice(h * R, (h + 1) * R)
        a, b = slice(0, GA), slice(GA, BLK)
        cut = {0: GA + 48, 1: GA + 32}
        m = {}

        def bx(k):
            lo, hi = GROUPS[k]
            m["bx+", k] = send(q.at[lo:hi, 0, b, hs], q.at[lo:hi, 3, b, hs], "x+")
            m["bx-", k] = send(q.at[lo:hi, 0, b, hs], q.at[lo:hi, 1, b, hs], "x-")

        def bxf(k):
            lo, hi = GROUPS[k]
            e = cut[k % 2]
            m["bx+", k].wait_recv()
            m["bf+", k] = send(q.at[lo:hi, 3, GA:e, hs], q.at[lo:hi, 2, GA:e, hs], "x+")
            m["bx-", k].wait_recv()
            m["bf-", k] = send(q.at[lo:hi, 1, e:BLK, hs], q.at[lo:hi, 2, e:BLK, hs], "x-")

        def az(d):
            lo, hi = (0, 4) if d < 4 else (0, 2)
            m["az+", d] = send(q.at[ORDER[1 - d], lo:hi, a, hs],
                               q.at[ORDER[-d if d < 4 else 4], lo:hi, a, hs], "z+")
            lo, hi = (0, 4) if d < 4 else (2, 4)
            m["az-", d] = send(q.at[ORDER[d - 1], lo:hi, a, hs], q.at[ORDER[d], lo:hi, a, hs], "z-")

        def bz(d):
            e = BLK if d < 4 else GA + 48
            m["bz+", d] = send(q.at[ORDER[1 - d], 0, GA:e, hs],
                               q.at[ORDER[-d if d < 4 else 4], 0, GA:e, hs], "z+")
            s = GA if d < 4 else GA + 48
            m["bz-", d] = send(q.at[ORDER[d - 1], 0, s:BLK, hs], q.at[ORDER[d], 0, s:BLK, hs], "z-")

        def wait(kind, d):
            m[kind + "+", d].wait_recv()
            m[kind + "-", d].wait_recv()

        m["ax+"] = send(q.at[0, 0, a, hs], q.at[0, 3, a, hs], "x+")
        m["ax-"] = send(q.at[0, 0, a, hs], q.at[0, 1, a, hs], "x-")
        bz(1)
        bx(0)
        yield
        m["ax+"].wait_recv()
        m["af+"] = send(q.at[0, 3, 0:32, hs], q.at[0, 2, 0:32, hs], "x+")
        m["ax-"].wait_recv()
        m["af-"] = send(q.at[0, 1, 32:GA, hs], q.at[0, 2, 32:GA, hs], "x-")
        wait("bz", 1)
        bz(2)
        bx(1)
        m["af+"].wait_recv()
        m["af-"].wait_recv()
        az(1)
        bxf(0)
        yield
        wait("az", 1)
        az(2)
        wait("bz", 2)
        bz(3)
        bx(2)
        bxf(1)
        wait("bf", 0)
        if h == 0:
            to_smem.wait()
            for load in loads:
                load.wait()
            densify(0, 2)
        yield
        wait("az", 2)
        az(3)
        wait("bz", 3)
        bz(4)
        bx(3)
        bxf(2)
        wait("bf", 1)
        if h == 0:
            densify(2, 4)
        yield
        wait("az", 3)
        az(4)
        wait("bz", 4)
        bx(4)
        bxf(3)
        wait("bf", 2)
        if h == 0:
            densify(4, 6)
        yield
        bxf(4)
        wait("bf", 3)
        if h == 0:
            densify(6, 8)
            to_hbm = pltpu.make_async_copy(xd, xd_out, out_sem)
            to_hbm.start()
            to_hbm.wait()
        wait("az", 4)
        wait("bf", 4)
        yield

    for _ in gather(0):
        pass
    for copy in board.sent:
        copy.wait_send()


def cells_kernel(p_in, cbt, p, pcr, yr, ssem, rsem):
    c = lax.axis_index("cells")
    g = lax.axis_index("genes")
    z, x = c // NX, c % NX
    y, core = g // 2, g % 2

    def at(dz, dx, dy, dc):
        return (((z + dz + NZ) % NZ) * NX + (x + dx + NX) % NX,
                ((y + dy + NY) % NY) * 2 + (core + dc) % 2)

    where = {
        "x+": at(0, 1, 0, 0), "x-": at(0, -1, 0, 0),
        "z+": at(1, 0, 0, 0), "z-": at(-1, 0, 0, 0),
        "y+": at(0, 0, 1, 0), "y-": at(0, 0, -1, 0),
        "c": at(0, 0, 0, 1),
    }
    board = Board(ssem, rsem, where)
    send = board.send

    barrier = pltpu.get_barrier_semaphore()
    for to in where.values():
        pl.semaphore_signal(barrier, inc=1, device_id=to, device_id_type=MESH)
    pl.semaphore_wait(barrier, len(where))

    def reduce_cells(h):
        hs = slice(h * R, (h + 1) * R)
        half = CHUNK // 2
        m = {}

        def to_pair(i, n):
            rows = pl.ds(i * CHUNK if isinstance(i, int) else pl.multiple_of(i * CHUNK, CHUNK), CHUNK)
            return pltpu.make_async_remote_copy(
                src_ref=p_in.at[rows, hs], dst_ref=pcr.at[i, :, hs], send_sem=ssem.at[n],
                recv_sem=rsem.at[n], device_id=where["c"], device_id_type=MESH)

        first = len(board.sent)
        pair = [to_pair(i, first + i) for i in range(4)]
        board.sent += pair

        for copy in pair:
            copy.start()
        yield

        lows = [slice((4 + i) * CHUNK, (4 + i) * CHUNK + half) for i in range(4)]
        highs = [slice((4 + i) * CHUNK + half, (5 + i) * CHUNK) for i in range(4)]

        def own(i):
            rows = slice((4 + i) * CHUNK, (5 + i) * CHUNK)
            pair[i].wait_recv()
            p[rows, hs] = p_in[rows, hs] + pcr[i, :, hs]

        own(0)
        m["h+"] = send(p.at[lows[0], hs], yr.at[0, :, hs], "y+")
        m["h-"] = send(p.at[highs[0], hs], yr.at[1, :, hs], "y-")
        own(1)
        m["s+"] = send(p.at[highs[1], hs], yr.at[2, :, hs], "y+")
        own(2)
        m["s-"] = send(p.at[lows[2], hs], yr.at[3, :, hs], "y-")
        yield
        m["h+"].wait_recv()
        p[lows[1], hs] = p[lows[1], hs] + yr[0, :, hs]
        m["f+"] = send(p.at[lows[1], hs], yr.at[4, :, hs], "y+")
        m["h-"].wait_recv()
        p[highs[2], hs] = p[highs[2], hs] + yr[1, :, hs]
        m["f-"] = send(p.at[highs[2], hs], yr.at[5, :, hs], "y-")
        own(3)
        yield
        m["s+"].wait_recv()
        m["s-"].wait_recv()
        low = p[lows[3], hs] + yr[3, :, hs]
        high = p[highs[3], hs] + yr[2, :, hs]
        m["f+"].wait_recv()
        m["f-"].wait_recv()
        total = jnp.concatenate([low + yr[4, :, hs], high + yr[5, :, hs]], axis=0)

        def lanes(i):
            return slice(i * CHUNK, (i + 1) * CHUNK)

        mid = h * R + R // 2
        up, down = slice(h * R, mid), slice(mid, (h + 1) * R)
        cbt[hs, lanes(7)] = total.T.astype(BF)
        m["g+"] = send(cbt.at[hs, lanes(7)], cbt.at[hs, lanes(6)], "y+")
        m["g-"] = send(cbt.at[hs, lanes(7)], cbt.at[hs, lanes(5)], "y-")
        m["c3"] = send(cbt.at[hs, lanes(7)], cbt.at[hs, lanes(3)], "c")
        yield
        m["g+"].wait_recv()
        m["k+"] = send(cbt.at[up, lanes(6)], cbt.at[up, lanes(4)], "y+")
        m["c2"] = send(cbt.at[hs, lanes(6)], cbt.at[hs, lanes(2)], "c")
        m["g-"].wait_recv()
        m["k-"] = send(cbt.at[down, lanes(5)], cbt.at[down, lanes(4)], "y-")
        m["c1"] = send(cbt.at[hs, lanes(5)], cbt.at[hs, lanes(1)], "c")
        yield
        m["k+"].wait_recv()
        m["k-"].wait_recv()
        m["c0"] = send(cbt.at[hs, lanes(4)], cbt.at[hs, lanes(0)], "c")
        for i in range(4):
            m["c%d" % i].wait_recv()
        yield

    for _ in reduce_cells(0):
        pass
    for copy in board.sent:
        copy.wait_send()


def genes_kernel(zt, out, za, zb, as_p, as_m, ar_p, ar_m, bs, br, axr, bzr_p, bzr_m, ssem, rsem):
    c = lax.axis_index("cells")
    g = lax.axis_index("genes")
    z, x = c // NX, c % NX
    y, core = g // 2, g % 2

    def at(dz, dx, dy, dc):
        return (((z + dz + NZ) % NZ) * NX + (x + dx + NX) % NX,
                ((y + dy + NY) % NY) * 2 + (core + dc) % 2)

    where = {
        "x+": at(0, 1, 0, 0), "x-": at(0, -1, 0, 0),
        "z+": at(1, 0, 0, 0), "z-": at(-1, 0, 0, 0),
        "y+": at(0, 0, 1, 0), "y-": at(0, 0, -1, 0),
        "c": at(0, 0, 0, 1),
    }
    board = Board(ssem, rsem, where)
    send = board.send

    barrier = pltpu.get_barrier_semaphore()
    for to in where.values():
        pl.semaphore_signal(barrier, inc=1, device_id=to, device_id_type=MESH)
    pl.semaphore_wait(barrier, len(where))

    def reduce_genes(h):
        hs = slice(h * R, (h + 1) * R)
        a = slice(h * R, h * R + RA)
        b1 = slice(h * R + RA, h * R + RA + RB1)
        b2 = slice(h * R + RA + RB1, (h + 1) * R)
        v1, v2 = slice(0, RB1), slice(RB1, RB)
        m = {}

        def lanes(dx):
            return slice(dx * BLK, (dx + 1) * BLK)

        def plane(n, i):
            return zt[a, n * 512 + i * 256:n * 512 + (i + 1) * 256]

        def part(n, rows, dx):
            return jnp.stack([zt[rows, i * 512 + dx * BLK:i * 512 + (dx + 1) * BLK]
                              for i in range(n.start, n.stop)])

        def a_z(d):
            if d == 4:
                as_p[h, 3, :, 0:256] = plane(7, 0).astype(BF)
                m["az+", 4] = send(as_p.at[h, 3, :, 0:256], ar_p.at[h, 3, :, 0:256], "z+")
                as_m[h, 3, :, 0:256] = plane(7, 1).astype(BF)
                m["az-", 4] = send(as_m.at[h, 3, :, 0:256], ar_m.at[h, 3, :, 0:256], "z-")
                return
            i = d - 1
            m["az+", d + 1].wait_recv()
            lo, hi = slice(0, 256), slice(256, 512)
            as_p[h, i, :, lo] = (plane(ORDER[d], 0) + ar_p[h, i + 1, :, lo].astype(F32)).astype(BF)
            high = plane(ORDER[d], 1)
            if d < 3:
                high = high + ar_p[h, i + 1, :, hi].astype(F32)
            as_p[h, i, :, hi] = high.astype(BF)
            m["az+", d] = send(as_p.at[h, i], ar_p.at[h, i], "z+")
            m["az-", d + 1].wait_recv()
            low = plane(ORDER[-d], 0)
            if d < 3:
                low = low + ar_m[h, i + 1, :, lo].astype(F32)
            as_m[h, i, :, lo] = low.astype(BF)
            far = lo if d == 3 else hi
            as_m[h, i, :, hi] = (plane(ORDER[-d], 1) + ar_m[h, i + 1, :, far].astype(F32)).astype(BF)
            m["az-", d] = send(as_m.at[h, i], ar_m.at[h, i], "z-")

        def b_send(kind, k, value, to):
            lo, hi = GROUPS[k]
            rows = v1 if kind in (0, 3, 4) else slice(0, RB - RB1)
            bs[h, kind, lo:hi, rows] = value.astype(BF)
            m["b", kind, k] = send(bs.at[h, kind, lo:hi, rows], br.at[h, kind, lo:hi, rows], to)

        def b_got(kind, k):
            lo, hi = GROUPS[k]
            rows = v1 if kind in (0, 3, 4) else slice(0, RB - RB1)
            m["b", kind, k].wait_recv()
            return br[h, kind, lo:hi, rows].astype(F32)

        def b_first(k):
            lo, hi = GROUPS[k]
            b_send(0, k, part(slice(lo, hi), b1, 2), "x+")
            b_send(1, k, part(slice(lo, hi), b2, 2), "x-")
            b_send(2, k, part(slice(lo, hi), b2, 1), "x+")
            b_send(3, k, part(slice(lo, hi), b1, 3), "x-")

        def b_merge(k):
            lo, hi = GROUPS[k]
            b_send(4, k, part(slice(lo, hi), b1, 1) + b_got(0, k), "x+")
            b_send(5, k, part(slice(lo, hi), b2, 3) + b_got(1, k), "x-")

        def b_total(k):
            lo, hi = GROUPS[k]
            zb[h, lo:hi, v1] = part(slice(lo, hi), b1, 0) + b_got(3, k) + b_got(4, k)
            zb[h, lo:hi, v2] = part(slice(lo, hi), b2, 0) + b_got(2, k) + b_got(5, k)

        def b_z(d):
            if d == 4:
                m["bz+", 4] = send(zb.at[h, 7, v1], bzr_p.at[h, 3, v1], "z+")
                m["bz-", 4] = send(zb.at[h, 7, v2], bzr_m.at[h, 3, v2], "z-")
                return
            i = d - 1
            up = v1 if d == 3 else slice(0, RB)
            down = v2 if d == 3 else slice(0, RB)
            m["bz+", d + 1].wait_recv()
            zb[h, ORDER[d], up] = zb[h, ORDER[d], up] + bzr_p[h, i + 1, up]
            m["bz+", d] = send(zb.at[h, ORDER[d]], bzr_p.at[h, i], "z+")
            m["bz-", d + 1].wait_recv()
            zb[h, ORDER[-d], down] = zb[h, ORDER[-d], down] + bzr_m[h, i + 1, down]
            m["bz-", d] = send(zb.at[h, ORDER[-d]], bzr_m.at[h, i], "z-")

        a_z(4)
        b_first(4)
        yield
        a_z(3)
        b_first(3)
        b_merge(4)
        yield
        a_z(2)
        b_first(2)
        b_merge(3)
        b_total(4)
        b_z(4)
        yield
        a_z(1)
        b_first(1)
        b_merge(2)
        b_total(3)
        b_z(3)
        yield
        b_first(0)
        b_merge(1)
        b_total(2)
        b_z(2)
        m["az+", 1].wait_recv()
        m["az-", 1].wait_recv()
        for i in range(2):
            cols = slice(i * 256, (i + 1) * 256)
            za[h, :, cols] = plane(0, i) + ar_p[h, 0, :, cols].astype(F32) + ar_m[h, 0, :, cols].astype(F32)
        r1, r2 = slice(0, RA // 2), slice(RA // 2, RA)
        m["a0"] = send(za.at[h, r1, lanes(2)], axr.at[h, 0], "x+")
        m["a1"] = send(za.at[h, r2, lanes(2)], axr.at[h, 1], "x-")
        m["a2"] = send(za.at[h, r2, lanes(1)], axr.at[h, 2], "x+")
        m["a3"] = send(za.at[h, r1, lanes(3)], axr.at[h, 3], "x-")
        yield
        b_merge(0)
        b_total(1)
        b_z(1)
        m["a0"].wait_recv()
        za[h, r1, lanes(1)] = za[h, r1, lanes(1)] + axr[h, 0]
        m["a4"] = send(za.at[h, r1, lanes(1)], axr.at[h, 4], "x+")
        m["a1"].wait_recv()
        za[h, r2, lanes(3)] = za[h, r2, lanes(3)] + axr[h, 1]
        m["a5"] = send(za.at[h, r2, lanes(3)], axr.at[h, 5], "x-")
        b_total(0)
        yield
        for i in range(2, 6):
            m["a%d" % i].wait_recv()
        top = jnp.concatenate([za[h, r1, lanes(0)] + axr[h, 3] + axr[h, 4],
                               za[h, r2, lanes(0)] + axr[h, 2] + axr[h, 5]], axis=0)
        m["bz+", 1].wait_recv()
        m["bz-", 1].wait_recv()
        bottom = zb[h, 0] + bzr_p[h, 0] + bzr_m[h, 0]
        out[:, hs] = jnp.concatenate([top, bottom], axis=0).T
        yield

    for _ in reduce_genes(0):
        pass
    for copy in board.sent:
        copy.wait_send()


def call(kernel, n, outs, ins, scratch):
    vmem = pl.BlockSpec(memory_space=pltpu.VMEM)
    return pl.pallas_call(
        kernel,
        out_shape=[jax.ShapeDtypeStruct(shape, dtype) for shape, dtype, _ in outs],
        in_specs=[pl.BlockSpec(memory_space=pl.ANY) if len(a.shape) == 3 else vmem for a in ins],
        out_specs=[vmem if kept else pl.BlockSpec(memory_space=pl.ANY) for _, _, kept in outs],
        scratch_shapes=scratch + [pltpu.SemaphoreType.DMA((N_SEM,)), pltpu.SemaphoreType.DMA((N_SEM,))] + (
            [pltpu.SemaphoreType.DMA((8,)), pltpu.SemaphoreType.DMA, pltpu.SemaphoreType.DMA] if n == 0 else []),
        compiler_params=pltpu.CompilerParams(
            collective_id=n, has_side_effects=True, vmem_limit_bytes=60 * 1024 * 1024),
    )(*ins)


def local(block_tiles, block_coords, block_counts, basis_rows):
    q, xd = call(gather_kernel, 0, [((NZ, NX, BLK, RANK), BF, True), ((ROWS, COLS), BF, False)],
                 [block_counts, block_coords.T, block_tiles, basis_rows], [
        pltpu.VMEM((SLOTS + 1, BLK, BLK), BF),
        pltpu.VMEM((ROWS, COLS), BF),
        pltpu.VMEM((1, 512), jnp.int32),
        pltpu.SMEM((1, 512), jnp.int32),
    ])
    part = jnp.dot(xd, q.reshape(COLS, RANK), preferred_element_type=F32)
    cbt, = call(cells_kernel, 1, [((RANK, ROWS), BF, True)], [part], [
        pltpu.VMEM((ROWS, RANK), F32),
        pltpu.VMEM((4, CHUNK, RANK), F32),
        pltpu.VMEM((6, CHUNK // 2, RANK), F32),
    ])
    zt = jnp.dot(cbt, xd, preferred_element_type=F32)
    out, = call(genes_kernel, 2, [((BLK, RANK), F32, True)], [zt], [
        pltpu.VMEM((NH, RA, 512), F32),
        pltpu.VMEM((NH, NZ, RB, BLK), F32),
        pltpu.VMEM((NH, 4, RA, 512), BF),
        pltpu.VMEM((NH, 4, RA, 512), BF),
        pltpu.VMEM((NH, 4, RA, 512), BF),
        pltpu.VMEM((NH, 4, RA, 512), BF),
        pltpu.VMEM((NH, 6, NZ, RB1, BLK), BF),
        pltpu.VMEM((NH, 6, NZ, RB1, BLK), BF),
        pltpu.VMEM((NH, 6, RA // 2, BLK), F32),
        pltpu.VMEM((NH, 4, RB, BLK), F32),
        pltpu.VMEM((NH, 4, RB, BLK), F32),
    ])
    return out


def solution(mesh):
    return jax.shard_map(
        local,
        mesh=mesh,
        in_specs=(
            P("cells", "genes", None),
            P("cells", "genes"),
            P("cells", "genes"),
            P(("cells", "genes"), None),
        ),
        out_specs=P(("cells", "genes"), None),
        check_vma=False,
    )
```

```python
import jax
import jax.numpy as jnp
import numpy as np
from jax import lax
from jax.experimental import pallas as pl
from jax.experimental.pallas import tpu as pltpu
from jax.sharding import PartitionSpec as P

MESH = pl.DeviceIdType.MESH
BF = jnp.bfloat16
F32 = jnp.float32

NX, NY, NZ = 4, 4, 8
BLK = 128
RANK = 256
ROWS = 2048
COLS = 4096
CHUNK = 256
HALF = CHUNK // 2
SLOTS = 320
GA = 48
RA = 96
RB = RANK - RA
RB1 = 80

ORDER = {0: 0, 1: 1, -1: 2, 2: 3, -2: 4, 3: 5, -3: 6, 4: 7, -4: 7}
GROUPS = ((0, 1), (1, 3), (3, 5), (5, 7), (7, 8))
SIGNS = (("+", 1), ("-", -1))

HOP = 1.5
LINK = {"x+": 50e3, "x-": 50e3, "z+": 50e3, "z-": 50e3, "y+": 50e3, "y-": 50e3, "c": 500e3}
ISSUE = 0.08
N_SEM = 136


class Plan:
    def __init__(self, ssem, rsem, where):
        self.ssem, self.rsem, self.where = ssem, rsem, where
        self.tasks = {}
        self.count = 0

    def task(self, name, needs, cost, run, message=None):
        assert name not in self.tasks, name
        self.tasks[name] = (tuple(needs), cost, run, message)

    def send(self, name, needs, src, dst, to, run=None, cost=0.0):
        copy = pltpu.make_async_remote_copy(
            src_ref=src, dst_ref=dst, send_sem=self.ssem.at[self.count],
            recv_sem=self.rsem.at[self.count], device_id=self.where[to], device_id_type=MESH)
        self.count += 1
        time = float(np.prod(src.shape)) * np.dtype(src.dtype).itemsize / LINK[to]
        self.task(name, needs, cost + ISSUE, run, (copy, to, time))

    def order(self):
        after = {name: [] for name in self.tasks}
        for name, (needs, *_) in self.tasks.items():
            for need in needs:
                after[need].append(name)
        rank = {}

        def longest(name):
            if name not in rank:
                _, cost, _, message = self.tasks[name]
                tail = max([longest(n) for n in after[name]], default=0.0)
                rank[name] = cost + (message[2] + HOP if message else 0.0) + tail
            return rank[name]

        for name in self.tasks:
            longest(name)
        now, free, ready_at, order = 0.0, {}, {}, []
        left = dict.fromkeys(self.tasks)
        while left:
            can = {n: max([ready_at[d] for d in self.tasks[n][0]], default=0.0)
                   for n in left if all(d in ready_at for d in self.tasks[n][0])}
            now = max(now, min(can.values()))
            name = max((n for n in can if can[n] <= now), key=lambda n: rank[n])
            del left[name]
            order.append(name)
            _, cost, _, message = self.tasks[name]
            now += cost
            ready_at[name] = now
            if message:
                _, to, time = message
                free[to] = max(now, free.get(to, 0.0)) + time
                ready_at[name] = free[to] + HOP
        self.finish, self.ready_at = now, ready_at
        return order

    def run(self):
        got = set()
        assert self.count <= N_SEM
        order = self.order()
        for name in order:
            needs, _, run, message = self.tasks[name]
            for need in needs:
                if self.tasks[need][3] and need not in got:
                    self.tasks[need][3][0].wait_recv()
                    got.add(need)
            if run:
                run()
            if message:
                message[0].start()
        for name in order:
            if self.tasks[name][3]:
                assert name in got, name
                self.tasks[name][3][0].wait_send()


def kernel(count_ref, coords, tiles_hbm, basis, out, tiles, xd, q, p, pcr, yr, cbt, zt,
           za, zb, azs, azr, axr, bs, br, bzr, slot_v, slot_ref, ssem, rsem, tsem, slot_sem):
    c = lax.axis_index("cells")
    g = lax.axis_index("genes")
    z, x = c // NX, c % NX
    y, core = g // 2, g % 2

    def at(dz, dx, dy, dc):
        return (((z + dz + NZ) % NZ) * NX + (x + dx + NX) % NX,
                ((y + dy + NY) % NY) * 2 + (core + dc) % 2)

    where = {
        "x+": at(0, 1, 0, 0), "x-": at(0, -1, 0, 0),
        "z+": at(1, 0, 0, 0), "z-": at(-1, 0, 0, 0),
        "y+": at(0, 0, 1, 0), "y-": at(0, 0, -1, 0),
        "c": at(0, 0, 0, 1),
    }
    plan = Plan(ssem, rsem, where)
    task, send = plan.task, plan.send

    n_loads = 8
    per = SLOTS // n_loads
    loads = [pltpu.make_async_copy(tiles_hbm.at[pl.ds(i * per, per)],
                                   tiles.at[pl.ds(i * per, per)], tsem.at[i]) for i in range(n_loads)]
    for load in loads:
        load.start()

    barrier = pltpu.get_barrier_semaphore()
    for to in where.values():
        pl.semaphore_signal(barrier, inc=1, device_id=to, device_id_type=MESH)
    q[0, 0] = basis[...]
    tiles[SLOTS] = jnp.zeros((BLK, BLK), BF)

    b, k = coords[0:1, :], coords[1:2, :]
    chunk = lax.shift_right_logical(b, 1)
    dy = ((chunk & 3) - y) & 3
    dy = jnp.where(dy == 0, 3, jnp.where(dy == 3, 2, 2 - dy))
    pos = jnp.where(lax.shift_right_logical(chunk, 2) == core, 4, 0) + dy
    dz = (lax.shift_right_logical(k, 2) - z) & 7
    dz = jnp.where(dz == 0, 0, jnp.where(dz <= 3, 2 * dz - 1, jnp.where(dz == 4, 7, 2 * (NZ - dz))))
    dx = ((k & 3) - x) & 3
    dx = jnp.where(dx >= 2, 5 - dx, dx)
    place = (pos * 2 + (b & 1)) * 32 + dz * NX + dx
    live = lax.broadcasted_iota(jnp.int32, (1, SLOTS), 1) < count_ref[...]
    place = jnp.broadcast_to(jnp.where(live, place, -1), (8, SLOTS)).T[:, 0:1]
    ids = lax.broadcasted_iota(jnp.int32, (SLOTS, 1), 0)
    hit = place == lax.broadcasted_iota(jnp.int32, (SLOTS, 512), 1)
    slot_v[...] = jnp.min(jnp.where(hit, ids, SLOTS), axis=0, keepdims=True)
    to_smem = pltpu.make_async_copy(slot_v, slot_ref, slot_sem)
    to_smem.start()
    pl.semaphore_wait(barrier, len(where))

    def densify(lo, hi):
        def row(r, carry):
            for col in range(lo * 4, hi * 4):
                s = slot_ref[0, r * 32 + col]
                xd[pl.ds(pl.multiple_of(r * BLK, BLK), BLK), col * BLK:(col + 1) * BLK] = tiles[s]
            return carry
        lax.fori_loop(0, ROWS // BLK, row, 0)

    def loaded():
        to_smem.wait()
        for load in loads:
            load.wait()

    a, b = slice(0, GA), slice(GA, BLK)
    send("ax+", [], q.at[0, 0, a], q.at[0, 2, a], "x+")
    send("ax-", [], q.at[0, 0, a], q.at[0, 1, a], "x-")
    send("af+", ["ax+"], q.at[0, 2, 0:32], q.at[0, 3, 0:32], "x+")
    send("af-", ["ax-"], q.at[0, 1, 32:GA], q.at[0, 3, 32:GA], "x-")
    for d in range(1, 5):
        for s, sign in SIGNS:
            src, dst = ORDER[-sign * (d - 1)], ORDER[-sign * d]
            last = [f"{d - 1}{s}"] if d > 1 else []
            rows = slice(0, BLK) if d < 4 else slice(0, 64) if sign > 0 else slice(64, BLK)
            send(f"zo{d}{s}", ["zo" + n for n in last], q.at[src, 0, rows], q.at[dst, 0, rows], "z" + s)
            cols = slice(1, 3) if d < 4 else slice(1, 2) if sign > 0 else slice(2, 3)
            send(f"zn{d}{s}", ["zn" + n for n in last] or ["ax+", "ax-"],
                 q.at[src, cols, a], q.at[dst, cols, a], "z" + s)
            rows = a if d < 4 else slice(0, 32) if sign > 0 else slice(32, GA)
            send(f"zf{d}{s}", ["zf" + n for n in last] or ["af+", "af-"],
                 q.at[src, 3, rows], q.at[dst, 3, rows], "z" + s)
    for k, (lo, hi) in enumerate(GROUPS):
        here = [f"zo{k}+", f"zo{k}-"] if k else []
        e = GA + (48 if k % 2 else 32)
        send(f"bx{k}+", here, q.at[lo:hi, 0, b], q.at[lo:hi, 2, b], "x+")
        send(f"bx{k}-", here, q.at[lo:hi, 0, b], q.at[lo:hi, 1, b], "x-")
        send(f"bf{k}+", [f"bx{k}+"], q.at[lo:hi, 2, GA:e], q.at[lo:hi, 3, GA:e], "x+")
        send(f"bf{k}-", [f"bx{k}-"], q.at[lo:hi, 1, e:BLK], q.at[lo:hi, 3, e:BLK], "x-")

    def cells_dot(lo, hi, rows):
        right = q[lo:hi].reshape((hi - lo) * 512, RANK)
        return jnp.dot(xd[rows, lo * 512:hi * 512], right, preferred_element_type=F32)

    def cells(lo, hi, rows):
        def run():
            part = cells_dot(lo, hi, rows)
            p[rows] = part if lo == 0 else p[rows] + part
        return run

    task("load", [], 0.1, loaded)
    for k, (lo, hi) in enumerate(GROUPS):
        task(f"x{k}", [f"x{k - 1}" if k else "load"], 0.4 * (hi - lo), lambda lo=lo, hi=hi: densify(lo, hi))
    for k, (lo, hi) in enumerate(GROUPS):
        came = [f"b{n}{k}{s}" for n in "xf" for s in "+-"] + (
            [f"z{n}{k}{s}" for n in "onf" for s in "+-"] if k else ["ax+", "ax-", "af+", "af-"])
        if k < 4:
            for i in range(4):
                task(f"c{k}.{i}", [f"x{k}"] + came + ([f"c{k - 1}.{i}"] if k else []), 0.3 * (hi - lo),
                     cells(lo, hi, slice(i * 512, (i + 1) * 512)))
        else:
            for i in range(8):
                task(f"c4.{i}", ["x4", f"c3.{i // 2}"] + came, 0.15, cells(lo, hi, slice(i * CHUNK, (i + 1) * CHUNK)))

    def lanes(i):
        return slice(i * CHUNK, (i + 1) * CHUNK)

    def add(rows, other):
        def run():
            p[rows] = p[rows] + other[...]
        return run

    lows = [slice((4 + i) * CHUNK, (4 + i) * CHUNK + HALF) for i in range(4)]
    highs = [slice((4 + i) * CHUNK + HALF, (5 + i) * CHUNK) for i in range(4)]
    for i in range(4):
        send(f"pair{i}", [f"c4.{i}"], p.at[lanes(i)], pcr.at[i], "c")
        task(f"own{i}", [f"c4.{4 + i}", f"pair{i}"], 0.1, add(lanes(4 + i), pcr.at[i]))
    send("yh+", ["own0"], p.at[lows[0]], yr.at[0], "y+")
    send("yh-", ["own0"], p.at[highs[0]], yr.at[1], "y-")
    send("ys+", ["own1"], p.at[highs[1]], yr.at[2], "y+")
    send("ys-", ["own2"], p.at[lows[2]], yr.at[3], "y-")
    send("yf+", ["own1", "yh+"], p.at[lows[1]], yr.at[4], "y+", add(lows[1], yr.at[0]), 0.05)
    send("yf-", ["own2", "yh-"], p.at[highs[2]], yr.at[5], "y-", add(highs[2], yr.at[1]), 0.05)

    def rounded():
        low = p[lows[3]] + yr[3] + yr[4]
        high = p[highs[3]] + yr[2] + yr[5]
        cbt[:, lanes(7)] = jnp.concatenate([low, high], axis=0).T.astype(BF)

    task("cb", ["own3", "ys+", "ys-", "yf+", "yf-"], 0.3, rounded)
    up, down = slice(0, RANK // 2), slice(RANK // 2, RANK)
    send("g+", ["cb"], cbt.at[:, lanes(7)], cbt.at[:, lanes(6)], "y+")
    send("g-", ["cb"], cbt.at[:, lanes(7)], cbt.at[:, lanes(5)], "y-")
    send("k3", ["cb"], cbt.at[:, lanes(7)], cbt.at[:, lanes(3)], "c")
    send("k+", ["g+"], cbt.at[up, lanes(6)], cbt.at[up, lanes(4)], "y+")
    send("k-", ["g-"], cbt.at[down, lanes(5)], cbt.at[down, lanes(4)], "y-")
    send("k2", ["g+"], cbt.at[:, lanes(6)], cbt.at[:, lanes(2)], "c")
    send("k1", ["g-"], cbt.at[:, lanes(5)], cbt.at[:, lanes(1)], "c")
    send("k0", ["k+", "k-"], cbt.at[:, lanes(4)], cbt.at[:, lanes(0)], "c")

    def genes(n, i):
        def run():
            cols = slice((2 * n + i) * 256, (2 * n + i + 1) * 256)
            zt[n, i] = jnp.dot(cbt[...], xd[:, cols], preferred_element_type=F32)
        return run

    for n in range(8):
        for i in range(2):
            task(f"z{n}.{i}", ["cb", "g+", "g-", "k+", "k-", "k0", "k1", "k2", "k3"], 0.6, genes(n, i))

    SPOT = {0: (0, 0), 1: (0, 1), -1: (1, 0), 2: (1, 1)}

    def part(n, rows, dx):
        i, j = SPOT[dx]
        return zt[n, i, rows, j * BLK:(j + 1) * BLK]

    SLOT = {2: 0, 1: 1, -1: 2, 0: 3}
    cut = RA // 2
    a1, a2 = slice(0, cut), slice(cut, RA)
    tops = slice(0, RA)

    def a_z(label, pieces):
        for d in range(4, 0, -1):
            for i, (s, sign) in enumerate(SIGNS):
                if d == 4 and len(pieces) == 1:
                    spots, rows = pieces, (a1, a2)[i]
                else:
                    spots, rows = (pieces if d < 4 else pieces[i:i + 1]), tops
                n = ORDER[sign * d]

                def run(d=d, i=i, n=n, spots=spots, rows=rows):
                    for dx in spots:
                        value = part(n, rows, dx)
                        if d < 3 or d == 3 and len(pieces) == 2 and dx == pieces[i]:
                            value = value + azr[i, d, SLOT[dx], rows].astype(F32)
                        elif d == 3 and len(pieces) == 1:
                            mine = (a1, a2)[i]
                            got = azr[i, 3, SLOT[dx], mine].astype(F32)
                            fill = jnp.zeros_like(got)
                            value = value + jnp.concatenate([got, fill] if i == 0 else [fill, got], axis=0)
                        azs[i, d - 1, SLOT[dx], rows] = value.astype(BF)

                m = slice(SLOT[spots[0]], SLOT[spots[-1]] + 1)
                tiles_of = {f"z{n}.{SPOT[dx][0]}" for dx in spots}
                send(f"{label}{d}{s}", sorted(tiles_of) + ([f"{label}{d + 1}{s}"] if d < 4 else []),
                     azs.at[i, d - 1, m, rows], azr.at[i, d - 1, m, rows], "z" + s, run, 0.08 * len(spots))

    a_z("af", [2])
    a_z("an", [1, -1])
    a_z("ao", [0])

    def a_sum(pieces):
        def run():
            for dx in pieces:
                za[SLOT[dx]] = part(0, tops, dx) + azr[0, 0, SLOT[dx]].astype(F32) + azr[1, 0, SLOT[dx]].astype(F32)
        return run

    task("asf", ["z0.1", "af1+", "af1-"], 0.08, a_sum([2]))
    task("asn", ["z0.0", "z0.1", "an1+", "an1-"], 0.15, a_sum([1, -1]))
    task("aso", ["z0.0", "ao1+", "ao1-"], 0.08, a_sum([0]))

    def a_add(spot, rows, n):
        def run():
            za[spot, rows] = za[spot, rows] + axr[n]
        return run

    send("a0", ["asf"], za.at[0, a1], axr.at[0], "x+")
    send("a1", ["asf"], za.at[0, a2], axr.at[1], "x-")
    send("a2", ["asn"], za.at[1, a2], axr.at[2], "x+")
    send("a3", ["asn"], za.at[2, a1], axr.at[3], "x-")
    send("a4", ["asn", "a0"], za.at[1, a1], axr.at[4], "x+", a_add(1, a1, 0), 0.05)
    send("a5", ["asn", "a1"], za.at[2, a2], axr.at[5], "x-", a_add(2, a2, 1), 0.05)

    b1, b2 = slice(RA, RA + RB1), slice(RA + RB1, RANK)
    v1, v2, v = slice(0, RB1), slice(RB1, RB), slice(0, RB)

    KINDS = ((2, b1, None), (2, b2, None), (1, b2, None), (-1, b1, None), (1, b1, 0), (-1, b2, 1))

    def b_x(kind, k):
        lo, hi = GROUPS[k]
        dx, rows, first = KINDS[kind]

        def run():
            for n in range(lo, hi):
                value = part(n, rows, dx)
                if first is not None:
                    value = value + br[first, n].astype(F32)
                bs[kind, n] = value.astype(BF)

        send(f"b{kind}.{k}", [f"z{n}.{SPOT[dx][0]}" for n in range(lo, hi)] + (
            [] if first is None else [f"b{first}.{k}"]), bs.at[kind, lo:hi], br.at[kind, lo:hi],
            "x-" if kind % 2 else "x+", run, 0.07 * (hi - lo))

    def b_total(k):
        lo, hi = GROUPS[k]

        def run():
            for n in range(lo, hi):
                zb[n, v1] = part(n, b1, 0) + br[3, n].astype(F32) + br[4, n].astype(F32)
                zb[n, v2] = part(n, b2, 0) + br[2, n].astype(F32) + br[5, n].astype(F32)
        task(f"bt{k}", [f"z{n}.0" for n in range(lo, hi)] + [f"b{i}.{k}" for i in range(2, 6)],
             0.12 * (hi - lo), run)

    for k in range(5):
        for kind in range(6):
            b_x(kind, k)
        b_total(k)
    for d in range(4, 0, -1):
        for i, (s, sign) in enumerate(SIGNS):
            n = ORDER[sign * d]
            rows = (v1, v2)[i] if d == 4 else v
            came = (v1, v2)[i] if d == 3 else v

            def run(n=n, i=i, d=d, came=came):
                if d < 4:
                    zb[n, came] = zb[n, came] + bzr[i, d, came]
            send(f"bz{d}{s}", [f"bt{d}"] + ([f"bz{d + 1}{s}"] if d < 4 else []),
                 zb.at[n, rows], bzr.at[i, d - 1, rows], "z" + s, run, 0.05)

    def result():
        top = jnp.concatenate([za[3, a1] + axr[3] + axr[4], za[3, a2] + axr[2] + axr[5]], axis=0)
        bottom = zb[0] + bzr[0, 0] + bzr[1, 0]
        out[...] = jnp.concatenate([top, bottom], axis=0).T

    task("out", ["aso", "a2", "a3", "a4", "a5", "bt0", "bz1+", "bz1-"], 0.3, result)
    plan.run()


def local(block_tiles, block_coords, block_counts, basis_rows):
    vmem = pl.BlockSpec(memory_space=pltpu.VMEM)
    return pl.pallas_call(
        kernel,
        out_shape=jax.ShapeDtypeStruct((BLK, RANK), F32),
        in_specs=[vmem, vmem, pl.BlockSpec(memory_space=pl.ANY), vmem],
        out_specs=vmem,
        scratch_shapes=[
            pltpu.VMEM((SLOTS + 1, BLK, BLK), BF),
            pltpu.VMEM((ROWS, COLS), BF),
            pltpu.VMEM((NZ, NX, BLK, RANK), BF),
            pltpu.VMEM((ROWS, RANK), F32),
            pltpu.VMEM((4, CHUNK, RANK), F32),
            pltpu.VMEM((6, CHUNK // 2, RANK), F32),
            pltpu.VMEM((RANK, ROWS), BF),
            pltpu.VMEM((NZ, 2, RANK, 256), F32),
            pltpu.VMEM((4, RA, BLK), F32),
            pltpu.VMEM((NZ, RB, BLK), F32),
            pltpu.VMEM((2, 4, 4, RA, BLK), BF),
            pltpu.VMEM((2, 4, 4, RA, BLK), BF),
            pltpu.VMEM((6, RA // 2, BLK), F32),
            pltpu.VMEM((6, NZ, RB1, BLK), BF),
            pltpu.VMEM((6, NZ, RB1, BLK), BF),
            pltpu.VMEM((2, 4, RB, BLK), F32),
            pltpu.VMEM((1, 512), jnp.int32),
            pltpu.SMEM((1, 512), jnp.int32),
            pltpu.SemaphoreType.DMA((N_SEM,)),
            pltpu.SemaphoreType.DMA((N_SEM,)),
            pltpu.SemaphoreType.DMA((8,)),
            pltpu.SemaphoreType.DMA,
        ],
        compiler_params=pltpu.CompilerParams(
            collective_id=0, has_side_effects=True, vmem_limit_bytes=60 * 1024 * 1024),
        cost_estimate=pl.CostEstimate(flops=4 * ROWS * COLS * RANK, bytes_accessed=11_000_000,
                                      transcendentals=0),
    )(block_counts, block_coords.T, block_tiles, basis_rows)


def solution(mesh):
    return jax.shard_map(
        local,
        mesh=mesh,
        in_specs=(
            P("cells", "genes", None),
            P("cells", "genes"),
            P("cells", "genes"),
            P(("cells", "genes"), None),
        ),
        out_specs=P(("cells", "genes"), None),
        check_vma=False,
    )
```

```python
import jax
import jax.numpy as jnp
import numpy as np
from jax import lax
from jax.experimental import pallas as pl
from jax.experimental.pallas import tpu as pltpu
from jax.sharding import PartitionSpec as P

MESH = pl.DeviceIdType.MESH
BF = jnp.bfloat16
F32 = jnp.float32

NX, NY, NZ = 4, 4, 8
BLK = 128
RANK = 256
ROWS = 2048
COLS = 4096
CHUNK = 256
HALF = CHUNK // 2
SLOTS = 320
GA = 48
RA = 96
RB = RANK - RA
RB1 = 80

ORDER = {0: 0, 1: 1, -1: 2, 2: 3, -2: 4, 3: 5, -3: 6, 4: 7, -4: 7}
GROUPS = ((0, 1), (1, 3), (3, 5), (5, 7), (7, 8))
SIGNS = (("+", 1), ("-", -1))

HOP = 1.5
LINK = {"x+": 50e3, "x-": 50e3, "z+": 50e3, "z-": 50e3, "y+": 50e3, "y-": 50e3, "c": 500e3}
ISSUE = 0.08
C_A, C_B, C_P = 0.04, 0.035, 0.1
N_SEM = 150
HEAD = 16


def pack(value):
    top = jnp.max(jnp.abs(value), axis=0, keepdims=True)
    power = jnp.floor(jnp.log2(jnp.maximum(top, 1e-30))) + 1.0
    whole = jnp.clip(jnp.round(value * jnp.exp2(15.0 - power)), -32767.0, 32767.0)
    both = jnp.concatenate([whole, jnp.broadcast_to(power, (HEAD, value.shape[1]))], axis=0)
    return both.astype(jnp.int32).astype(jnp.int16)


def unpack(packed):
    value = packed.astype(jnp.int32).astype(F32)
    rows = value.shape[0] - HEAD
    return value[:rows] * jnp.exp2(value[rows:rows + 1] - 15.0)


class Plan:
    def __init__(self, ssem, rsem, where):
        self.ssem, self.rsem, self.where = ssem, rsem, where
        self.tasks = {}
        self.count = 0

    def task(self, name, needs, cost, run, message=None):
        assert name not in self.tasks, name
        self.tasks[name] = (tuple(needs), cost, run, message)

    def send(self, name, needs, src, dst, to, run=None, cost=0.0):
        copy = pltpu.make_async_remote_copy(
            src_ref=src, dst_ref=dst, send_sem=self.ssem.at[self.count],
            recv_sem=self.rsem.at[self.count], device_id=self.where[to], device_id_type=MESH)
        self.count += 1
        time = float(np.prod(src.shape)) * np.dtype(src.dtype).itemsize / LINK[to]
        self.task(name, needs, cost + ISSUE, run, (copy, to, time))

    def order(self):
        after = {name: [] for name in self.tasks}
        for name, (needs, *_) in self.tasks.items():
            for need in needs:
                after[need].append(name)
        rank = {}

        def longest(name):
            if name not in rank:
                _, cost, _, message = self.tasks[name]
                tail = max([longest(n) for n in after[name]], default=0.0)
                rank[name] = cost + (message[2] + HOP if message else 0.0) + tail
            return rank[name]

        for name in self.tasks:
            longest(name)
        now, free, ready_at, order = 0.0, {}, {}, []
        left = dict.fromkeys(self.tasks)
        while left:
            can = {n: max([ready_at[d] for d in self.tasks[n][0]], default=0.0)
                   for n in left if all(d in ready_at for d in self.tasks[n][0])}
            now = max(now, min(can.values()))
            name = max((n for n in can if can[n] <= now), key=lambda n: rank[n])
            del left[name]
            order.append(name)
            _, cost, _, message = self.tasks[name]
            now += cost
            ready_at[name] = now
            if message:
                _, to, time = message
                free[to] = max(now, free.get(to, 0.0)) + time
                ready_at[name] = free[to] + HOP
        self.finish, self.ready_at = now, ready_at
        return order

    def run(self):
        got = set()
        assert self.count <= N_SEM
        order = self.order()
        for name in order:
            needs, _, run, message = self.tasks[name]
            for need in needs:
                if self.tasks[need][3] and need not in got:
                    self.tasks[need][3][0].wait_recv()
                    got.add(need)
            if run:
                run()
            if message:
                message[0].start()
        for name in order:
            if self.tasks[name][3]:
                assert name in got, name
                self.tasks[name][3][0].wait_send()


def kernel(count_ref, coords, tiles_hbm, basis, out, tiles, xd, q, p, pcr, ys, yr, cbt, zt,
           za, zb, azs, azr, axr, axr2, bs, br, bzs, bzr, slot_v, slot_ref, ssem, rsem, tsem, slot_sem):
    c = lax.axis_index("cells")
    g = lax.axis_index("genes")
    z, x = c // NX, c % NX
    y, core = g // 2, g % 2

    def at(dz, dx, dy, dc):
        return (((z + dz + NZ) % NZ) * NX + (x + dx + NX) % NX,
                ((y + dy + NY) % NY) * 2 + (core + dc) % 2)

    where = {
        "x+": at(0, 1, 0, 0), "x-": at(0, -1, 0, 0),
        "z+": at(1, 0, 0, 0), "z-": at(-1, 0, 0, 0),
        "y+": at(0, 0, 1, 0), "y-": at(0, 0, -1, 0),
        "c": at(0, 0, 0, 1),
    }
    plan = Plan(ssem, rsem, where)
    task, send = plan.task, plan.send

    n_loads = 8
    per = SLOTS // n_loads
    loads = [pltpu.make_async_copy(tiles_hbm.at[pl.ds(i * per, per)],
                                   tiles.at[pl.ds(i * per, per)], tsem.at[i]) for i in range(n_loads)]
    for load in loads:
        load.start()

    barrier = pltpu.get_barrier_semaphore()
    for to in where.values():
        pl.semaphore_signal(barrier, inc=1, device_id=to, device_id_type=MESH)
    q[0, 0] = basis[...]
    tiles[SLOTS] = jnp.zeros((BLK, BLK), BF)

    b, k = coords[0:1, :], coords[1:2, :]
    chunk = lax.shift_right_logical(b, 1)
    dy = ((chunk & 3) - y) & 3
    own = lax.shift_right_logical(chunk, 2) == core
    pos = jnp.where(own, jnp.where(dy == 0, 0, jnp.where(dy == 3, 2, jnp.where(dy == 1, 3, 6))),
                    jnp.where(dy == 0, 1, jnp.where(dy == 3, 4, jnp.where(dy == 1, 5, 7))))
    dz = (lax.shift_right_logical(k, 2) - z) & 7
    dz = jnp.where(dz == 0, 0, jnp.where(dz <= 3, 2 * dz - 1, jnp.where(dz == 4, 7, 2 * (NZ - dz))))
    dx = ((k & 3) - x) & 3
    dx = jnp.where(dx >= 2, 5 - dx, dx)
    place = (pos * 2 + (b & 1)) * 32 + dz * NX + dx
    live = lax.broadcasted_iota(jnp.int32, (1, SLOTS), 1) < count_ref[...]
    place = jnp.broadcast_to(jnp.where(live, place, -1), (8, SLOTS)).T[:, 0:1]
    ids = lax.broadcasted_iota(jnp.int32, (SLOTS, 1), 0)
    hit = place == lax.broadcasted_iota(jnp.int32, (SLOTS, 512), 1)
    slot_v[...] = jnp.min(jnp.where(hit, ids, SLOTS), axis=0, keepdims=True)
    to_smem = pltpu.make_async_copy(slot_v, slot_ref, slot_sem)
    to_smem.start()
    pl.semaphore_wait(barrier, len(where))

    def densify(lo, hi):
        def row(r, carry):
            for col in range(lo * 4, hi * 4):
                s = slot_ref[0, r * 32 + col]
                xd[pl.ds(pl.multiple_of(r * BLK, BLK), BLK), col * BLK:(col + 1) * BLK] = tiles[s]
            return carry
        lax.fori_loop(0, ROWS // BLK, row, 0)

    def loaded():
        to_smem.wait()
        for load in loads:
            load.wait()

    a, b = slice(0, GA), slice(GA, BLK)
    send("ax+", [], q.at[0, 0, a], q.at[0, 2, a], "x+")
    send("ax-", [], q.at[0, 0, a], q.at[0, 1, a], "x-")
    send("af+", ["ax+"], q.at[0, 2, 0:32], q.at[0, 3, 0:32], "x+")
    send("af-", ["ax-"], q.at[0, 1, 32:GA], q.at[0, 3, 32:GA], "x-")
    for d in range(1, 5):
        for s, sign in SIGNS:
            src, dst = ORDER[-sign * (d - 1)], ORDER[-sign * d]
            last = [f"{d - 1}{s}"] if d > 1 else []
            rows = slice(0, BLK) if d < 4 else slice(0, 64) if sign > 0 else slice(64, BLK)
            send(f"zo{d}{s}", ["zo" + n for n in last], q.at[src, 0, rows], q.at[dst, 0, rows], "z" + s)
            cols = slice(1, 3) if d < 4 else slice(1, 2) if sign > 0 else slice(2, 3)
            send(f"zn{d}{s}", ["zn" + n for n in last] or ["ax+", "ax-"],
                 q.at[src, cols, a], q.at[dst, cols, a], "z" + s)
            rows = a if d < 4 else slice(0, 32) if sign > 0 else slice(32, GA)
            send(f"zf{d}{s}", ["zf" + n for n in last] or ["af+", "af-"],
                 q.at[src, 3, rows], q.at[dst, 3, rows], "z" + s)
    for k, (lo, hi) in enumerate(GROUPS):
        here = [f"zo{k}+", f"zo{k}-"] if k else []
        e = GA + (48 if k % 2 else 32)
        send(f"bx{k}+", here, q.at[lo:hi, 0, b], q.at[lo:hi, 2, b], "x+")
        send(f"bx{k}-", here, q.at[lo:hi, 0, b], q.at[lo:hi, 1, b], "x-")
        send(f"bf{k}+", [f"bx{k}+"], q.at[lo:hi, 2, GA:e], q.at[lo:hi, 3, GA:e], "x+")
        send(f"bf{k}-", [f"bx{k}-"], q.at[lo:hi, 1, e:BLK], q.at[lo:hi, 3, e:BLK], "x-")

    def cells_dot(lo, hi, rows):
        right = q[lo:hi].reshape((hi - lo) * 512, RANK)
        return jnp.dot(xd[rows, lo * 512:hi * 512], right, preferred_element_type=F32)

    def cells(lo, hi, rows):
        def run():
            part = cells_dot(lo, hi, rows)
            p[rows] = part if lo == 0 else p[rows] + part
        return run

    task("load", [], 0.1, loaded)
    for k, (lo, hi) in enumerate(GROUPS):
        task(f"x{k}", [f"x{k - 1}" if k else "load"], 0.4 * (hi - lo), lambda lo=lo, hi=hi: densify(lo, hi))
    for k, (lo, hi) in enumerate(GROUPS):
        came = [f"b{n}{k}{s}" for n in "xf" for s in "+-"] + (
            [f"z{n}{k}{s}" for n in "onf" for s in "+-"] if k else ["ax+", "ax-", "af+", "af-"])
        if k < 4:
            for i in range(4):
                task(f"c{k}.{i}", [f"x{k}"] + came + ([f"c{k - 1}.{i}"] if k else []), 0.3 * (hi - lo),
                     cells(lo, hi, slice(i * 512, (i + 1) * 512)))
        else:
            for i in range(8):
                task(f"c4.{i}", ["x4", f"c3.{i // 2}"] + came, 0.15, cells(lo, hi, slice(i * CHUNK, (i + 1) * CHUNK)))

    def lanes(i):
        return slice(i * CHUNK, (i + 1) * CHUNK)

    def add(rows, other):
        def run():
            p[rows] = p[rows] + other[...]
        return run

    OWN, OTHER = {0: 0, -1: 2, 1: 3, 2: 6}, {0: 1, -1: 4, 1: 5, 2: 7}
    low = {dy: slice(i * CHUNK, i * CHUNK + HALF) for dy, i in OWN.items()}
    high = {dy: slice(i * CHUNK + HALF, (i + 1) * CHUNK) for dy, i in OWN.items()}
    for dy in (2, 1, -1, 0):
        send(f"pair{dy}", [f"c4.{OTHER[dy]}"], p.at[lanes(OTHER[dy])], pcr.at[dy + 1], "c")
        task(f"own{dy}", [f"c4.{OWN[dy]}", f"pair{dy}"], 0.1, add(lanes(OWN[dy]), pcr.at[dy + 1]))

    def y_send(n, needs, rows, to, first=None):
        def run():
            ys[n] = pack(p[rows] if first is None else p[rows] + unpack(yr[first]))
        send(f"y{n}", needs, ys.at[n], yr.at[n], to, run, 0.15)

    y_send(0, ["own2"], low[2], "y+")
    y_send(1, ["own2"], high[2], "y-")
    y_send(2, ["own1"], high[1], "y+")
    y_send(3, ["own-1"], low[-1], "y-")
    y_send(4, ["own1", "y0"], low[1], "y+", 0)
    y_send(5, ["own-1", "y1"], high[-1], "y-", 1)

    def rounded():
        top = p[low[0]] + unpack(yr[3]) + unpack(yr[4])
        bottom = p[high[0]] + unpack(yr[2]) + unpack(yr[5])
        cbt[:, lanes(0)] = jnp.concatenate([top, bottom], axis=0).T.astype(BF)

    task("cb", ["own0", "y2", "y3", "y4", "y5"], 0.4, rounded)
    up, down = slice(0, RANK // 2), slice(RANK // 2, RANK)
    for half, rows in (("u", up), ("d", down)):
        send(f"g+{half}", ["cb"], cbt.at[rows, lanes(0)], cbt.at[rows, lanes(2)], "y+")
        send(f"g-{half}", ["cb"], cbt.at[rows, lanes(0)], cbt.at[rows, lanes(3)], "y-")
    send("k0", ["cb"], cbt.at[:, lanes(0)], cbt.at[:, lanes(1)], "c")
    send("k+", ["g+u"], cbt.at[up, lanes(2)], cbt.at[up, lanes(6)], "y+")
    send("k-", ["g-d"], cbt.at[down, lanes(3)], cbt.at[down, lanes(6)], "y-")
    send("k1", ["g+u", "g+d"], cbt.at[:, lanes(2)], cbt.at[:, lanes(4)], "c")
    send("k2", ["g-u", "g-d"], cbt.at[:, lanes(3)], cbt.at[:, lanes(5)], "c")
    send("k3", ["k+", "k-"], cbt.at[:, lanes(6)], cbt.at[:, lanes(7)], "c")

    def genes(n, i, lo, hi):
        def run():
            cols = slice((2 * n + i) * 256, (2 * n + i + 1) * 256)
            rows = slice(lo * CHUNK, hi * CHUNK)
            part = jnp.dot(cbt[:, rows], xd[rows, cols], preferred_element_type=F32)
            zt[n, i] = part if lo == 0 else zt[n, i] + part
        return run

    for n in range(8):
        for i in range(2):
            task(f"t{n}.{i}", ["cb", "k0"], 0.17, genes(n, i, 0, 2))
            task(f"u{n}.{i}", [f"t{n}.{i}", "g+u", "g+d", "g-u", "g-d"], 0.2, genes(n, i, 2, 4))
            task(f"v{n}.{i}", [f"u{n}.{i}", "k1", "k2"], 0.2, genes(n, i, 4, 6))
            task(f"z{n}.{i}", [f"v{n}.{i}", "k+", "k-", "k3"], 0.2, genes(n, i, 6, 8))

    SPOT = {0: (0, 0), 1: (0, 1), -1: (1, 0), 2: (1, 1)}

    def part(n, rows, dx):
        i, j = SPOT[dx]
        return zt[n, i, rows, j * BLK:(j + 1) * BLK]

    SLOT = {2: 0, -1: 1, 1: 2, 0: 3}
    cut = RA // 2
    a1, a2 = slice(0, cut), slice(cut, RA)
    tops = slice(0, RA)

    def a_z(label, pieces, far):
        for d in range(4, 0, -1):
            for i, (s, sign) in enumerate(SIGNS):
                spots, rows = far[i] if d == 4 else (pieces, tops)
                n = ORDER[sign * d]

                def run(d=d, i=i, n=n, spots=spots, rows=rows):
                    for dx in spots:
                        value = part(n, rows, dx)
                        if d < 3 or d == 3 and far[i][1] == tops and dx in far[i][0]:
                            value = value + azr[i, d, SLOT[dx], rows].astype(F32)
                        elif d == 3 and far[i][1] != tops:
                            got = azr[i, 3, SLOT[dx], far[i][1]].astype(F32)
                            fill = jnp.zeros_like(got)
                            value = value + jnp.concatenate([got, fill] if i == 0 else [fill, got], axis=0)
                        azs[i, d - 1, SLOT[dx], rows] = value.astype(BF)

                m = slice(SLOT[spots[0]], SLOT[spots[-1]] + 1)
                tiles_of = {f"z{n}.{SPOT[dx][0]}" for dx in spots}
                send(f"{label}{d}{s}", sorted(tiles_of) + ([f"{label}{d + 1}{s}"] if d < 4 else []),
                     azs.at[i, d - 1, m, rows], azr.at[i, d - 1, m, rows], "z" + s, run, C_A * len(spots))

    a_z("af", (2,), (((2,), a1), ((2,), a2)))
    a_z("an", (-1, 1, 0), (((1, 0), tops), ((-1,), tops)))

    def a_sum(pieces):
        def run():
            for dx in pieces:
                za[SLOT[dx]] = part(0, tops, dx) + azr[0, 0, SLOT[dx]].astype(F32) + azr[1, 0, SLOT[dx]].astype(F32)
        return run

    task("asf", ["z0.1", "af1+", "af1-"], C_A, a_sum([2]))
    task("asn", ["z0.0", "z0.1", "an1+", "an1-"], 3 * C_A, a_sum([-1, 1, 0]))

    def a_add(spot, rows, n):
        def run():
            za[spot, rows] = za[spot, rows] + axr[n]
        return run

    send("a0", ["asf"], za.at[0, a1], axr.at[0], "x+")
    send("a1", ["asf"], za.at[0, a2], axr.at[1], "x-")
    send("a2", ["asn", "a0"], za.at[2], axr2.at[0], "x+", a_add(2, a1, 0), 0.05)
    send("a3", ["asn", "a1"], za.at[1], axr2.at[1], "x-", a_add(1, a2, 1), 0.05)

    b1, b2 = slice(RA, RA + RB1), slice(RA + RB1, RANK)
    v1, v2, v = slice(0, RB1), slice(RB1, RB), slice(0, RB)

    KINDS = ((2, b1, None), (2, b2, None), (1, b1, 0), (1, b2, None), (-1, b1, None), (-1, b2, 1))

    def b_x(name, kinds, k, to):
        lo, hi = GROUPS[k]
        needs = set()
        for kind in kinds:
            dx, _, first = KINDS[kind]
            needs |= {f"z{n}.{SPOT[dx][0]}" for n in range(lo, hi)}
            if first is not None:
                needs.add(f"bh{first}.{k}")

        def run():
            for kind in kinds:
                dx, rows, first = KINDS[kind]
                for n in range(lo, hi):
                    value = part(n, rows, dx)
                    if first is not None:
                        value = value + br[first, n].astype(F32)
                    bs[kind, n] = value.astype(BF)

        m = slice(kinds[0], kinds[-1] + 1)
        send(f"{name}.{k}", sorted(needs), bs.at[m, lo:hi], br.at[m, lo:hi], to, run, C_B * len(kinds) * (hi - lo))

    def b_total(k):
        lo, hi = GROUPS[k]

        def run():
            for n in range(lo, hi):
                zb[n, v1] = part(n, b1, 0) + br[2, n].astype(F32) + br[4, n].astype(F32)
                zb[n, v2] = part(n, b2, 0) + br[3, n].astype(F32) + br[5, n].astype(F32)
        task(f"bt{k}", [f"z{n}.0" for n in range(lo, hi)] + [f"bf0.{k}", f"bf1.{k}"], 3 * C_B * (hi - lo), run)

    for k in range(5):
        b_x("bh0", (0,), k, "x+")
        b_x("bh1", (1,), k, "x-")
        b_x("bf0", (2, 3), k, "x+")
        b_x("bf1", (4, 5), k, "x-")
        b_total(k)
    for d in range(4, 0, -1):
        for i, (s, sign) in enumerate(SIGNS):
            for j, rows in enumerate((v1, v2)):
                if d == 4 and i != j:
                    continue
                first = d == 4 or d == 3 and i != j

                def run(n=ORDER[sign * d], i=i, j=j, d=d, rows=rows, first=first):
                    bzs[i, d - 1, j] = pack(zb[n, rows] if first else zb[n, rows] + unpack(bzr[i, d, j]))
                send(f"bz{d}{s}{j}", [f"bt{d}"] + ([] if first else [f"bz{d + 1}{s}{j}"]),
                     bzs.at[i, d - 1, j], bzr.at[i, d - 1, j], "z" + s, run, C_P)

    def result():
        top = za[3] + axr2[0] + axr2[1]
        bottom = [zb[0, rows] + unpack(bzr[0, 0, j]) + unpack(bzr[1, 0, j]) for j, rows in enumerate((v1, v2))]
        out[...] = jnp.concatenate([top] + bottom, axis=0).T

    task("out", ["asn", "a2", "a3", "bt0", "bz1+0", "bz1+1", "bz1-0", "bz1-1"], 0.3, result)
    plan.run()


def local(block_tiles, block_coords, block_counts, basis_rows):
    vmem = pl.BlockSpec(memory_space=pltpu.VMEM)
    return pl.pallas_call(
        kernel,
        out_shape=jax.ShapeDtypeStruct((BLK, RANK), F32),
        in_specs=[vmem, vmem, pl.BlockSpec(memory_space=pl.ANY), vmem],
        out_specs=vmem,
        scratch_shapes=[
            pltpu.VMEM((SLOTS + 1, BLK, BLK), BF),
            pltpu.VMEM((ROWS, COLS), BF),
            pltpu.VMEM((NZ, NX, BLK, RANK), BF),
            pltpu.VMEM((ROWS, RANK), F32),
            pltpu.VMEM((4, CHUNK, RANK), F32),
            pltpu.VMEM((6, HALF + HEAD, RANK), jnp.int16),
            pltpu.VMEM((6, HALF + HEAD, RANK), jnp.int16),
            pltpu.VMEM((RANK, ROWS), BF),
            pltpu.VMEM((NZ, 2, RANK, 256), F32),
            pltpu.VMEM((4, RA, BLK), F32),
            pltpu.VMEM((NZ, RB, BLK), F32),
            pltpu.VMEM((2, 4, 4, RA, BLK), BF),
            pltpu.VMEM((2, 4, 4, RA, BLK), BF),
            pltpu.VMEM((2, RA // 2, BLK), F32),
            pltpu.VMEM((2, RA, BLK), F32),
            pltpu.VMEM((6, NZ, RB1, BLK), BF),
            pltpu.VMEM((6, NZ, RB1, BLK), BF),
            pltpu.VMEM((2, 4, 2, RB1 + HEAD, BLK), jnp.int16),
            pltpu.VMEM((2, 4, 2, RB1 + HEAD, BLK), jnp.int16),
            pltpu.VMEM((1, 512), jnp.int32),
            pltpu.SMEM((1, 512), jnp.int32),
            pltpu.SemaphoreType.DMA((N_SEM,)),
            pltpu.SemaphoreType.DMA((N_SEM,)),
            pltpu.SemaphoreType.DMA((8,)),
            pltpu.SemaphoreType.DMA,
        ],
        compiler_params=pltpu.CompilerParams(
            collective_id=0, has_side_effects=True, vmem_limit_bytes=60 * 1024 * 1024),
        cost_estimate=pl.CostEstimate(flops=4 * ROWS * COLS * RANK, bytes_accessed=11_000_000,
                                      transcendentals=0),
    )(block_counts, block_coords.T, block_tiles, basis_rows)


def solution(mesh):
    return jax.shard_map(
        local,
        mesh=mesh,
        in_specs=(
            P("cells", "genes", None),
            P("cells", "genes"),
            P("cells", "genes"),
            P(("cells", "genes"), None),
        ),
        out_specs=P(("cells", "genes"), None),
        check_vma=False,
    )
```

```python
import jax
import jax.numpy as jnp
import numpy as np
from jax import lax
from jax.experimental import pallas as pl
from jax.experimental.pallas import tpu as pltpu
from jax.sharding import PartitionSpec as P

MESH = pl.DeviceIdType.MESH
BF = jnp.bfloat16
F32 = jnp.float32

NX, NY, NZ = 4, 4, 8
BLK = 128
RANK = 256
ROWS = 2048
COLS = 4096
CHUNK = 256
HALF = CHUNK // 2
SLOTS = 320
GA = 48
RA = 96
RB = RANK - RA
RB1 = 80

ORDER = {0: 0, 1: 1, -1: 2, 2: 3, -2: 4, 3: 5, -3: 6, 4: 7, -4: 7}
GROUPS = ((0, 1), (1, 3), (3, 5), (5, 7), (7, 8))
SIGNS = (("+", 1), ("-", -1))

HOP = 1.6
LINK = {"x+": 50e3, "x-": 50e3, "z+": 50e3, "z-": 50e3, "y+": 50e3, "y-": 50e3, "c": 500e3}
ISSUE = 0.08
LOADED = 5.0
C_A, C_B, C_P = 0.04, 0.035, 0.1
N_SEM = 150
HEAD = 16


def pack(value):
    top = jnp.max(jnp.abs(value), axis=0, keepdims=True)
    power = jnp.floor(jnp.log2(jnp.maximum(top, 1e-30))) + 1.0
    whole = jnp.clip(jnp.round(value * jnp.exp2(15.0 - power)), -32767.0, 32767.0)
    both = jnp.concatenate([whole, jnp.broadcast_to(power, (HEAD, value.shape[1]))], axis=0)
    return both.astype(jnp.int32).astype(jnp.int16)


def unpack(packed):
    value = packed.astype(jnp.int32).astype(F32)
    rows = value.shape[0] - HEAD
    return value[:rows] * jnp.exp2(value[rows:rows + 1] - 15.0)


class Plan:
    def __init__(self, ssem, rsem, where):
        self.ssem, self.rsem, self.where = ssem, rsem, where
        self.tasks = {}
        self.count = 0
        self.after = {}

    def task(self, name, needs, cost, run, message=None, after=0.0):
        assert name not in self.tasks, name
        self.tasks[name] = (tuple(needs), cost, run, message)
        self.after[name] = after

    def send(self, name, needs, src, dst, to, run=None, cost=0.0):
        copy = pltpu.make_async_remote_copy(
            src_ref=src, dst_ref=dst, send_sem=self.ssem.at[self.count],
            recv_sem=self.rsem.at[self.count], device_id=self.where[to], device_id_type=MESH)
        self.count += 1
        time = float(np.prod(src.shape)) * np.dtype(src.dtype).itemsize / LINK[to]
        self.task(name, needs, cost + ISSUE, run, (copy, to, time))

    def order(self):
        after = {name: [] for name in self.tasks}
        for name, (needs, *_) in self.tasks.items():
            for need in needs:
                after[need].append(name)
        rank = {}

        def longest(name):
            if name not in rank:
                _, cost, _, message = self.tasks[name]
                tail = max([longest(n) for n in after[name]], default=0.0)
                rank[name] = cost + (message[2] + HOP if message else 0.0) + tail
            return rank[name]

        for name in self.tasks:
            longest(name)
        now, free, ready_at, order = 0.0, {}, {}, []
        left = dict.fromkeys(self.tasks)
        while left:
            can = {n: max([ready_at[d] for d in self.tasks[n][0]] + [self.after[n]])
                   for n in left if all(d in ready_at for d in self.tasks[n][0])}
            now = max(now, min(can.values()))
            name = max((n for n in can if can[n] <= now), key=lambda n: rank[n])
            del left[name]
            order.append(name)
            _, cost, _, message = self.tasks[name]
            now += cost
            ready_at[name] = now
            if message:
                _, to, time = message
                free[to] = max(now, free.get(to, 0.0)) + time
                ready_at[name] = free[to] + HOP
        self.finish, self.ready_at = now, ready_at
        return order

    def run(self):
        got = set()
        assert self.count <= N_SEM
        order = self.order()
        for name in order:
            needs, _, run, message = self.tasks[name]
            for need in needs:
                if self.tasks[need][3] and need not in got:
                    self.tasks[need][3][0].wait_recv()
                    got.add(need)
            if run:
                run()
            if message:
                message[0].start()
        for name in order:
            if self.tasks[name][3]:
                assert name in got, name
                self.tasks[name][3][0].wait_send()


def kernel(count_ref, coords, tiles_hbm, basis, out, tiles, xd, q, p, pcr, ys, yr, cbt, zt,
           za, zb, azs, azr, axr, axr2, bs, br, bzs, bzr, slot_v, slot_ref, ssem, rsem, tsem, slot_sem):
    c = lax.axis_index("cells")
    g = lax.axis_index("genes")
    z, x = c // NX, c % NX
    y, core = g // 2, g % 2

    def at(dz, dx, dy, dc):
        return (((z + dz + NZ) % NZ) * NX + (x + dx + NX) % NX,
                ((y + dy + NY) % NY) * 2 + (core + dc) % 2)

    where = {
        "x+": at(0, 1, 0, 0), "x-": at(0, -1, 0, 0),
        "z+": at(1, 0, 0, 0), "z-": at(-1, 0, 0, 0),
        "y+": at(0, 0, 1, 0), "y-": at(0, 0, -1, 0),
        "c": at(0, 0, 0, 1),
    }
    plan = Plan(ssem, rsem, where)
    task, send = plan.task, plan.send

    n_loads = 8
    per = SLOTS // n_loads
    loads = [pltpu.make_async_copy(tiles_hbm.at[pl.ds(i * per, per)],
                                   tiles.at[pl.ds(i * per, per)], tsem.at[i]) for i in range(n_loads)]
    for load in loads:
        load.start()

    barrier = pltpu.get_barrier_semaphore()
    for to in where.values():
        pl.semaphore_signal(barrier, inc=1, device_id=to, device_id_type=MESH)
    q[0, 0] = basis[...]
    tiles[SLOTS] = jnp.zeros((BLK, BLK), BF)

    b, k = coords[0:1, :], coords[1:2, :]
    chunk = lax.shift_right_logical(b, 1)
    dy = ((chunk & 3) - y) & 3
    own = lax.shift_right_logical(chunk, 2) == core
    pos = jnp.where(own, jnp.where(dy == 0, 0, jnp.where(dy == 3, 2, jnp.where(dy == 1, 3, 6))),
                    jnp.where(dy == 0, 1, jnp.where(dy == 3, 4, jnp.where(dy == 1, 5, 7))))
    dz = (lax.shift_right_logical(k, 2) - z) & 7
    dz = jnp.where(dz == 0, 0, jnp.where(dz <= 3, 2 * dz - 1, jnp.where(dz == 4, 7, 2 * (NZ - dz))))
    dx = ((k & 3) - x) & 3
    dx = jnp.where(dx >= 2, 5 - dx, dx)
    place = (pos * 2 + (b & 1)) * 32 + dz * NX + dx
    live = lax.broadcasted_iota(jnp.int32, (1, SLOTS), 1) < count_ref[...]
    place = jnp.broadcast_to(jnp.where(live, place, -1), (8, SLOTS)).T[:, 0:1]
    ids = lax.broadcasted_iota(jnp.int32, (SLOTS, 1), 0)
    hit = place == lax.broadcasted_iota(jnp.int32, (SLOTS, 512), 1)
    slot_v[...] = jnp.min(jnp.where(hit, ids, SLOTS), axis=0, keepdims=True)
    to_smem = pltpu.make_async_copy(slot_v, slot_ref, slot_sem)
    to_smem.start()
    pl.semaphore_wait(barrier, len(where))

    def densify(n, i):
        def row(r, carry):
            for col in range(n * 4, n * 4 + 4):
                s = slot_ref[0, r * 32 + col]
                xd[pl.ds(pl.multiple_of(r * BLK, BLK), BLK), col * BLK:(col + 1) * BLK] = tiles[s]
            return carry
        lax.fori_loop(i * 4, i * 4 + 4, row, 0)

    def loaded():
        to_smem.wait()
        for load in loads:
            load.wait()

    a, b = slice(0, GA), slice(GA, BLK)
    send("ax+", [], q.at[0, 0, a], q.at[0, 2, a], "x+")
    send("ax-", [], q.at[0, 0, a], q.at[0, 1, a], "x-")
    send("af+", ["ax+"], q.at[0, 2, 0:32], q.at[0, 3, 0:32], "x+")
    send("af-", ["ax-"], q.at[0, 1, 32:GA], q.at[0, 3, 32:GA], "x-")
    for d in range(1, 5):
        for s, sign in SIGNS:
            src, dst = ORDER[-sign * (d - 1)], ORDER[-sign * d]
            last = [f"{d - 1}{s}"] if d > 1 else []
            rows = slice(0, BLK) if d < 4 else slice(0, 64) if sign > 0 else slice(64, BLK)
            send(f"zo{d}{s}", ["zo" + n for n in last], q.at[src, 0, rows], q.at[dst, 0, rows], "z" + s)
            cols = slice(1, 3) if d < 4 else slice(1, 2) if sign > 0 else slice(2, 3)
            send(f"zn{d}{s}", ["zn" + n for n in last] or ["ax+", "ax-"],
                 q.at[src, cols, a], q.at[dst, cols, a], "z" + s)
            rows = a if d < 4 else slice(0, 32) if sign > 0 else slice(32, GA)
            send(f"zf{d}{s}", ["zf" + n for n in last] or ["af+", "af-"],
                 q.at[src, 3, rows], q.at[dst, 3, rows], "z" + s)
    for k, (lo, hi) in enumerate(GROUPS):
        here = [f"zo{k}+", f"zo{k}-"] if k else []
        e = GA + (48 if k % 2 else 32)
        send(f"bx{k}+", here, q.at[lo:hi, 0, b], q.at[lo:hi, 2, b], "x+")
        send(f"bx{k}-", here, q.at[lo:hi, 0, b], q.at[lo:hi, 1, b], "x-")
        send(f"bf{k}+", [f"bx{k}+"], q.at[lo:hi, 2, GA:e], q.at[lo:hi, 3, GA:e], "x+")
        send(f"bf{k}-", [f"bx{k}-"], q.at[lo:hi, 1, e:BLK], q.at[lo:hi, 3, e:BLK], "x-")

    def cells_dot(lo, hi, rows):
        right = q[lo:hi].reshape((hi - lo) * 512, RANK)
        return jnp.dot(xd[rows, lo * 512:hi * 512], right, preferred_element_type=F32)

    def cells(lo, hi, rows):
        def run():
            part = cells_dot(lo, hi, rows)
            p[rows] = part if lo == 0 else p[rows] + part
        return run

    task("load", [], 0.2, loaded, after=LOADED)
    for n in range(NZ):
        for i in range(4):
            task(f"x{n}.{i}", ["load"], 0.15, lambda n=n, i=i: densify(n, i))
    for k, (lo, hi) in enumerate(GROUPS):
        came = [f"b{n}{k}{s}" for n in "xf" for s in "+-"] + (
            [f"z{n}{k}{s}" for n in "onf" for s in "+-"] if k else ["ax+", "ax-", "af+", "af-"])
        if k < 4:
            for i in range(4):
                task(f"c{k}.{i}", [f"x{n}.{i}" for n in range(lo, hi)] + came + ([f"c{k - 1}.{i}"] if k else []), 0.35 * (hi - lo),
                     cells(lo, hi, slice(i * 512, (i + 1) * 512)))
        else:
            for i in range(8):
                task(f"c4.{i}", [f"x7.{i // 2}", f"c3.{i // 2}"] + came, 0.18, cells(lo, hi, slice(i * CHUNK, (i + 1) * CHUNK)))

    def lanes(i):
        return slice(i * CHUNK, (i + 1) * CHUNK)

    def add(rows, other):
        def run():
            p[rows] = p[rows] + other[...]
        return run

    OWN, OTHER = {0: 0, -1: 2, 1: 3, 2: 6}, {0: 1, -1: 4, 1: 5, 2: 7}
    low = {dy: slice(i * CHUNK, i * CHUNK + HALF) for dy, i in OWN.items()}
    high = {dy: slice(i * CHUNK + HALF, (i + 1) * CHUNK) for dy, i in OWN.items()}
    for dy in (2, 1, -1, 0):
        send(f"pair{dy}", [f"c4.{OTHER[dy]}"], p.at[lanes(OTHER[dy])], pcr.at[dy + 1], "c")
        task(f"own{dy}", [f"c4.{OWN[dy]}", f"pair{dy}"], 0.1, add(lanes(OWN[dy]), pcr.at[dy + 1]))

    def y_send(n, needs, rows, to, first=None):
        def run():
            ys[n] = pack(p[rows] if first is None else p[rows] + unpack(yr[first]))
        send(f"y{n}", needs, ys.at[n], yr.at[n], to, run, 0.15)

    y_send(0, ["own2"], low[2], "y+")
    y_send(1, ["own2"], high[2], "y-")
    y_send(2, ["own1"], high[1], "y+")
    y_send(3, ["own-1"], low[-1], "y-")
    y_send(4, ["own1", "y0"], low[1], "y+", 0)
    y_send(5, ["own-1", "y1"], high[-1], "y-", 1)

    def rounded():
        top = p[low[0]] + unpack(yr[3]) + unpack(yr[4])
        bottom = p[high[0]] + unpack(yr[2]) + unpack(yr[5])
        cbt[:, lanes(0)] = jnp.concatenate([top, bottom], axis=0).T.astype(BF)

    task("cb", ["own0", "y2", "y3", "y4", "y5"], 0.4, rounded)
    up, down = slice(0, RANK // 2), slice(RANK // 2, RANK)
    for half, rows in (("u", up), ("d", down)):
        send(f"g+{half}", ["cb"], cbt.at[rows, lanes(0)], cbt.at[rows, lanes(2)], "y+")
        send(f"g-{half}", ["cb"], cbt.at[rows, lanes(0)], cbt.at[rows, lanes(3)], "y-")
    send("k0", ["cb"], cbt.at[:, lanes(0)], cbt.at[:, lanes(1)], "c")
    send("k+", ["g+u"], cbt.at[up, lanes(2)], cbt.at[up, lanes(6)], "y+")
    send("k-", ["g-d"], cbt.at[down, lanes(3)], cbt.at[down, lanes(6)], "y-")
    send("k1", ["g+u", "g+d"], cbt.at[:, lanes(2)], cbt.at[:, lanes(4)], "c")
    send("k2", ["g-u", "g-d"], cbt.at[:, lanes(3)], cbt.at[:, lanes(5)], "c")
    send("k3", ["k+", "k-"], cbt.at[:, lanes(6)], cbt.at[:, lanes(7)], "c")

    def genes(n, i, lo, hi):
        def run():
            cols = slice((2 * n + i) * 256, (2 * n + i + 1) * 256)
            rows = slice(lo * CHUNK, hi * CHUNK)
            part = jnp.dot(cbt[:, rows], xd[rows, cols], preferred_element_type=F32)
            zt[n, i] = part if lo == 0 else zt[n, i] + part
        return run

    for n in range(8):
        for i in range(2):
            task(f"t{n}.{i}", ["cb", "k0"], 0.17, genes(n, i, 0, 2))
            task(f"u{n}.{i}", [f"t{n}.{i}", "g+u", "g+d", "g-u", "g-d"], 0.2, genes(n, i, 2, 4))
            task(f"v{n}.{i}", [f"u{n}.{i}", "k1", "k2"], 0.2, genes(n, i, 4, 6))
            task(f"z{n}.{i}", [f"v{n}.{i}", "k+", "k-", "k3"], 0.2, genes(n, i, 6, 8))

    SPOT = {0: (0, 0), 1: (0, 1), -1: (1, 0), 2: (1, 1)}

    def part(n, rows, dx):
        i, j = SPOT[dx]
        return zt[n, i, rows, j * BLK:(j + 1) * BLK]

    SLOT = {2: 0, -1: 1, 1: 2, 0: 3}
    cut = RA // 2
    a1, a2 = slice(0, cut), slice(cut, RA)
    tops = slice(0, RA)

    def a_z(label, pieces, far):
        for d in range(4, 0, -1):
            for i, (s, sign) in enumerate(SIGNS):
                spots, rows = far[i] if d == 4 else (pieces, tops)
                n = ORDER[sign * d]

                def run(d=d, i=i, n=n, spots=spots, rows=rows):
                    for dx in spots:
                        value = part(n, rows, dx)
                        if d < 3 or d == 3 and far[i][1] == tops and dx in far[i][0]:
                            value = value + azr[i, d, SLOT[dx], rows].astype(F32)
                        elif d == 3 and far[i][1] != tops:
                            got = azr[i, 3, SLOT[dx], far[i][1]].astype(F32)
                            fill = jnp.zeros_like(got)
                            value = value + jnp.concatenate([got, fill] if i == 0 else [fill, got], axis=0)
                        azs[i, d - 1, SLOT[dx], rows] = value.astype(BF)

                m = slice(SLOT[spots[0]], SLOT[spots[-1]] + 1)
                tiles_of = {f"z{n}.{SPOT[dx][0]}" for dx in spots}
                send(f"{label}{d}{s}", sorted(tiles_of) + ([f"{label}{d + 1}{s}"] if d < 4 else []),
                     azs.at[i, d - 1, m, rows], azr.at[i, d - 1, m, rows], "z" + s, run, C_A * len(spots))

    a_z("af", (2,), (((2,), a1), ((2,), a2)))
    a_z("an", (-1, 1, 0), (((1, 0), tops), ((-1,), tops)))

    def a_sum(pieces):
        def run():
            for dx in pieces:
                za[SLOT[dx]] = part(0, tops, dx) + azr[0, 0, SLOT[dx]].astype(F32) + azr[1, 0, SLOT[dx]].astype(F32)
        return run

    task("asf", ["z0.1", "af1+", "af1-"], C_A, a_sum([2]))
    task("asn", ["z0.0", "z0.1", "an1+", "an1-"], 3 * C_A, a_sum([-1, 1, 0]))

    def a_add(spot, rows, n):
        def run():
            za[spot, rows] = za[spot, rows] + axr[n]
        return run

    send("a0", ["asf"], za.at[0, a1], axr.at[0], "x+")
    send("a1", ["asf"], za.at[0, a2], axr.at[1], "x-")
    send("a2", ["asn", "a0"], za.at[2], axr2.at[0], "x+", a_add(2, a1, 0), 0.05)
    send("a3", ["asn", "a1"], za.at[1], axr2.at[1], "x-", a_add(1, a2, 1), 0.05)

    b1, b2 = slice(RA, RA + RB1), slice(RA + RB1, RANK)
    v1, v2, v = slice(0, RB1), slice(RB1, RB), slice(0, RB)

    KINDS = ((2, b1, None), (2, b2, None), (1, b1, 0), (1, b2, None), (-1, b1, None), (-1, b2, 1))

    def b_x(name, kinds, k, to):
        lo, hi = GROUPS[k]
        needs = set()
        for kind in kinds:
            dx, _, first = KINDS[kind]
            needs |= {f"z{n}.{SPOT[dx][0]}" for n in range(lo, hi)}
            if first is not None:
                needs.add(f"bh{first}.{k}")

        def run():
            for kind in kinds:
                dx, rows, first = KINDS[kind]
                for n in range(lo, hi):
                    value = part(n, rows, dx)
                    if first is not None:
                        value = value + br[first, n].astype(F32)
                    bs[kind, n] = value.astype(BF)

        m = slice(kinds[0], kinds[-1] + 1)
        send(f"{name}.{k}", sorted(needs), bs.at[m, lo:hi], br.at[m, lo:hi], to, run, C_B * len(kinds) * (hi - lo))

    def b_total(k):
        lo, hi = GROUPS[k]

        def run():
            for n in range(lo, hi):
                zb[n, v1] = part(n, b1, 0) + br[2, n].astype(F32) + br[4, n].astype(F32)
                zb[n, v2] = part(n, b2, 0) + br[3, n].astype(F32) + br[5, n].astype(F32)
        task(f"bt{k}", [f"z{n}.0" for n in range(lo, hi)] + [f"bf0.{k}", f"bf1.{k}"], 3 * C_B * (hi - lo), run)

    for k in range(5):
        b_x("bh0", (0,), k, "x+")
        b_x("bh1", (1,), k, "x-")
        b_x("bf0", (2, 3), k, "x+")
        b_x("bf1", (4, 5), k, "x-")
        b_total(k)
    for d in range(4, 0, -1):
        for i, (s, sign) in enumerate(SIGNS):
            for j, rows in enumerate((v1, v2)):
                if d == 4 and i != j:
                    continue
                first = d == 4 or d == 3 and i != j

                def run(n=ORDER[sign * d], i=i, j=j, d=d, rows=rows, first=first):
                    bzs[i, d - 1, j] = pack(zb[n, rows] if first else zb[n, rows] + unpack(bzr[i, d, j]))
                send(f"bz{d}{s}{j}", [f"bt{d}"] + ([] if first else [f"bz{d + 1}{s}{j}"]),
                     bzs.at[i, d - 1, j], bzr.at[i, d - 1, j], "z" + s, run, C_P)

    def result():
        top = za[3] + axr2[0] + axr2[1]
        bottom = [zb[0, rows] + unpack(bzr[0, 0, j]) + unpack(bzr[1, 0, j]) for j, rows in enumerate((v1, v2))]
        out[...] = jnp.concatenate([top] + bottom, axis=0).T

    task("out", ["asn", "a2", "a3", "bt0", "bz1+0", "bz1+1", "bz1-0", "bz1-1"], 0.3, result)
    plan.run()


def local(block_tiles, block_coords, block_counts, basis_rows):
    vmem = pl.BlockSpec(memory_space=pltpu.VMEM)
    return pl.pallas_call(
        kernel,
        out_shape=jax.ShapeDtypeStruct((BLK, RANK), F32),
        in_specs=[vmem, vmem, pl.BlockSpec(memory_space=pl.ANY), vmem],
        out_specs=vmem,
        scratch_shapes=[
            pltpu.VMEM((SLOTS + 1, BLK, BLK), BF),
            pltpu.VMEM((ROWS, COLS), BF),
            pltpu.VMEM((NZ, NX, BLK, RANK), BF),
            pltpu.VMEM((ROWS, RANK), F32),
            pltpu.VMEM((4, CHUNK, RANK), F32),
            pltpu.VMEM((6, HALF + HEAD, RANK), jnp.int16),
            pltpu.VMEM((6, HALF + HEAD, RANK), jnp.int16),
            pltpu.VMEM((RANK, ROWS), BF),
            pltpu.VMEM((NZ, 2, RANK, 256), F32),
            pltpu.VMEM((4, RA, BLK), F32),
            pltpu.VMEM((NZ, RB, BLK), F32),
            pltpu.VMEM((2, 4, 4, RA, BLK), BF),
            pltpu.VMEM((2, 4, 4, RA, BLK), BF),
            pltpu.VMEM((2, RA // 2, BLK), F32),
            pltpu.VMEM((2, RA, BLK), F32),
            pltpu.VMEM((6, NZ, RB1, BLK), BF),
            pltpu.VMEM((6, NZ, RB1, BLK), BF),
            pltpu.VMEM((2, 4, 2, RB1 + HEAD, BLK), jnp.int16),
            pltpu.VMEM((2, 4, 2, RB1 + HEAD, BLK), jnp.int16),
            pltpu.VMEM((1, 512), jnp.int32),
            pltpu.SMEM((1, 512), jnp.int32),
            pltpu.SemaphoreType.DMA((N_SEM,)),
            pltpu.SemaphoreType.DMA((N_SEM,)),
            pltpu.SemaphoreType.DMA((8,)),
            pltpu.SemaphoreType.DMA,
        ],
        compiler_params=pltpu.CompilerParams(
            collective_id=0, has_side_effects=True, vmem_limit_bytes=60 * 1024 * 1024),
        cost_estimate=pl.CostEstimate(flops=4 * ROWS * COLS * RANK, bytes_accessed=11_000_000,
                                      transcendentals=0),
    )(block_counts, block_coords.T, block_tiles, basis_rows)


def solution(mesh):
    return jax.shard_map(
        local,
        mesh=mesh,
        in_specs=(
            P("cells", "genes", None),
            P("cells", "genes"),
            P("cells", "genes"),
            P(("cells", "genes"), None),
        ),
        out_specs=P(("cells", "genes"), None),
        check_vma=False,
    )
```

```python
import jax
import jax.numpy as jnp
import numpy as np
from jax import lax
from jax.experimental import pallas as pl
from jax.experimental.pallas import tpu as pltpu
from jax.sharding import PartitionSpec as P

MESH = pl.DeviceIdType.MESH
BF = jnp.bfloat16
F32 = jnp.float32

NX, NY, NZ = 4, 4, 8
BLK = 128
RANK = 256
ROWS = 2048
COLS = 4096
CHUNK = 256
HALF = CHUNK // 2
SLOTS = 320
GA = 48
RA = 96
RB = RANK - RA
RB1 = 80

ORDER = {0: 0, 1: 1, -1: 2, 2: 3, -2: 4, 3: 5, -3: 6, 4: 7, -4: 7}
GROUPS = ((0, 1), (1, 3), (3, 5), (5, 7), (7, 8))
SIGNS = (("+", 1), ("-", -1))

HOP = 1.6
LINK = {"x+": 50e3, "x-": 50e3, "z+": 50e3, "z-": 50e3, "y+": 50e3, "y-": 50e3, "c": 500e3}
ISSUE = 0.08
LOADED = 5.0
C_A, C_B, C_P = 0.04, 0.035, 0.1
N_SEM = 150
HEAD = 16


def pack(value):
    top = jnp.max(jnp.abs(value), axis=0, keepdims=True)
    power = jnp.floor(jnp.log2(jnp.maximum(top, 1e-30))) + 1.0
    whole = jnp.clip(jnp.round(value * jnp.exp2(15.0 - power)), -32767.0, 32767.0)
    both = jnp.concatenate([whole, jnp.broadcast_to(power, (HEAD, value.shape[1]))], axis=0)
    return both.astype(jnp.int32).astype(jnp.int16)


def unpack(packed):
    value = packed.astype(jnp.int32).astype(F32)
    rows = value.shape[0] - HEAD
    return value[:rows] * jnp.exp2(value[rows:rows + 1] - 15.0)


class Plan:
    def __init__(self, ssem, rsem, where):
        self.ssem, self.rsem, self.where = ssem, rsem, where
        self.tasks = {}
        self.count = 0
        self.after = {}

    def task(self, name, needs, cost, run, message=None, after=0.0):
        assert name not in self.tasks, name
        self.tasks[name] = (tuple(needs), cost, run, message)
        self.after[name] = after

    def send(self, name, needs, src, dst, to, run=None, cost=0.0):
        copy = pltpu.make_async_remote_copy(
            src_ref=src, dst_ref=dst, send_sem=self.ssem.at[self.count],
            recv_sem=self.rsem.at[self.count], device_id=self.where[to], device_id_type=MESH)
        self.count += 1
        time = float(np.prod(src.shape)) * np.dtype(src.dtype).itemsize / LINK[to]
        self.task(name, needs, cost + ISSUE, run, (copy, to, time))

    def order(self):
        after = {name: [] for name in self.tasks}
        for name, (needs, *_) in self.tasks.items():
            for need in needs:
                after[need].append(name)
        rank = {}

        def longest(name):
            if name not in rank:
                _, cost, _, message = self.tasks[name]
                tail = max([longest(n) for n in after[name]], default=0.0)
                rank[name] = cost + (message[2] + HOP if message else 0.0) + tail
            return rank[name]

        for name in self.tasks:
            longest(name)
        now, free, ready_at, order = 0.0, {}, {}, []
        left = dict.fromkeys(self.tasks)
        while left:
            can = {n: max([ready_at[d] for d in self.tasks[n][0]] + [self.after[n]])
                   for n in left if all(d in ready_at for d in self.tasks[n][0])}
            now = max(now, min(can.values()))
            name = max((n for n in can if can[n] <= now), key=lambda n: rank[n])
            del left[name]
            order.append(name)
            _, cost, _, message = self.tasks[name]
            now += cost
            ready_at[name] = now
            if message:
                _, to, time = message
                free[to] = max(now, free.get(to, 0.0)) + time
                ready_at[name] = free[to] + HOP
        self.finish, self.ready_at = now, ready_at
        return order

    def run(self):
        got = set()
        assert self.count <= N_SEM
        order = self.order()
        for name in order:
            needs, _, run, message = self.tasks[name]
            for need in needs:
                if self.tasks[need][3] and need not in got:
                    self.tasks[need][3][0].wait_recv()
                    got.add(need)
            if run:
                run()
            if message:
                message[0].start()
        for name in order:
            if self.tasks[name][3]:
                assert name in got, name
                self.tasks[name][3][0].wait_send()


def kernel(count_ref, coords, tiles_hbm, basis, out, tiles, q, p, pcr, ys, yr, cbt, zt,
           za, zb, azs, azr, axr, axr2, bs, br, bzs, bzr, slot_v, slot_ref, ssem, rsem, tsem, slot_sem, basis_sem):
    c = lax.axis_index("cells")
    g = lax.axis_index("genes")
    z, x = c // NX, c % NX
    y, core = g // 2, g % 2

    def at(dz, dx, dy, dc):
        return (((z + dz + NZ) % NZ) * NX + (x + dx + NX) % NX,
                ((y + dy + NY) % NY) * 2 + (core + dc) % 2)

    where = {
        "x+": at(0, 1, 0, 0), "x-": at(0, -1, 0, 0),
        "z+": at(1, 0, 0, 0), "z-": at(-1, 0, 0, 0),
        "y+": at(0, 0, 1, 0), "y-": at(0, 0, -1, 0),
        "c": at(0, 0, 0, 1),
    }
    plan = Plan(ssem, rsem, where)
    task, send = plan.task, plan.send

    n_loads = 8
    per = SLOTS // n_loads
    loads = [pltpu.make_async_copy(tiles_hbm.at[pl.ds(i * per, per)],
                                   tiles.at[pl.ds(i * per, per)], tsem.at[i]) for i in range(n_loads)]
    own_basis = pltpu.make_async_copy(basis, q.at[0, 0], basis_sem)
    own_basis.start()
    for load in loads:
        load.start()
    barrier = pltpu.get_barrier_semaphore()
    for to in where.values():
        pl.semaphore_signal(barrier, inc=1, device_id=to, device_id_type=MESH)
    tiles[SLOTS] = jnp.zeros((BLK, BLK), BF)

    own_basis.wait()
    pl.semaphore_wait(barrier, len(where))

    to_smem = pltpu.make_async_copy(slot_v, slot_ref, slot_sem)

    def table():
        b, k = coords[0:1, :], coords[1:2, :]
        chunk = lax.shift_right_logical(b, 1)
        dy = ((chunk & 3) - y) & 3
        own = lax.shift_right_logical(chunk, 2) == core
        pos = jnp.where(own, jnp.where(dy == 0, 0, jnp.where(dy == 3, 2, jnp.where(dy == 1, 3, 6))),
                        jnp.where(dy == 0, 1, jnp.where(dy == 3, 4, jnp.where(dy == 1, 5, 7))))
        dz = (lax.shift_right_logical(k, 2) - z) & 7
        dz = jnp.where(dz == 0, 0, jnp.where(dz <= 3, 2 * dz - 1, jnp.where(dz == 4, 7, 2 * (NZ - dz))))
        dx = ((k & 3) - x) & 3
        dx = jnp.where(dx >= 2, 5 - dx, dx)
        place = (pos * 2 + (b & 1)) * 32 + dz * NX + dx
        live = lax.broadcasted_iota(jnp.int32, (1, SLOTS), 1) < count_ref[...]
        place = jnp.broadcast_to(jnp.where(live, place, -1), (8, SLOTS)).T[:, 0:1]
        ids = lax.broadcasted_iota(jnp.int32, (SLOTS, 1), 0)
        hit = place == lax.broadcasted_iota(jnp.int32, (SLOTS, 512), 1)
        slot_v[...] = jnp.min(jnp.where(hit, ids, SLOTS), axis=0, keepdims=True)
        to_smem.start()

    def block(rows, cols):
        return jnp.concatenate([jnp.concatenate([tiles[slot_ref[0, r * 32 + c]] for c in range(*cols)], axis=1)
                                for r in range(*rows)], axis=0)

    def loaded():
        to_smem.wait()
        for load in loads:
            load.wait()

    a, b = slice(0, GA), slice(GA, BLK)
    send("ax+", [], q.at[0, 0, a], q.at[0, 2, a], "x+")
    send("ax-", [], q.at[0, 0, a], q.at[0, 1, a], "x-")
    send("af+", ["ax+"], q.at[0, 2, 0:32], q.at[0, 3, 0:32], "x+")
    send("af-", ["ax-"], q.at[0, 1, 32:GA], q.at[0, 3, 32:GA], "x-")
    for d in range(1, 5):
        for s, sign in SIGNS:
            src, dst = ORDER[-sign * (d - 1)], ORDER[-sign * d]
            last = [f"{d - 1}{s}"] if d > 1 else []
            rows = slice(0, BLK) if d < 4 else slice(0, 64) if sign > 0 else slice(64, BLK)
            send(f"zo{d}{s}", ["zo" + n for n in last], q.at[src, 0, rows], q.at[dst, 0, rows], "z" + s)
            cols = slice(1, 3) if d < 4 else slice(1, 2) if sign > 0 else slice(2, 3)
            send(f"zn{d}{s}", ["zn" + n for n in last] or ["ax+", "ax-"],
                 q.at[src, cols, a], q.at[dst, cols, a], "z" + s)
            rows = a if d < 4 else slice(0, 32) if sign > 0 else slice(32, GA)
            send(f"zf{d}{s}", ["zf" + n for n in last] or ["af+", "af-"],
                 q.at[src, 3, rows], q.at[dst, 3, rows], "z" + s)
    for k, (lo, hi) in enumerate(GROUPS):
        here = [f"zo{k}+", f"zo{k}-"] if k else []
        e = GA + (48 if k % 2 else 32)
        send(f"bx{k}+", here, q.at[lo:hi, 0, b], q.at[lo:hi, 2, b], "x+")
        send(f"bx{k}-", here, q.at[lo:hi, 0, b], q.at[lo:hi, 1, b], "x-")
        send(f"bf{k}+", [f"bx{k}+"], q.at[lo:hi, 2, GA:e], q.at[lo:hi, 3, GA:e], "x+")
        send(f"bf{k}-", [f"bx{k}-"], q.at[lo:hi, 1, e:BLK], q.at[lo:hi, 3, e:BLK], "x-")

    def cells_dot(lo, hi, rows):
        right = q[lo:hi].reshape((hi - lo) * 512, RANK)
        left = block((rows.start // BLK, rows.stop // BLK), (lo * 4, hi * 4))
        return jnp.dot(left, right, preferred_element_type=F32)

    def cells(lo, hi, rows):
        def run():
            part = cells_dot(lo, hi, rows)
            p[rows] = part if lo == 0 else p[rows] + part
        return run

    task("table", [], 0.8, table)
    task("load", ["table"], 0.2, loaded, after=LOADED)
    for k, (lo, hi) in enumerate(GROUPS):
        came = [f"b{n}{k}{s}" for n in "xf" for s in "+-"] + (
            [f"z{n}{k}{s}" for n in "onf" for s in "+-"] if k else ["ax+", "ax-", "af+", "af-"])
        if k < 4:
            for i in range(4):
                task(f"c{k}.{i}", ["load"] + came + ([f"c{k - 1}.{i}"] if k else []), 0.35 * (hi - lo),
                     cells(lo, hi, slice(i * 512, (i + 1) * 512)))
        else:
            for i in range(8):
                task(f"c4.{i}", ["load", f"c3.{i // 2}"] + came, 0.18, cells(lo, hi, slice(i * CHUNK, (i + 1) * CHUNK)))

    def lanes(i):
        return slice(i * CHUNK, (i + 1) * CHUNK)

    def add(rows, other):
        def run():
            p[rows] = p[rows] + other[...]
        return run

    OWN, OTHER = {0: 0, -1: 2, 1: 3, 2: 6}, {0: 1, -1: 4, 1: 5, 2: 7}
    low = {dy: slice(i * CHUNK, i * CHUNK + HALF) for dy, i in OWN.items()}
    high = {dy: slice(i * CHUNK + HALF, (i + 1) * CHUNK) for dy, i in OWN.items()}
    for dy in (2, 1, -1, 0):
        send(f"pair{dy}", [f"c4.{OTHER[dy]}"], p.at[lanes(OTHER[dy])], pcr.at[dy + 1], "c")
        task(f"own{dy}", [f"c4.{OWN[dy]}", f"pair{dy}"], 0.1, add(lanes(OWN[dy]), pcr.at[dy + 1]))

    def y_send(n, needs, rows, to, first=None):
        def run():
            ys[n] = pack(p[rows] if first is None else p[rows] + unpack(yr[first]))
        send(f"y{n}", needs, ys.at[n], yr.at[n], to, run, 0.15)

    y_send(0, ["own2"], low[2], "y+")
    y_send(1, ["own2"], high[2], "y-")
    y_send(2, ["own1"], high[1], "y+")
    y_send(3, ["own-1"], low[-1], "y-")
    y_send(4, ["own1", "y0"], low[1], "y+", 0)
    y_send(5, ["own-1", "y1"], high[-1], "y-", 1)

    def rounded():
        top = p[low[0]] + unpack(yr[3]) + unpack(yr[4])
        bottom = p[high[0]] + unpack(yr[2]) + unpack(yr[5])
        cbt[:, lanes(0)] = jnp.concatenate([top, bottom], axis=0).T.astype(BF)

    task("cb", ["own0", "y2", "y3", "y4", "y5"], 0.4, rounded)
    up, down = slice(0, RANK // 2), slice(RANK // 2, RANK)
    for half, rows in (("u", up), ("d", down)):
        send(f"g+{half}", ["cb"], cbt.at[rows, lanes(0)], cbt.at[rows, lanes(2)], "y+")
        send(f"g-{half}", ["cb"], cbt.at[rows, lanes(0)], cbt.at[rows, lanes(3)], "y-")
    send("k0", ["cb"], cbt.at[:, lanes(0)], cbt.at[:, lanes(1)], "c")
    send("k+", ["g+u"], cbt.at[up, lanes(2)], cbt.at[up, lanes(6)], "y+")
    send("k-", ["g-d"], cbt.at[down, lanes(3)], cbt.at[down, lanes(6)], "y-")
    send("k1", ["g+u", "g+d"], cbt.at[:, lanes(2)], cbt.at[:, lanes(4)], "c")
    send("k2", ["g-u", "g-d"], cbt.at[:, lanes(3)], cbt.at[:, lanes(5)], "c")
    send("k3", ["k+", "k-"], cbt.at[:, lanes(6)], cbt.at[:, lanes(7)], "c")

    def genes(n, i, lo, hi):
        def run():
            col = (2 * n + i) * 2
            right = block((lo * 2, hi * 2), (col, col + 2))
            part = jnp.dot(cbt[:, lo * CHUNK:hi * CHUNK], right, preferred_element_type=F32)
            zt[n, i] = part if lo == 0 else zt[n, i] + part
        return run

    for n in range(8):
        for i in range(2):
            task(f"t{n}.{i}", ["cb", "k0"], 0.17, genes(n, i, 0, 2))
            task(f"u{n}.{i}", [f"t{n}.{i}", "g+u", "g+d", "g-u", "g-d"], 0.2, genes(n, i, 2, 4))
            task(f"v{n}.{i}", [f"u{n}.{i}", "k1", "k2"], 0.2, genes(n, i, 4, 6))
            task(f"z{n}.{i}", [f"v{n}.{i}", "k+", "k-", "k3"], 0.2, genes(n, i, 6, 8))

    SPOT = {0: (0, 0), 1: (0, 1), -1: (1, 0), 2: (1, 1)}

    def part(n, rows, dx):
        i, j = SPOT[dx]
        return zt[n, i, rows, j * BLK:(j + 1) * BLK]

    SLOT = {2: 0, -1: 1, 1: 2, 0: 3}
    cut = RA // 2
    a1, a2 = slice(0, cut), slice(cut, RA)
    tops = slice(0, RA)

    def a_z(label, pieces, far):
        for d in range(4, 0, -1):
            for i, (s, sign) in enumerate(SIGNS):
                spots, rows = far[i] if d == 4 else (pieces, tops)
                n = ORDER[sign * d]

                def run(d=d, i=i, n=n, spots=spots, rows=rows):
                    for dx in spots:
                        value = part(n, rows, dx)
                        if d < 3 or d == 3 and far[i][1] == tops and dx in far[i][0]:
                            value = value + azr[i, d, SLOT[dx], rows].astype(F32)
                        elif d == 3 and far[i][1] != tops:
                            got = azr[i, 3, SLOT[dx], far[i][1]].astype(F32)
                            fill = jnp.zeros_like(got)
                            value = value + jnp.concatenate([got, fill] if i == 0 else [fill, got], axis=0)
                        azs[i, d - 1, SLOT[dx], rows] = value.astype(BF)

                m = slice(SLOT[spots[0]], SLOT[spots[-1]] + 1)
                tiles_of = {f"z{n}.{SPOT[dx][0]}" for dx in spots}
                send(f"{label}{d}{s}", sorted(tiles_of) + ([f"{label}{d + 1}{s}"] if d < 4 else []),
                     azs.at[i, d - 1, m, rows], azr.at[i, d - 1, m, rows], "z" + s, run, C_A * len(spots))

    a_z("af", (2,), (((2,), a1), ((2,), a2)))
    a_z("an", (-1, 1, 0), (((1, 0), tops), ((-1,), tops)))

    def a_sum(pieces):
        def run():
            for dx in pieces:
                za[SLOT[dx]] = part(0, tops, dx) + azr[0, 0, SLOT[dx]].astype(F32) + azr[1, 0, SLOT[dx]].astype(F32)
        return run

    task("asf", ["z0.1", "af1+", "af1-"], C_A, a_sum([2]))
    task("asn", ["z0.0", "z0.1", "an1+", "an1-"], 3 * C_A, a_sum([-1, 1, 0]))

    def a_add(spot, rows, n):
        def run():
            za[spot, rows] = za[spot, rows] + axr[n]
        return run

    send("a0", ["asf"], za.at[0, a1], axr.at[0], "x+")
    send("a1", ["asf"], za.at[0, a2], axr.at[1], "x-")
    send("a2", ["asn", "a0"], za.at[2], axr2.at[0], "x+", a_add(2, a1, 0), 0.05)
    send("a3", ["asn", "a1"], za.at[1], axr2.at[1], "x-", a_add(1, a2, 1), 0.05)

    b1, b2 = slice(RA, RA + RB1), slice(RA + RB1, RANK)
    v1, v2, v = slice(0, RB1), slice(RB1, RB), slice(0, RB)

    KINDS = ((2, b1, None), (2, b2, None), (1, b1, 0), (1, b2, None), (-1, b1, None), (-1, b2, 1))

    def b_x(name, kinds, k, to):
        lo, hi = GROUPS[k]
        needs = set()
        for kind in kinds:
            dx, _, first = KINDS[kind]
            needs |= {f"z{n}.{SPOT[dx][0]}" for n in range(lo, hi)}
            if first is not None:
                needs.add(f"bh{first}.{k}")

        def run():
            for kind in kinds:
                dx, rows, first = KINDS[kind]
                for n in range(lo, hi):
                    value = part(n, rows, dx)
                    if first is not None:
                        value = value + br[first, n].astype(F32)
                    bs[kind, n] = value.astype(BF)

        m = slice(kinds[0], kinds[-1] + 1)
        send(f"{name}.{k}", sorted(needs), bs.at[m, lo:hi], br.at[m, lo:hi], to, run, C_B * len(kinds) * (hi - lo))

    def b_total(k):
        lo, hi = GROUPS[k]

        def run():
            for n in range(lo, hi):
                zb[n, v1] = part(n, b1, 0) + br[2, n].astype(F32) + br[4, n].astype(F32)
                zb[n, v2] = part(n, b2, 0) + br[3, n].astype(F32) + br[5, n].astype(F32)
        task(f"bt{k}", [f"z{n}.0" for n in range(lo, hi)] + [f"bf0.{k}", f"bf1.{k}"], 3 * C_B * (hi - lo), run)

    for k in range(5):
        b_x("bh0", (0,), k, "x+")
        b_x("bh1", (1,), k, "x-")
        b_x("bf0", (2, 3), k, "x+")
        b_x("bf1", (4, 5), k, "x-")
        b_total(k)
    for d in range(4, 0, -1):
        for i, (s, sign) in enumerate(SIGNS):
            for j, rows in enumerate((v1, v2)):
                if d == 4 and i != j:
                    continue
                first = d == 4 or d == 3 and i != j

                def run(n=ORDER[sign * d], i=i, j=j, d=d, rows=rows, first=first):
                    bzs[i, d - 1, j] = pack(zb[n, rows] if first else zb[n, rows] + unpack(bzr[i, d, j]))
                send(f"bz{d}{s}{j}", [f"bt{d}"] + ([] if first else [f"bz{d + 1}{s}{j}"]),
                     bzs.at[i, d - 1, j], bzr.at[i, d - 1, j], "z" + s, run, C_P)

    def result():
        top = za[3] + axr2[0] + axr2[1]
        bottom = [zb[0, rows] + unpack(bzr[0, 0, j]) + unpack(bzr[1, 0, j]) for j, rows in enumerate((v1, v2))]
        out[...] = jnp.concatenate([top] + bottom, axis=0).T

    task("out", ["asn", "a2", "a3", "bt0", "bz1+0", "bz1+1", "bz1-0", "bz1-1"], 0.3, result)
    plan.run()


def local(block_tiles, block_coords, block_counts, basis_rows):
    vmem = pl.BlockSpec(memory_space=pltpu.VMEM)
    return pl.pallas_call(
        kernel,
        out_shape=jax.ShapeDtypeStruct((BLK, RANK), F32),
        in_specs=[vmem, vmem, pl.BlockSpec(memory_space=pl.ANY),
                  pl.BlockSpec(memory_space=pl.ANY)],
        out_specs=vmem,
        scratch_shapes=[
            pltpu.VMEM((SLOTS + 1, BLK, BLK), BF),
            pltpu.VMEM((NZ, NX, BLK, RANK), BF),
            pltpu.VMEM((ROWS, RANK), F32),
            pltpu.VMEM((4, CHUNK, RANK), F32),
            pltpu.VMEM((6, HALF + HEAD, RANK), jnp.int16),
            pltpu.VMEM((6, HALF + HEAD, RANK), jnp.int16),
            pltpu.VMEM((RANK, ROWS), BF),
            pltpu.VMEM((NZ, 2, RANK, 256), F32),
            pltpu.VMEM((4, RA, BLK), F32),
            pltpu.VMEM((NZ, RB, BLK), F32),
            pltpu.VMEM((2, 4, 4, RA, BLK), BF),
            pltpu.VMEM((2, 4, 4, RA, BLK), BF),
            pltpu.VMEM((2, RA // 2, BLK), F32),
            pltpu.VMEM((2, RA, BLK), F32),
            pltpu.VMEM((6, NZ, RB1, BLK), BF),
            pltpu.VMEM((6, NZ, RB1, BLK), BF),
            pltpu.VMEM((2, 4, 2, RB1 + HEAD, BLK), jnp.int16),
            pltpu.VMEM((2, 4, 2, RB1 + HEAD, BLK), jnp.int16),
            pltpu.VMEM((1, 512), jnp.int32),
            pltpu.SMEM((1, 512), jnp.int32),
            pltpu.SemaphoreType.DMA((N_SEM,)),
            pltpu.SemaphoreType.DMA((N_SEM,)),
            pltpu.SemaphoreType.DMA((8,)),
            pltpu.SemaphoreType.DMA,
            pltpu.SemaphoreType.DMA,
        ],
        compiler_params=pltpu.CompilerParams(
            collective_id=0, has_side_effects=True, vmem_limit_bytes=60 * 1024 * 1024),
        cost_estimate=pl.CostEstimate(flops=4 * ROWS * COLS * RANK, bytes_accessed=11_000_000,
                                      transcendentals=0),
    )(block_counts, block_coords.T, block_tiles, basis_rows)


def solution(mesh):
    return jax.shard_map(
        local,
        mesh=mesh,
        in_specs=(
            P("cells", "genes", None),
            P("cells", "genes"),
            P("cells", "genes"),
            P(("cells", "genes"), None),
        ),
        out_specs=P(("cells", "genes"), None),
        check_vma=False,
    )
```

```python
import jax
import jax.numpy as jnp
import numpy as np
from jax import lax
from jax.experimental import pallas as pl
from jax.experimental.pallas import tpu as pltpu
from jax.sharding import PartitionSpec as P

MESH = pl.DeviceIdType.MESH
BF = jnp.bfloat16
F32 = jnp.float32

NX, NY, NZ = 4, 4, 8
BLK = 128
RANK = 256
ROWS = 2048
COLS = 4096
CHUNK = 256
HALF = CHUNK // 2
SLOTS = 320
GA = 48
RA = 64
RB = RANK - RA
RB1 = 96

ORDER = {0: 0, 1: 1, -1: 2, 2: 3, -2: 4, 3: 5, -3: 6, 4: 7, -4: 7}
GROUPS = ((0, 1), (1, 3), (3, 5), (5, 7), (7, 8))
SIGNS = (("+", 1), ("-", -1))

HOP = 1.6
LINK = {"x+": 50e3, "x-": 50e3, "z+": 50e3, "z-": 50e3, "y+": 50e3, "y-": 50e3, "c": 500e3}
ISSUE = 0.08
LOADED = 5.0
C_A, C_B, C_P = 0.04, 0.035, 0.1
N_SEM = 150
HEAD = 16


def pack(value):
    top = jnp.max(jnp.abs(value), axis=0, keepdims=True)
    power = jnp.floor(jnp.log2(jnp.maximum(top, 1e-30))) + 1.0
    whole = jnp.clip(jnp.round(value * jnp.exp2(15.0 - power)), -32767.0, 32767.0)
    both = jnp.concatenate([whole, jnp.broadcast_to(power, (HEAD, value.shape[1]))], axis=0)
    return both.astype(jnp.int32).astype(jnp.int16)


def unpack(packed):
    value = packed.astype(jnp.int32).astype(F32)
    rows = value.shape[0] - HEAD
    return value[:rows] * jnp.exp2(value[rows:rows + 1] - 15.0)


class Plan:
    def __init__(self, ssem, rsem, where):
        self.ssem, self.rsem, self.where = ssem, rsem, where
        self.tasks = {}
        self.count = 0
        self.after = {}

    def task(self, name, needs, cost, run, message=None, after=0.0):
        assert name not in self.tasks, name
        self.tasks[name] = (tuple(needs), cost, run, message)
        self.after[name] = after

    def send(self, name, needs, src, dst, to, run=None, cost=0.0):
        copy = pltpu.make_async_remote_copy(
            src_ref=src, dst_ref=dst, send_sem=self.ssem.at[self.count],
            recv_sem=self.rsem.at[self.count], device_id=self.where[to], device_id_type=MESH)
        self.count += 1
        time = float(np.prod(src.shape)) * np.dtype(src.dtype).itemsize / LINK[to]
        self.task(name, needs, cost + ISSUE, run, (copy, to, time))

    def order(self):
        after = {name: [] for name in self.tasks}
        for name, (needs, *_) in self.tasks.items():
            for need in needs:
                after[need].append(name)
        rank = {}

        def longest(name):
            if name not in rank:
                _, cost, _, message = self.tasks[name]
                tail = max([longest(n) for n in after[name]], default=0.0)
                rank[name] = cost + (message[2] + HOP if message else 0.0) + tail
            return rank[name]

        for name in self.tasks:
            longest(name)
        now, free, ready_at, order = 0.0, {}, {}, []
        left = dict.fromkeys(self.tasks)
        while left:
            can = {n: max([ready_at[d] for d in self.tasks[n][0]] + [self.after[n]])
                   for n in left if all(d in ready_at for d in self.tasks[n][0])}
            now = max(now, min(can.values()))
            name = max((n for n in can if can[n] <= now), key=lambda n: rank[n])
            del left[name]
            order.append(name)
            _, cost, _, message = self.tasks[name]
            now += cost
            ready_at[name] = now
            if message:
                _, to, time = message
                free[to] = max(now, free.get(to, 0.0)) + time
                ready_at[name] = free[to] + HOP
        self.finish, self.ready_at = now, ready_at
        return order

    def run(self):
        got = set()
        assert self.count <= N_SEM
        order = self.order()
        for name in order:
            needs, _, run, message = self.tasks[name]
            for need in needs:
                if self.tasks[need][3] and need not in got:
                    self.tasks[need][3][0].wait_recv()
                    got.add(need)
            if run:
                run()
            if message:
                message[0].start()
        for name in order:
            if self.tasks[name][3]:
                assert name in got, name
                self.tasks[name][3][0].wait_send()


def kernel(count_ref, coords, tiles_hbm, basis, out, tiles, q, p, pcr, ys, yr, cbt, zt,
           za, zb, azs, azr, axr, axr2, bs, br, bzs, bzr, slot_v, slot_ref, ssem, rsem, tsem, slot_sem, basis_sem):
    c = lax.axis_index("cells")
    g = lax.axis_index("genes")
    z, x = c // NX, c % NX
    y, core = g // 2, g % 2

    def at(dz, dx, dy, dc):
        return (((z + dz + NZ) % NZ) * NX + (x + dx + NX) % NX,
                ((y + dy + NY) % NY) * 2 + (core + dc) % 2)

    where = {
        "x+": at(0, 1, 0, 0), "x-": at(0, -1, 0, 0),
        "z+": at(1, 0, 0, 0), "z-": at(-1, 0, 0, 0),
        "y+": at(0, 0, 1, 0), "y-": at(0, 0, -1, 0),
        "c": at(0, 0, 0, 1),
    }
    plan = Plan(ssem, rsem, where)
    task, send = plan.task, plan.send

    n_loads = 8
    per = SLOTS // n_loads
    loads = [pltpu.make_async_copy(tiles_hbm.at[pl.ds(i * per, per)],
                                   tiles.at[pl.ds(i * per, per)], tsem.at[i]) for i in range(n_loads)]
    own_basis = pltpu.make_async_copy(basis, q.at[0, 0], basis_sem)
    own_basis.start()
    for load in loads:
        load.start()
    barrier = pltpu.get_barrier_semaphore()
    for to in where.values():
        pl.semaphore_signal(barrier, inc=1, device_id=to, device_id_type=MESH)
    tiles[SLOTS] = jnp.zeros((BLK, BLK), BF)

    own_basis.wait()
    pl.semaphore_wait(barrier, len(where))

    to_smem = pltpu.make_async_copy(slot_v, slot_ref, slot_sem)

    def table():
        b, k = coords[0:1, :], coords[1:2, :]
        chunk = lax.shift_right_logical(b, 1)
        dy = ((chunk & 3) - y) & 3
        own = lax.shift_right_logical(chunk, 2) == core
        pos = jnp.where(own, jnp.where(dy == 0, 0, jnp.where(dy == 3, 2, jnp.where(dy == 1, 3, 6))),
                        jnp.where(dy == 0, 1, jnp.where(dy == 3, 4, jnp.where(dy == 1, 5, 7))))
        dz = (lax.shift_right_logical(k, 2) - z) & 7
        dz = jnp.where(dz == 0, 0, jnp.where(dz <= 3, 2 * dz - 1, jnp.where(dz == 4, 7, 2 * (NZ - dz))))
        dx = ((k & 3) - x) & 3
        dx = jnp.where(dx >= 2, 5 - dx, dx)
        place = (pos * 2 + (b & 1)) * 32 + dz * NX + dx
        live = lax.broadcasted_iota(jnp.int32, (1, SLOTS), 1) < count_ref[...]
        place = jnp.broadcast_to(jnp.where(live, place, -1), (8, SLOTS)).T[:, 0:1]
        ids = lax.broadcasted_iota(jnp.int32, (SLOTS, 1), 0)
        hit = place == lax.broadcasted_iota(jnp.int32, (SLOTS, 512), 1)
        slot_v[...] = jnp.min(jnp.where(hit, ids, SLOTS), axis=0, keepdims=True)
        to_smem.start()

    def block(rows, cols):
        return jnp.concatenate([jnp.concatenate([tiles[slot_ref[0, r * 32 + c]] for c in range(*cols)], axis=1)
                                for r in range(*rows)], axis=0)

    def loaded():
        to_smem.wait()
        for load in loads:
            load.wait()

    a, b = slice(0, GA), slice(GA, BLK)
    send("ax+", [], q.at[0, 0, a], q.at[0, 2, a], "x+")
    send("ax-", [], q.at[0, 0, a], q.at[0, 1, a], "x-")
    send("af+", ["ax+"], q.at[0, 2, 0:32], q.at[0, 3, 0:32], "x+")
    send("af-", ["ax-"], q.at[0, 1, 32:GA], q.at[0, 3, 32:GA], "x-")
    for d in range(1, 5):
        for s, sign in SIGNS:
            src, dst = ORDER[-sign * (d - 1)], ORDER[-sign * d]
            last = [f"{d - 1}{s}"] if d > 1 else []
            rows = slice(0, BLK) if d < 4 else slice(0, 64) if sign > 0 else slice(64, BLK)
            send(f"zo{d}{s}", ["zo" + n for n in last], q.at[src, 0, rows], q.at[dst, 0, rows], "z" + s)
            cols = slice(1, 3) if d < 4 else slice(1, 2) if sign > 0 else slice(2, 3)
            send(f"zn{d}{s}", ["zn" + n for n in last] or ["ax+", "ax-"],
                 q.at[src, cols, a], q.at[dst, cols, a], "z" + s)
            rows = a if d < 4 else slice(0, 32) if sign > 0 else slice(32, GA)
            send(f"zf{d}{s}", ["zf" + n for n in last] or ["af+", "af-"],
                 q.at[src, 3, rows], q.at[dst, 3, rows], "z" + s)
    for k, (lo, hi) in enumerate(GROUPS):
        here = [f"zo{k}+", f"zo{k}-"] if k else []
        e = GA + (48 if k % 2 else 32)
        send(f"bx{k}+", here, q.at[lo:hi, 0, b], q.at[lo:hi, 2, b], "x+")
        send(f"bx{k}-", here, q.at[lo:hi, 0, b], q.at[lo:hi, 1, b], "x-")
        send(f"bf{k}+", [f"bx{k}+"], q.at[lo:hi, 2, GA:e], q.at[lo:hi, 3, GA:e], "x+")
        send(f"bf{k}-", [f"bx{k}-"], q.at[lo:hi, 1, e:BLK], q.at[lo:hi, 3, e:BLK], "x-")

    def cells_dot(lo, hi, rows):
        right = q[lo:hi].reshape((hi - lo) * 512, RANK)
        left = block((rows.start // BLK, rows.stop // BLK), (lo * 4, hi * 4))
        return jnp.dot(left, right, preferred_element_type=F32)

    def cells(lo, hi, rows):
        def run():
            part = cells_dot(lo, hi, rows)
            p[rows] = part if lo == 0 else p[rows] + part
        return run

    task("table", [], 0.8, table)
    task("load", ["table"], 0.2, loaded, after=LOADED)
    for k, (lo, hi) in enumerate(GROUPS):
        came = [f"b{n}{k}{s}" for n in "xf" for s in "+-"] + (
            [f"z{n}{k}{s}" for n in "onf" for s in "+-"] if k else ["ax+", "ax-", "af+", "af-"])
        if k < 4:
            for i in range(4):
                task(f"c{k}.{i}", ["load"] + came + ([f"c{k - 1}.{i}"] if k else []), 0.35 * (hi - lo),
                     cells(lo, hi, slice(i * 512, (i + 1) * 512)))
        else:
            for i in range(8):
                task(f"c4.{i}", ["load", f"c3.{i // 2}"] + came, 0.18, cells(lo, hi, slice(i * CHUNK, (i + 1) * CHUNK)))

    def lanes(i):
        return slice(i * CHUNK, (i + 1) * CHUNK)

    def add(rows, other):
        def run():
            p[rows] = p[rows] + other[...]
        return run

    OWN, OTHER = {0: 0, -1: 2, 1: 3, 2: 6}, {0: 1, -1: 4, 1: 5, 2: 7}
    low = {dy: slice(i * CHUNK, i * CHUNK + HALF) for dy, i in OWN.items()}
    high = {dy: slice(i * CHUNK + HALF, (i + 1) * CHUNK) for dy, i in OWN.items()}
    for dy in (2, 1, -1, 0):
        send(f"pair{dy}", [f"c4.{OTHER[dy]}"], p.at[lanes(OTHER[dy])], pcr.at[dy + 1], "c")
        task(f"own{dy}", [f"c4.{OWN[dy]}", f"pair{dy}"], 0.1, add(lanes(OWN[dy]), pcr.at[dy + 1]))

    def y_send(n, needs, rows, to, first=None):
        def run():
            ys[n] = pack(p[rows] if first is None else p[rows] + unpack(yr[first]))
        send(f"y{n}", needs, ys.at[n], yr.at[n], to, run, 0.15)

    y_send(0, ["own2"], low[2], "y+")
    y_send(1, ["own2"], high[2], "y-")
    y_send(2, ["own1"], high[1], "y+")
    y_send(3, ["own-1"], low[-1], "y-")
    y_send(4, ["own1", "y0"], low[1], "y+", 0)
    y_send(5, ["own-1", "y1"], high[-1], "y-", 1)

    def rounded():
        top = p[low[0]] + unpack(yr[3]) + unpack(yr[4])
        bottom = p[high[0]] + unpack(yr[2]) + unpack(yr[5])
        cbt[:, lanes(0)] = jnp.concatenate([top, bottom], axis=0).T.astype(BF)

    task("cb", ["own0", "y2", "y3", "y4", "y5"], 0.4, rounded)
    up, down = slice(0, RANK // 2), slice(RANK // 2, RANK)
    for half, rows in (("u", up), ("d", down)):
        send(f"g+{half}", ["cb"], cbt.at[rows, lanes(0)], cbt.at[rows, lanes(2)], "y+")
        send(f"g-{half}", ["cb"], cbt.at[rows, lanes(0)], cbt.at[rows, lanes(3)], "y-")
    send("k0", ["cb"], cbt.at[:, lanes(0)], cbt.at[:, lanes(1)], "c")
    send("k+", ["g+u"], cbt.at[up, lanes(2)], cbt.at[up, lanes(6)], "y+")
    send("k-", ["g-d"], cbt.at[down, lanes(3)], cbt.at[down, lanes(6)], "y-")
    send("k1", ["g+u", "g+d"], cbt.at[:, lanes(2)], cbt.at[:, lanes(4)], "c")
    send("k2", ["g-u", "g-d"], cbt.at[:, lanes(3)], cbt.at[:, lanes(5)], "c")
    send("k3", ["k+", "k-"], cbt.at[:, lanes(6)], cbt.at[:, lanes(7)], "c")

    def genes(n, i, lo, hi):
        def run():
            col = (2 * n + i) * 2
            right = block((lo * 2, hi * 2), (col, col + 2))
            part = jnp.dot(cbt[:, lo * CHUNK:hi * CHUNK], right, preferred_element_type=F32)
            zt[n, i] = part if lo == 0 else zt[n, i] + part
        return run

    for n in range(8):
        for i in range(2):
            task(f"t{n}.{i}", ["cb", "k0"], 0.17, genes(n, i, 0, 2))
            task(f"u{n}.{i}", [f"t{n}.{i}", "g+u", "g+d", "g-u", "g-d"], 0.2, genes(n, i, 2, 4))
            task(f"v{n}.{i}", [f"u{n}.{i}", "k1", "k2"], 0.2, genes(n, i, 4, 6))
            task(f"z{n}.{i}", [f"v{n}.{i}", "k+", "k-", "k3"], 0.2, genes(n, i, 6, 8))

    SPOT = {0: (0, 0), 1: (0, 1), -1: (1, 0), 2: (1, 1)}

    def part(n, rows, dx):
        i, j = SPOT[dx]
        return zt[n, i, rows, j * BLK:(j + 1) * BLK]

    SLOT = {2: 0, -1: 1, 1: 2, 0: 3}
    cut = RA // 2
    a1, a2 = slice(0, cut), slice(cut, RA)
    tops = slice(0, RA)

    def a_z(label, pieces, far):
        for d in range(4, 0, -1):
            for i, (s, sign) in enumerate(SIGNS):
                spots, rows = far[i] if d == 4 else (pieces, tops)
                n = ORDER[sign * d]

                def run(d=d, i=i, n=n, spots=spots, rows=rows):
                    for dx in spots:
                        value = part(n, rows, dx)
                        if d < 3 or d == 3 and far[i][1] == tops and dx in far[i][0]:
                            value = value + azr[i, d, SLOT[dx], rows].astype(F32)
                        elif d == 3 and far[i][1] != tops:
                            got = azr[i, 3, SLOT[dx], far[i][1]].astype(F32)
                            fill = jnp.zeros_like(got)
                            value = value + jnp.concatenate([got, fill] if i == 0 else [fill, got], axis=0)
                        azs[i, d - 1, SLOT[dx], rows] = value.astype(BF)

                m = slice(SLOT[spots[0]], SLOT[spots[-1]] + 1)
                tiles_of = {f"z{n}.{SPOT[dx][0]}" for dx in spots}
                send(f"{label}{d}{s}", sorted(tiles_of) + ([f"{label}{d + 1}{s}"] if d < 4 else []),
                     azs.at[i, d - 1, m, rows], azr.at[i, d - 1, m, rows], "z" + s, run, C_A * len(spots))

    a_z("af", (2,), (((2,), a1), ((2,), a2)))
    a_z("an", (-1, 1, 0), (((1, 0), tops), ((-1,), tops)))

    def a_sum(pieces):
        def run():
            for dx in pieces:
                za[SLOT[dx]] = part(0, tops, dx) + azr[0, 0, SLOT[dx]].astype(F32) + azr[1, 0, SLOT[dx]].astype(F32)
        return run

    task("asf", ["z0.1", "af1+", "af1-"], C_A, a_sum([2]))
    task("asn", ["z0.0", "z0.1", "an1+", "an1-"], 3 * C_A, a_sum([-1, 1, 0]))

    def a_add(spot, rows, n):
        def run():
            za[spot, rows] = za[spot, rows] + axr[n]
        return run

    send("a0", ["asf"], za.at[0, a1], axr.at[0], "x+")
    send("a1", ["asf"], za.at[0, a2], axr.at[1], "x-")
    send("a2", ["asn", "a0"], za.at[2], axr2.at[0], "x+", a_add(2, a1, 0), 0.05)
    send("a3", ["asn", "a1"], za.at[1], axr2.at[1], "x-", a_add(1, a2, 1), 0.05)

    b1, b2 = slice(RA, RA + RB1), slice(RA + RB1, RANK)
    v1, v2, v = slice(0, RB1), slice(RB1, RB), slice(0, RB)

    KINDS = ((2, b1, None), (2, b2, None), (1, b1, 0), (1, b2, None), (-1, b1, None), (-1, b2, 1))

    def b_x(name, kinds, k, to):
        lo, hi = GROUPS[k]
        needs = set()
        for kind in kinds:
            dx, _, first = KINDS[kind]
            needs |= {f"z{n}.{SPOT[dx][0]}" for n in range(lo, hi)}
            if first is not None:
                needs.add(f"bh{first}.{k}")

        def run():
            for kind in kinds:
                dx, rows, first = KINDS[kind]
                for n in range(lo, hi):
                    value = part(n, rows, dx)
                    if first is not None:
                        value = value + br[first, n].astype(F32)
                    bs[kind, n] = value.astype(BF)

        m = slice(kinds[0], kinds[-1] + 1)
        send(f"{name}.{k}", sorted(needs), bs.at[m, lo:hi], br.at[m, lo:hi], to, run, C_B * len(kinds) * (hi - lo))

    def b_total(k):
        lo, hi = GROUPS[k]

        def run():
            for n in range(lo, hi):
                zb[n, v1] = part(n, b1, 0) + br[2, n].astype(F32) + br[4, n].astype(F32)
                zb[n, v2] = part(n, b2, 0) + br[3, n].astype(F32) + br[5, n].astype(F32)
        task(f"bt{k}", [f"z{n}.0" for n in range(lo, hi)] + [f"bf0.{k}", f"bf1.{k}"], 3 * C_B * (hi - lo), run)

    for k in range(5):
        b_x("bh0", (0,), k, "x+")
        b_x("bh1", (1,), k, "x-")
        b_x("bf0", (2, 3), k, "x+")
        b_x("bf1", (4, 5), k, "x-")
        b_total(k)
    for d in range(4, 0, -1):
        for i, (s, sign) in enumerate(SIGNS):
            for j, rows in enumerate((v1, v2)):
                if d == 4 and i != j:
                    continue
                first = d == 4 or d == 3 and i != j

                def run(n=ORDER[sign * d], i=i, j=j, d=d, rows=rows, first=first):
                    bzs[i, d - 1, j] = pack(zb[n, rows] if first else zb[n, rows] + unpack(bzr[i, d, j]))
                send(f"bz{d}{s}{j}", [f"bt{d}"] + ([] if first else [f"bz{d + 1}{s}{j}"]),
                     bzs.at[i, d - 1, j], bzr.at[i, d - 1, j], "z" + s, run, C_P)

    def result():
        top = za[3] + axr2[0] + axr2[1]
        bottom = [zb[0, rows] + unpack(bzr[0, 0, j]) + unpack(bzr[1, 0, j]) for j, rows in enumerate((v1, v2))]
        out[...] = jnp.concatenate([top] + bottom, axis=0).T

    task("out", ["asn", "a2", "a3", "bt0", "bz1+0", "bz1+1", "bz1-0", "bz1-1"], 0.3, result)
    plan.run()


def local(block_tiles, block_coords, block_counts, basis_rows):
    vmem = pl.BlockSpec(memory_space=pltpu.VMEM)
    return pl.pallas_call(
        kernel,
        out_shape=jax.ShapeDtypeStruct((BLK, RANK), F32),
        in_specs=[vmem, vmem, pl.BlockSpec(memory_space=pl.ANY),
                  pl.BlockSpec(memory_space=pl.ANY)],
        out_specs=vmem,
        scratch_shapes=[
            pltpu.VMEM((SLOTS + 1, BLK, BLK), BF),
            pltpu.VMEM((NZ, NX, BLK, RANK), BF),
            pltpu.VMEM((ROWS, RANK), F32),
            pltpu.VMEM((4, CHUNK, RANK), F32),
            pltpu.VMEM((6, HALF + HEAD, RANK), jnp.int16),
            pltpu.VMEM((6, HALF + HEAD, RANK), jnp.int16),
            pltpu.VMEM((RANK, ROWS), BF),
            pltpu.VMEM((NZ, 2, RANK, 256), F32),
            pltpu.VMEM((4, RA, BLK), F32),
            pltpu.VMEM((NZ, RB, BLK), F32),
            pltpu.VMEM((2, 4, 4, RA, BLK), BF),
            pltpu.VMEM((2, 4, 4, RA, BLK), BF),
            pltpu.VMEM((2, RA // 2, BLK), F32),
            pltpu.VMEM((2, RA, BLK), F32),
            pltpu.VMEM((6, NZ, RB1, BLK), BF),
            pltpu.VMEM((6, NZ, RB1, BLK), BF),
            pltpu.VMEM((2, 4, 2, RB1 + HEAD, BLK), jnp.int16),
            pltpu.VMEM((2, 4, 2, RB1 + HEAD, BLK), jnp.int16),
            pltpu.VMEM((1, 512), jnp.int32),
            pltpu.SMEM((1, 512), jnp.int32),
            pltpu.SemaphoreType.DMA((N_SEM,)),
            pltpu.SemaphoreType.DMA((N_SEM,)),
            pltpu.SemaphoreType.DMA((8,)),
            pltpu.SemaphoreType.DMA,
            pltpu.SemaphoreType.DMA,
        ],
        compiler_params=pltpu.CompilerParams(
            collective_id=0, has_side_effects=True, vmem_limit_bytes=60 * 1024 * 1024),
        cost_estimate=pl.CostEstimate(flops=4 * ROWS * COLS * RANK, bytes_accessed=11_000_000,
                                      transcendentals=0),
    )(block_counts, block_coords.T, block_tiles, basis_rows)


def solution(mesh):
    return jax.shard_map(
        local,
        mesh=mesh,
        in_specs=(
            P("cells", "genes", None),
            P("cells", "genes"),
            P("cells", "genes"),
            P(("cells", "genes"), None),
        ),
        out_specs=P(("cells", "genes"), None),
        check_vma=False,
    )
```

```python
import jax
import jax.numpy as jnp
import numpy as np
from jax import lax
from jax.experimental import pallas as pl
from jax.experimental.pallas import tpu as pltpu
from jax.sharding import PartitionSpec as P

MESH = pl.DeviceIdType.MESH
BF = jnp.bfloat16
F32 = jnp.float32

NX, NY, NZ = 4, 4, 8
BLK = 128
RANK = 256
ROWS = 2048
COLS = 4096
CHUNK = 256
HALF = CHUNK // 2
SLOTS = 320
GA = 48
RA = 64
RB = RANK - RA
RB1 = 96

ORDER = {0: 0, 1: 1, -1: 2, 2: 3, -2: 4, 3: 5, -3: 6, 4: 7, -4: 7}
GROUPS = ((0, 1), (1, 3), (3, 5), (5, 7), (7, 8))
SIGNS = (("+", 1), ("-", -1))

HOP = 1.6
LINK = {"x+": 50e3, "x-": 50e3, "z+": 50e3, "z-": 50e3, "y+": 50e3, "y-": 50e3, "c": 500e3}
ISSUE = 0.08
LOADED = 5.0
C_A, C_B, C_P = 0.04, 0.035, 0.1
N_SEM = 150
HEAD = 16


def pack(value):
    top = jnp.max(jnp.abs(value), axis=0, keepdims=True)
    power = jnp.floor(jnp.log2(jnp.maximum(top, 1e-30))) + 1.0
    whole = jnp.clip(jnp.round(value * jnp.exp2(15.0 - power)), -32767.0, 32767.0)
    both = jnp.concatenate([whole, jnp.broadcast_to(power, (HEAD, value.shape[1]))], axis=0)
    return both.astype(jnp.int32).astype(jnp.int16)


def unpack(packed):
    value = packed.astype(jnp.int32).astype(F32)
    rows = value.shape[0] - HEAD
    return value[:rows] * jnp.exp2(value[rows:rows + 1] - 15.0)


class Plan:
    def __init__(self, ssem, rsem, where):
        self.ssem, self.rsem, self.where = ssem, rsem, where
        self.tasks = {}
        self.count = 0
        self.after = {}

    def task(self, name, needs, cost, run, message=None, after=0.0):
        assert name not in self.tasks, name
        self.tasks[name] = (tuple(needs), cost, run, message)
        self.after[name] = after

    def send(self, name, needs, src, dst, to, run=None, cost=0.0):
        copy = pltpu.make_async_remote_copy(
            src_ref=src, dst_ref=dst, send_sem=self.ssem.at[self.count],
            recv_sem=self.rsem.at[self.count], device_id=self.where[to], device_id_type=MESH)
        self.count += 1
        time = float(np.prod(src.shape)) * np.dtype(src.dtype).itemsize / LINK[to]
        self.task(name, needs, cost + ISSUE, run, (copy, to, time))

    def order(self):
        after = {name: [] for name in self.tasks}
        for name, (needs, *_) in self.tasks.items():
            for need in needs:
                after[need].append(name)
        rank = {}

        def longest(name):
            if name not in rank:
                _, cost, _, message = self.tasks[name]
                tail = max([longest(n) for n in after[name]], default=0.0)
                rank[name] = cost + (message[2] + HOP if message else 0.0) + tail
            return rank[name]

        for name in self.tasks:
            longest(name)
        now, free, ready_at, order = 0.0, {}, {}, []
        left = dict.fromkeys(self.tasks)
        while left:
            can = {n: max([ready_at[d] for d in self.tasks[n][0]] + [self.after[n]])
                   for n in left if all(d in ready_at for d in self.tasks[n][0])}
            now = max(now, min(can.values()))
            name = max((n for n in can if can[n] <= now), key=lambda n: rank[n])
            del left[name]
            order.append(name)
            _, cost, _, message = self.tasks[name]
            now += cost
            ready_at[name] = now
            if message:
                _, to, time = message
                free[to] = max(now, free.get(to, 0.0)) + time
                ready_at[name] = free[to] + HOP
        self.finish, self.ready_at = now, ready_at
        return order

    def run(self):
        got = set()
        assert self.count <= N_SEM
        order = self.order()
        for name in order:
            needs, _, run, message = self.tasks[name]
            for need in needs:
                if self.tasks[need][3] and need not in got:
                    self.tasks[need][3][0].wait_recv()
                    got.add(need)
            if run:
                run()
            if message:
                message[0].start()
        for name in order:
            if self.tasks[name][3]:
                assert name in got, name
                self.tasks[name][3][0].wait_send()


def kernel(count_ref, coords, tiles_hbm, basis, out, tiles, q, p, pcs, pcr, ys, yr, cbt, zt,
           za, zb, azs, azr, axr, axr2, bs, br, bzs, bzr, slot_v, slot_ref, ssem, rsem, tsem, slot_sem, basis_sem):
    c = lax.axis_index("cells")
    g = lax.axis_index("genes")
    z, x = c // NX, c % NX
    y, core = g // 2, g % 2

    def at(dz, dx, dy, dc):
        return (((z + dz + NZ) % NZ) * NX + (x + dx + NX) % NX,
                ((y + dy + NY) % NY) * 2 + (core + dc) % 2)

    where = {
        "x+": at(0, 1, 0, 0), "x-": at(0, -1, 0, 0),
        "z+": at(1, 0, 0, 0), "z-": at(-1, 0, 0, 0),
        "y+": at(0, 0, 1, 0), "y-": at(0, 0, -1, 0),
        "c": at(0, 0, 0, 1),
    }
    plan = Plan(ssem, rsem, where)
    task, send = plan.task, plan.send

    n_loads = 8
    per = SLOTS // n_loads
    loads = [pltpu.make_async_copy(tiles_hbm.at[pl.ds(i * per, per)],
                                   tiles.at[pl.ds(i * per, per)], tsem.at[i]) for i in range(n_loads)]
    own_basis = pltpu.make_async_copy(basis, q.at[0, 0], basis_sem)
    own_basis.start()
    for load in loads:
        load.start()
    barrier = pltpu.get_barrier_semaphore()
    for to in where.values():
        pl.semaphore_signal(barrier, inc=1, device_id=to, device_id_type=MESH)
    tiles[SLOTS] = jnp.zeros((BLK, BLK), BF)

    own_basis.wait()
    pl.semaphore_wait(barrier, len(where))

    to_smem = pltpu.make_async_copy(slot_v, slot_ref, slot_sem)

    def table():
        b, k = coords[0:1, :], coords[1:2, :]
        chunk = lax.shift_right_logical(b, 1)
        dy = ((chunk & 3) - y) & 3
        own = lax.shift_right_logical(chunk, 2) == core
        pos = jnp.where(own, jnp.where(dy == 0, 0, jnp.where(dy == 3, 2, jnp.where(dy == 1, 3, 6))),
                        jnp.where(dy == 0, 1, jnp.where(dy == 3, 4, jnp.where(dy == 1, 5, 7))))
        dz = (lax.shift_right_logical(k, 2) - z) & 7
        dz = jnp.where(dz == 0, 0, jnp.where(dz <= 3, 2 * dz - 1, jnp.where(dz == 4, 7, 2 * (NZ - dz))))
        dx = ((k & 3) - x) & 3
        dx = jnp.where(dx >= 2, 5 - dx, dx)
        place = (pos * 2 + (b & 1)) * 32 + dz * NX + dx
        live = lax.broadcasted_iota(jnp.int32, (1, SLOTS), 1) < count_ref[...]
        place = jnp.broadcast_to(jnp.where(live, place, -1), (8, SLOTS)).T[:, 0:1]
        ids = lax.broadcasted_iota(jnp.int32, (SLOTS, 1), 0)
        hit = place == lax.broadcasted_iota(jnp.int32, (SLOTS, 512), 1)
        slot_v[...] = jnp.min(jnp.where(hit, ids, SLOTS), axis=0, keepdims=True)
        to_smem.start()

    def block(rows, cols):
        return jnp.concatenate([jnp.concatenate([tiles[slot_ref[0, r * 32 + c]] for c in range(*cols)], axis=1)
                                for r in range(*rows)], axis=0)

    def loaded():
        to_smem.wait()
        for load in loads:
            load.wait()

    a, b = slice(0, GA), slice(GA, BLK)
    send("ax+", [], q.at[0, 0, a], q.at[0, 2, a], "x+")
    send("ax-", [], q.at[0, 0, a], q.at[0, 1, a], "x-")
    send("af+", ["ax+"], q.at[0, 2, 0:32], q.at[0, 3, 0:32], "x+")
    send("af-", ["ax-"], q.at[0, 1, 32:GA], q.at[0, 3, 32:GA], "x-")
    for d in range(1, 5):
        for s, sign in SIGNS:
            src, dst = ORDER[-sign * (d - 1)], ORDER[-sign * d]
            last = [f"{d - 1}{s}"] if d > 1 else []
            rows = slice(0, BLK) if d < 4 else slice(0, 64) if sign > 0 else slice(64, BLK)
            send(f"zo{d}{s}", ["zo" + n for n in last], q.at[src, 0, rows], q.at[dst, 0, rows], "z" + s)
            cols = slice(1, 3) if d < 4 else slice(1, 2) if sign > 0 else slice(2, 3)
            send(f"zn{d}{s}", ["zn" + n for n in last] or ["ax+", "ax-"],
                 q.at[src, cols, a], q.at[dst, cols, a], "z" + s)
            rows = a if d < 4 else slice(0, 32) if sign > 0 else slice(32, GA)
            send(f"zf{d}{s}", ["zf" + n for n in last] or ["af+", "af-"],
                 q.at[src, 3, rows], q.at[dst, 3, rows], "z" + s)
    for k, (lo, hi) in enumerate(GROUPS):
        here = [f"zo{k}+", f"zo{k}-"] if k else []
        e = GA + (48 if k % 2 else 32)
        send(f"bx{k}+", here, q.at[lo:hi, 0, b], q.at[lo:hi, 2, b], "x+")
        send(f"bx{k}-", here, q.at[lo:hi, 0, b], q.at[lo:hi, 1, b], "x-")
        send(f"bf{k}+", [f"bx{k}+"], q.at[lo:hi, 2, GA:e], q.at[lo:hi, 3, GA:e], "x+")
        send(f"bf{k}-", [f"bx{k}-"], q.at[lo:hi, 1, e:BLK], q.at[lo:hi, 3, e:BLK], "x-")

    def cells_dot(lo, hi, rows):
        right = q[lo:hi].reshape((hi - lo) * 512, RANK)
        left = block((rows.start // BLK, rows.stop // BLK), (lo * 4, hi * 4))
        return jnp.dot(left, right, preferred_element_type=F32)

    def cells(lo, hi, rows):
        def run():
            part = cells_dot(lo, hi, rows)
            p[rows] = part if lo == 0 else p[rows] + part
        return run

    task("table", [], 0.8, table)
    task("load", ["table"], 0.2, loaded, after=LOADED)
    for k, (lo, hi) in enumerate(GROUPS):
        came = [f"b{n}{k}{s}" for n in "xf" for s in "+-"] + (
            [f"z{n}{k}{s}" for n in "onf" for s in "+-"] if k else ["ax+", "ax-", "af+", "af-"])
        if k < 4:
            for i in range(4):
                task(f"c{k}.{i}", ["load"] + came + ([f"c{k - 1}.{i}"] if k else []), 0.35 * (hi - lo),
                     cells(lo, hi, slice(i * 512, (i + 1) * 512)))
        else:
            for i in range(8):
                task(f"c4.{i}", ["load", f"c3.{i // 2}"] + came, 0.18, cells(lo, hi, slice(i * CHUNK, (i + 1) * CHUNK)))

    def lanes(i):
        return slice(i * CHUNK, (i + 1) * CHUNK)

    OWN, OTHER = {0: 0, -1: 2, 1: 3, 2: 6}, {0: 1, -1: 4, 1: 5, 2: 7}
    low = {dy: slice(i * CHUNK, i * CHUNK + HALF) for dy, i in OWN.items()}
    high = {dy: slice(i * CHUNK + HALF, (i + 1) * CHUNK) for dy, i in OWN.items()}
    for dy in (2, 1, -1, 0):
        def to_other(dy=dy):
            pcs[dy + 1] = pack(p[lanes(OTHER[dy])])

        def from_other(dy=dy):
            p[lanes(OWN[dy])] = p[lanes(OWN[dy])] + unpack(pcr[dy + 1])

        send(f"pair{dy}", [f"c4.{OTHER[dy]}"], pcs.at[dy + 1], pcr.at[dy + 1], "c", to_other, 0.25)
        task(f"own{dy}", [f"c4.{OWN[dy]}", f"pair{dy}"], 0.15, from_other)

    def y_send(n, needs, rows, to, first=None):
        def run():
            ys[n] = pack(p[rows] if first is None else p[rows] + unpack(yr[first]))
        send(f"y{n}", needs, ys.at[n], yr.at[n], to, run, 0.15)

    y_send(0, ["own2"], low[2], "y+")
    y_send(1, ["own2"], high[2], "y-")
    y_send(2, ["own1"], high[1], "y+")
    y_send(3, ["own-1"], low[-1], "y-")
    y_send(4, ["own1", "y0"], low[1], "y+", 0)
    y_send(5, ["own-1", "y1"], high[-1], "y-", 1)

    def rounded():
        top = p[low[0]] + unpack(yr[3]) + unpack(yr[4])
        bottom = p[high[0]] + unpack(yr[2]) + unpack(yr[5])
        cbt[:, lanes(0)] = jnp.concatenate([top, bottom], axis=0).T.astype(BF)

    task("cb", ["own0", "y2", "y3", "y4", "y5"], 0.4, rounded)
    up, down = slice(0, RANK // 2), slice(RANK // 2, RANK)
    for half, rows in (("u", up), ("d", down)):
        send(f"g+{half}", ["cb"], cbt.at[rows, lanes(0)], cbt.at[rows, lanes(2)], "y+")
        send(f"g-{half}", ["cb"], cbt.at[rows, lanes(0)], cbt.at[rows, lanes(3)], "y-")
    send("k0", ["cb"], cbt.at[:, lanes(0)], cbt.at[:, lanes(1)], "c")
    send("k+", ["g+u"], cbt.at[up, lanes(2)], cbt.at[up, lanes(6)], "y+")
    send("k-", ["g-d"], cbt.at[down, lanes(3)], cbt.at[down, lanes(6)], "y-")
    send("k1", ["g+u", "g+d"], cbt.at[:, lanes(2)], cbt.at[:, lanes(4)], "c")
    send("k2", ["g-u", "g-d"], cbt.at[:, lanes(3)], cbt.at[:, lanes(5)], "c")
    send("k3", ["k+", "k-"], cbt.at[:, lanes(6)], cbt.at[:, lanes(7)], "c")

    def genes(n, i, lo, hi):
        def run():
            col = (2 * n + i) * 2
            right = block((lo * 2, hi * 2), (col, col + 2))
            part = jnp.dot(cbt[:, lo * CHUNK:hi * CHUNK], right, preferred_element_type=F32)
            zt[n, i] = part if lo == 0 else zt[n, i] + part
        return run

    for n in range(8):
        for i in range(2):
            task(f"t{n}.{i}", ["cb", "k0"], 0.17, genes(n, i, 0, 2))
            task(f"u{n}.{i}", [f"t{n}.{i}", "g+u", "g+d", "g-u", "g-d"], 0.2, genes(n, i, 2, 4))
            task(f"v{n}.{i}", [f"u{n}.{i}", "k1", "k2"], 0.2, genes(n, i, 4, 6))
            task(f"z{n}.{i}", [f"v{n}.{i}", "k+", "k-", "k3"], 0.2, genes(n, i, 6, 8))

    SPOT = {0: (0, 0), 1: (0, 1), -1: (1, 0), 2: (1, 1)}

    def part(n, rows, dx):
        i, j = SPOT[dx]
        return zt[n, i, rows, j * BLK:(j + 1) * BLK]

    SLOT = {2: 0, -1: 1, 1: 2, 0: 3}
    cut = RA // 2
    a1, a2 = slice(0, cut), slice(cut, RA)
    tops = slice(0, RA)

    def a_z(label, pieces, far):
        for d in range(4, 0, -1):
            for i, (s, sign) in enumerate(SIGNS):
                spots, rows = far[i] if d == 4 else (pieces, tops)
                n = ORDER[sign * d]

                def run(d=d, i=i, n=n, spots=spots, rows=rows):
                    for dx in spots:
                        value = part(n, rows, dx)
                        if d < 3 or d == 3 and far[i][1] == tops and dx in far[i][0]:
                            value = value + azr[i, d, SLOT[dx], rows].astype(F32)
                        elif d == 3 and far[i][1] != tops:
                            got = azr[i, 3, SLOT[dx], far[i][1]].astype(F32)
                            fill = jnp.zeros_like(got)
                            value = value + jnp.concatenate([got, fill] if i == 0 else [fill, got], axis=0)
                        azs[i, d - 1, SLOT[dx], rows] = value.astype(BF)

                m = slice(SLOT[spots[0]], SLOT[spots[-1]] + 1)
                tiles_of = {f"z{n}.{SPOT[dx][0]}" for dx in spots}
                send(f"{label}{d}{s}", sorted(tiles_of) + ([f"{label}{d + 1}{s}"] if d < 4 else []),
                     azs.at[i, d - 1, m, rows], azr.at[i, d - 1, m, rows], "z" + s, run, C_A * len(spots))

    a_z("af", (2,), (((2,), a1), ((2,), a2)))
    a_z("an", (-1, 1, 0), (((1, 0), tops), ((-1,), tops)))

    def a_sum(pieces):
        def run():
            for dx in pieces:
                za[SLOT[dx]] = part(0, tops, dx) + azr[0, 0, SLOT[dx]].astype(F32) + azr[1, 0, SLOT[dx]].astype(F32)
        return run

    task("asf", ["z0.1", "af1+", "af1-"], C_A, a_sum([2]))
    task("asn", ["z0.0", "z0.1", "an1+", "an1-"], 3 * C_A, a_sum([-1, 1, 0]))

    def a_add(spot, rows, n):
        def run():
            za[spot, rows] = za[spot, rows] + axr[n]
        return run

    send("a0", ["asf"], za.at[0, a1], axr.at[0], "x+")
    send("a1", ["asf"], za.at[0, a2], axr.at[1], "x-")
    send("a2", ["asn", "a0"], za.at[2], axr2.at[0], "x+", a_add(2, a1, 0), 0.05)
    send("a3", ["asn", "a1"], za.at[1], axr2.at[1], "x-", a_add(1, a2, 1), 0.05)

    b1, b2 = slice(RA, RA + RB1), slice(RA + RB1, RANK)
    v1, v2, v = slice(0, RB1), slice(RB1, RB), slice(0, RB)

    KINDS = ((2, b1, None), (2, b2, None), (1, b1, 0), (1, b2, None), (-1, b1, None), (-1, b2, 1))

    def b_x(name, kinds, k, to):
        lo, hi = GROUPS[k]
        needs = set()
        for kind in kinds:
            dx, _, first = KINDS[kind]
            needs |= {f"z{n}.{SPOT[dx][0]}" for n in range(lo, hi)}
            if first is not None:
                needs.add(f"bh{first}.{k}")

        def run():
            for kind in kinds:
                dx, rows, first = KINDS[kind]
                for n in range(lo, hi):
                    value = part(n, rows, dx)
                    if first is not None:
                        value = value + br[first, n].astype(F32)
                    bs[kind, n] = value.astype(BF)

        m = slice(kinds[0], kinds[-1] + 1)
        send(f"{name}.{k}", sorted(needs), bs.at[m, lo:hi], br.at[m, lo:hi], to, run, C_B * len(kinds) * (hi - lo))

    def b_total(k):
        lo, hi = GROUPS[k]

        def run():
            for n in range(lo, hi):
                zb[n, v1] = part(n, b1, 0) + br[2, n].astype(F32) + br[4, n].astype(F32)
                zb[n, v2] = part(n, b2, 0) + br[3, n].astype(F32) + br[5, n].astype(F32)
        task(f"bt{k}", [f"z{n}.0" for n in range(lo, hi)] + [f"bf0.{k}", f"bf1.{k}"], 3 * C_B * (hi - lo), run)

    for k in range(5):
        b_x("bh0", (0,), k, "x+")
        b_x("bh1", (1,), k, "x-")
        b_x("bf0", (2, 3), k, "x+")
        b_x("bf1", (4, 5), k, "x-")
        b_total(k)
    for d in range(4, 0, -1):
        for i, (s, sign) in enumerate(SIGNS):
            for j, rows in enumerate((v1, v2)):
                if d == 4 and i != j:
                    continue
                first = d == 4 or d == 3 and i != j

                def run(n=ORDER[sign * d], i=i, j=j, d=d, rows=rows, first=first):
                    bzs[i, d - 1, j] = pack(zb[n, rows] if first else zb[n, rows] + unpack(bzr[i, d, j]))
                send(f"bz{d}{s}{j}", [f"bt{d}"] + ([] if first else [f"bz{d + 1}{s}{j}"]),
                     bzs.at[i, d - 1, j], bzr.at[i, d - 1, j], "z" + s, run, C_P)

    def result():
        top = za[3] + axr2[0] + axr2[1]
        bottom = [zb[0, rows] + unpack(bzr[0, 0, j]) + unpack(bzr[1, 0, j]) for j, rows in enumerate((v1, v2))]
        out[...] = jnp.concatenate([top] + bottom, axis=0).T

    task("out", ["asn", "a2", "a3", "bt0", "bz1+0", "bz1+1", "bz1-0", "bz1-1"], 0.3, result)
    plan.run()


def local(block_tiles, block_coords, block_counts, basis_rows):
    vmem = pl.BlockSpec(memory_space=pltpu.VMEM)
    return pl.pallas_call(
        kernel,
        out_shape=jax.ShapeDtypeStruct((BLK, RANK), F32),
        in_specs=[vmem, vmem, pl.BlockSpec(memory_space=pl.ANY),
                  pl.BlockSpec(memory_space=pl.ANY)],
        out_specs=vmem,
        scratch_shapes=[
            pltpu.VMEM((SLOTS + 1, BLK, BLK), BF),
            pltpu.VMEM((NZ, NX, BLK, RANK), BF),
            pltpu.VMEM((ROWS, RANK), F32),
            pltpu.VMEM((4, CHUNK + HEAD, RANK), jnp.int16),
            pltpu.VMEM((4, CHUNK + HEAD, RANK), jnp.int16),
            pltpu.VMEM((6, HALF + HEAD, RANK), jnp.int16),
            pltpu.VMEM((6, HALF + HEAD, RANK), jnp.int16),
            pltpu.VMEM((RANK, ROWS), BF),
            pltpu.VMEM((NZ, 2, RANK, 256), F32),
            pltpu.VMEM((4, RA, BLK), F32),
            pltpu.VMEM((NZ, RB, BLK), F32),
            pltpu.VMEM((2, 4, 4, RA, BLK), BF),
            pltpu.VMEM((2, 4, 4, RA, BLK), BF),
            pltpu.VMEM((2, RA // 2, BLK), F32),
            pltpu.VMEM((2, RA, BLK), F32),
            pltpu.VMEM((6, NZ, RB1, BLK), BF),
            pltpu.VMEM((6, NZ, RB1, BLK), BF),
            pltpu.VMEM((2, 4, 2, RB1 + HEAD, BLK), jnp.int16),
            pltpu.VMEM((2, 4, 2, RB1 + HEAD, BLK), jnp.int16),
            pltpu.VMEM((1, 512), jnp.int32),
            pltpu.SMEM((1, 512), jnp.int32),
            pltpu.SemaphoreType.DMA((N_SEM,)),
            pltpu.SemaphoreType.DMA((N_SEM,)),
            pltpu.SemaphoreType.DMA((8,)),
            pltpu.SemaphoreType.DMA,
            pltpu.SemaphoreType.DMA,
        ],
        compiler_params=pltpu.CompilerParams(
            collective_id=0, has_side_effects=True, vmem_limit_bytes=60 * 1024 * 1024),
        cost_estimate=pl.CostEstimate(flops=4 * ROWS * COLS * RANK, bytes_accessed=11_000_000,
                                      transcendentals=0),
    )(block_counts, block_coords.T, block_tiles, basis_rows)


def solution(mesh):
    return jax.shard_map(
        local,
        mesh=mesh,
        in_specs=(
            P("cells", "genes", None),
            P("cells", "genes"),
            P("cells", "genes"),
            P(("cells", "genes"), None),
        ),
        out_specs=P(("cells", "genes"), None),
        check_vma=False,
    )
```
